32 devices in a mesh: fsdp: 8 (over y, x, core), tp: 4 (over z).
Axes of the slice: x: 2, y: 2, z: 4, core: 2. Of those that a mesh axis runs over, the one named last changes fastest.
Arguments:
- learner_flat: bfloat16 [2, 39845888], P(None, ('fsdp', 'tp')), may hold values from -1.796875 to 1.796875
- param_offsets: int32 [2, 32, 4], replicated, may hold values from 0 to 1243136, as said below
- owner_map: int32 [2, 32], replicated, may hold values from 0 to 7, as said below
- slice_map: int32 [8, 4], replicated, may hold values from 0 to 3, each once within a row
Outputs:
- query_absorbed: bfloat16 [2, 32, 1536, 512], P(None, 'fsdp', 'tp')
- output_absorbed: bfloat16 [2, 32, 7168, 512], P(None, 'fsdp', 'tp')
The draws below stay inside these ranges and needn't reach their ends.
Inputs may be any that keep to these rules, and one draw needn't show every extreme that they name: `param_offsets`: in each layer the pieces of all heads' four parameters lie in a rank's 1245184 entries one after another in some order, without gaps or intersections; a piece of a parameter holds that parameter's entries divided by 32; the last piece of each layer is a key up-projection piece. `owner_map`: in each layer every index of fsdp owns exactly 4 heads.
All inputs are finite; a program needn't handle non-finite values.
Results may differ from the reference program's by a relative error of at most 0.001.
Values may be sent and summed in bfloat16 or wider, within the bound.
No kernel may reach another device: no remote copies, remote signals or barrier semaphores. Data moves between devices by JAX's collectives and lax.ppermute only.
A program may use at most 64 MiB of HBM per device.

```python
import jax
import jax.numpy as jnp
from jax import lax

D = 7168
QR = 1536
KVR = 512
QK_NOPE = 128
V_DIM = 128
HEAD_DEV = 4
LAYERS = 2
HEADS = 32
RANKS = 32
REC = 1245184
SHARD = 1245184
Q_SLICE = 384
O_SLICE = 1792
N_FSDP = 8
N_TP = 4


def draw_param_offsets(key, part):
    piece_sizes = jnp.array([QR * QK_NOPE // RANKS, QK_NOPE * KVR // RANKS, V_DIM * KVR // RANKS, D * V_DIM // RANKS], dtype=jnp.int32)
    layer_keys = jax.random.split(jax.random.fold_in(key, 11), LAYERS)
    piece_count = HEADS * 4

    def one_layer(layer_key):
        order_key, pick_key = jax.random.split(layer_key)
        piece_order = jax.random.permutation(order_key, piece_count).astype(jnp.int32)
        target = (jax.random.randint(pick_key, (), 0, HEADS) * 4 + 1).astype(jnp.int32)
        position = jnp.argmax((piece_order == target).astype(jnp.int32)).astype(jnp.int32)
        last_value = piece_order[piece_count - 1]
        piece_order = piece_order.at[position].set(last_value).at[piece_count - 1].set(target)
        sizes_here = jnp.tile(piece_sizes, HEADS)[piece_order]
        start_at = (jnp.cumsum(sizes_here) - sizes_here).astype(jnp.int32)
        placed = jnp.zeros((piece_count,), dtype=jnp.int32).at[piece_order].set(start_at)
        return placed.reshape(HEADS, 4)
    return jax.vmap(one_layer)(layer_keys)


def draw_owner_map(key, part):
    layer_keys = jax.random.split(jax.random.fold_in(key, 23), LAYERS)

    def one_layer(layer_key):
        return (jax.random.permutation(layer_key, HEADS) // HEAD_DEV).astype(jnp.int32)
    return jax.vmap(one_layer)(layer_keys)


def block_scale(key, dims, cuts, smallest, largest):
    def one(axis_at, blocks):
        heights = jax.random.uniform(jax.random.fold_in(jax.random.fold_in(key, 6), axis_at), (blocks,), jnp.float32, smallest / len(cuts), largest / len(cuts))
        return jnp.repeat(jnp.exp(heights), dims[axis_at] // blocks).reshape((-1,) + (1,) * (len(dims) - axis_at - 1))

    gain = one(*cuts[0])
    for cut in cuts[1:]:
        gain = gain * one(*cut)
    return gain


def normal_values(stream_key, shape, deviation, reach, cuts=(), kind=jnp.bfloat16):
    values = deviation * jax.random.normal(stream_key, shape, jnp.float32)
    if cuts:
        values = values * block_scale(stream_key, shape, cuts, -0.22, 0.18)
    return jnp.clip(values, -reach, reach).astype(kind)


def setup_inputs(seed: int = 0) -> dict:
    key_list = jax.random.split(jax.random.key(seed), 5)
    return {
        "learner_flat": normal_values(key_list[0], (LAYERS, HEADS * REC), 0.3, 1.796875, ((1, 32),)),
        "param_offsets": draw_param_offsets(jax.random.fold_in(key_list[4], 71), 0),
        "owner_map": draw_owner_map(jax.random.fold_in(key_list[4], 71), 0),
        "slice_map": jax.vmap(lambda own: jax.random.permutation(own, N_TP))(jax.random.split(key_list[3], N_FSDP)).reshape((N_FSDP, N_TP)).astype(jnp.int32),
    }


def head_order(owner_map, per_group):
    head_count = owner_map.shape[1]
    head_index = jnp.arange(head_count, dtype=jnp.int32)
    same_owner = owner_map[:, :, None] == owner_map[:, None, :]
    before = head_index[None, None, :] < head_index[None, :, None]
    head_rank = jnp.sum(jnp.logical_and(same_owner, before).astype(jnp.int32), axis=2)
    head_slot = owner_map * per_group + head_rank
    slot_hits = head_slot[:, :, None] == head_index[None, None, :]
    return jnp.sum(jnp.where(slot_hits, head_index[None, :, None], 0), axis=1).astype(jnp.int32)


def reference(learner_flat, param_offsets, owner_map, slice_map):
    widths = (QR * QK_NOPE // RANKS, QK_NOPE * KVR // RANKS, V_DIM * KVR // RANKS, D * V_DIM // RANKS)
    head_at = head_order(owner_map, HEAD_DEV)
    query_layers = []
    output_layers = []
    for layer_id in range(LAYERS):
        flat_table = learner_flat[layer_id].reshape(RANKS, SHARD)

        def one_head(slot_id):
            head_id = head_at[layer_id, slot_id]
            begins = param_offsets[layer_id, head_id]

            def fetch_param(kind_id, param_shape):
                pieces = lax.dynamic_slice(flat_table, (jnp.int32(0), begins[kind_id].astype(jnp.int32)), (RANKS, widths[kind_id]))
                return pieces.reshape(param_shape).astype(jnp.float32)

            query_up = fetch_param(0, (QR, QK_NOPE))
            key_up = fetch_param(1, (QK_NOPE, KVR))
            value_up = fetch_param(2, (V_DIM, KVR))
            out_proj = fetch_param(3, (D, V_DIM))
            absorbed_query = jnp.dot(query_up, key_up, precision=lax.Precision.HIGHEST, preferred_element_type=jnp.float32)
            absorbed_output = jnp.dot(out_proj, value_up, precision=lax.Precision.HIGHEST, preferred_element_type=jnp.float32)
            row_order = slice_map[slot_id // HEAD_DEV]
            absorbed_query = jnp.take(absorbed_query.reshape(N_TP, Q_SLICE, KVR), row_order, axis=0).reshape(QR, KVR)
            absorbed_output = jnp.take(absorbed_output.reshape(N_TP, O_SLICE, KVR), row_order, axis=0).reshape(D, KVR)
            return absorbed_query.astype(jnp.bfloat16), absorbed_output.astype(jnp.bfloat16)

        query_here, output_here = lax.map(one_head, jnp.arange(HEADS, dtype=jnp.int32))
        query_layers.append(query_here)
        output_layers.append(output_here)
    return jnp.stack(query_layers, axis=0), jnp.stack(output_layers, axis=0)
```

```python
import functools
import math

import jax
import jax.numpy as jnp
from jax import lax
from jax.experimental import pallas as pl
from jax.experimental.pallas import tpu as pltpu
from jax.sharding import PartitionSpec as P

D = 7168
QR = 1536
KVR = 512
QK_NOPE = 128
V_DIM = 128
LANES = 128
QUERY, KEY, VALUE, OUT = range(4)
VMEM_LIMIT = 48 * 1024 * 1024


def piece_widths(rank_total):
    return (
        QR * QK_NOPE // rank_total,
        QK_NOPE * KVR // rank_total,
        V_DIM * KVR // rank_total,
        D * V_DIM // rank_total,
    )


def pack(table, param_offsets, owner_map, ways, widths, granule, layers, kinds):
    head_count = owner_map.shape[1]
    per_group = head_count // ways
    steps = [widths[kind] // granule for kind in kinds]
    starts = [sum(steps[:i]) for i in range(len(kinds))]
    out = jax.ShapeDtypeStruct(
        (ways, len(layers), per_group, sum(steps)) + table.shape[2:], table.dtype
    )

    def kernel(offsets, owners, source, target, taken, sem):
        for at, layer in enumerate(layers):
            for way in range(ways):
                taken[way] = 0

            @pl.loop(0, head_count)
            def _(head):
                way = owners[layer, head]
                slot = taken[way]
                taken[way] = slot + 1
                for kind, step, start in zip(kinds, steps, starts):
                    begin = lax.div(offsets[layer, head, kind], jnp.int32(granule))
                    pltpu.make_async_copy(
                        source.at[layer, pl.ds(begin, step)],
                        target.at[way, at, slot, pl.ds(start, step)],
                        sem,
                    ).start()

        pltpu.make_async_copy(target, target, sem).wait()

    return pl.pallas_call(
        kernel,
        out_shape=out,
        in_specs=[
            pl.BlockSpec(memory_space=pltpu.SMEM),
            pl.BlockSpec(memory_space=pltpu.SMEM),
            pl.BlockSpec(memory_space=pl.ANY),
        ],
        out_specs=pl.BlockSpec(memory_space=pl.ANY),
        scratch_shapes=[pltpu.SMEM((ways,), jnp.int32), pltpu.SemaphoreType.DMA],
        cost_estimate=pl.CostEstimate(
            flops=0, transcendentals=0, bytes_accessed=2 * 2 * math.prod(out.shape)
        ),
        name="pack",
    )(param_offsets, owner_map, table)


def assemble(gathered):
    t_ways, f_ways, layers, heads, kinds, rows, _ = gathered.shape
    depth = t_ways * f_ways * rows * LANES // KVR
    cuts = KVR // LANES

    def kernel(pieces, out, scratch):
        for kind in range(kinds):
            for f in range(f_ways):
                for t in range(t_ways):
                    scratch[pl.ds((f * t_ways + t) * rows, rows), :] = pieces[t, f, 0, 0, kind].astype(
                        jnp.float32
                    )
            for cut in range(cuts):
                out[0, 0, kind, :, pl.ds(cut * LANES, LANES)] = scratch[
                    pl.ds(cut, depth, stride=cuts), :
                ].astype(jnp.bfloat16)

    return pl.pallas_call(
        kernel,
        grid=(layers, heads),
        out_shape=jax.ShapeDtypeStruct((layers, heads, kinds, depth, KVR), gathered.dtype),
        in_specs=[
            pl.BlockSpec(
                (t_ways, f_ways, 1, 1, kinds, rows, LANES), lambda l, j: (0, 0, l, j, 0, 0, 0)
            )
        ],
        out_specs=pl.BlockSpec((1, 1, kinds, depth, KVR), lambda l, j: (l, j, 0, 0, 0)),
        scratch_shapes=[pltpu.VMEM((depth * cuts, LANES), jnp.float32)],
        compiler_params=pltpu.CompilerParams(vmem_limit_bytes=VMEM_LIMIT),
        name="assemble",
    )(gathered)


def absorb(layer, came_from, part, matrices, outs, shapes, t_ways, rows):
    f_count, heads = part.shape[0], part.shape[1]
    q_rows, o_rows = rows

    def kernel(_, rows_in, mats, *refs):
        q_out, o_out = refs[-2:]
        q_out[0, 0] = jnp.dot(
            rows_in[0, 0, :q_rows], mats[0, 0, 0], preferred_element_type=jnp.float32
        ).astype(jnp.bfloat16)
        o_out[0, 0] = jnp.dot(
            rows_in[0, 0, q_rows:], mats[0, 0, 1], preferred_element_type=jnp.float32
        ).astype(jnp.bfloat16)

    in_specs = [
        pl.BlockSpec((1, 1, q_rows + o_rows, LANES), lambda j, f, t: (f, j, 0, 0)),
        pl.BlockSpec((1, 1) + matrices.shape[2:], lambda j, f, t: (layer, j, 0, 0, 0)),
    ]
    aliases = {}
    args = [part, matrices]
    if outs is not None:
        in_specs += [pl.BlockSpec(memory_space=pl.ANY)] * 2
        aliases = {3: 0, 4: 1}
        args += list(outs)
    work = f_count * heads * (q_rows + o_rows)
    return pl.pallas_call(
        kernel,
        grid_spec=pltpu.PrefetchScalarGridSpec(
            num_scalar_prefetch=1,
            grid=(heads, f_count),
            in_specs=in_specs,
            out_specs=[
                pl.BlockSpec((1, 1, q_rows, KVR), lambda j, f, t: (layer, j, f * t_ways + t[0], 0)),
                pl.BlockSpec((1, 1, o_rows, KVR), lambda j, f, t: (layer, j, f * t_ways + t[0], 0)),
            ],
        ),
        out_shape=shapes,
        input_output_aliases=aliases,
        compiler_params=pltpu.CompilerParams(vmem_limit_bytes=VMEM_LIMIT),
        cost_estimate=pl.CostEstimate(
            flops=2 * work * LANES * KVR,
            transcendentals=0,
            bytes_accessed=2 * work * (LANES + KVR),
        ),
        name="absorb",
    )(came_from.reshape(1), *args)


def absorb_plain(parts, me, matrices, layers, per_group, t_ways, steps, granule):
    results = []
    for kind, (start, step) in enumerate(steps):
        by_layer = []
        for layer in range(layers):
            stacked = jnp.stack([parts[layer][d] for d in range(t_ways)])
            order = lax.rem(me - jnp.arange(t_ways, dtype=jnp.int32) + t_ways, jnp.int32(t_ways))
            rows = jnp.take(stacked, order, axis=0)[:, :, :, start : start + step]
            rows = rows.transpose(2, 1, 0, 3, 4, 5).reshape(per_group, -1, LANES)
            by_layer.append(rows)
        results.append(
            jnp.einsum(
                "lhrc,lhck->lhrk",
                jnp.stack(by_layer),
                matrices[:, :, kind],
                preferred_element_type=jnp.float32,
            ).astype(jnp.bfloat16)
        )
    return tuple(results)


def per_device(learner_flat, param_offsets, owner_map, slice_map):
    f_ways, t_ways = lax.axis_size("fsdp"), lax.axis_size("tp")
    layer_count = learner_flat.shape[0]
    per_group = owner_map.shape[1] // f_ways
    widths = piece_widths(f_ways * t_ways)
    granule = functools.reduce(math.gcd, widths)
    table = learner_flat.reshape(layer_count, -1, granule // LANES, LANES)
    whole_tiles = granule % (16 * LANES) == 0
    steps = [width // granule for width in widths]

    me = lax.axis_index("tp")
    slice_row = lax.dynamic_index_in_dim(slice_map, lax.axis_index("fsdp"), 0, keepdims=False)
    blocks = f_ways // t_ways

    def packed(layers, kinds):
        return pack(table, param_offsets, owner_map, f_ways, widths, granule, layers, kinds)

    def over_fsdp(x):
        return lax.all_to_all(x, "fsdp", split_axis=0, concat_axis=0, tiled=True)

    pairs = packed(tuple(range(layer_count)), (KEY, VALUE))
    pairs = lax.all_gather(over_fsdp(pairs), "tp", axis=0)
    pairs = pairs.reshape(t_ways, f_ways, layer_count, per_group, 2, steps[KEY] * granule // LANES, LANES)
    if whole_tiles:
        matrices = assemble(pairs)
    else:
        matrices = pairs.transpose(2, 3, 4, 1, 0, 5, 6).reshape(layer_count, per_group, 2, -1, KVR)

    parts = []
    for layer in range(layer_count):
        rows = over_fsdp(packed((layer,), (QUERY, OUT)))[:, 0]
        got = []
        for shift in range(t_ways):
            target = lax.rem(me + shift, t_ways)
            piece = lax.dynamic_slice_in_dim(rows, slice_row[target] * blocks, blocks, 0)
            if shift:
                piece = lax.ppermute(
                    piece, "tp", [(i, (i + shift) % t_ways) for i in range(t_ways)]
                )
            got.append(piece)
        parts.append(got)

    if not whole_tiles:
        at = [(0, steps[QUERY]), (steps[QUERY], steps[OUT])]
        return absorb_plain(parts, me, matrices, layer_count, per_group, t_ways, at, granule)

    shapes = tuple(
        jax.ShapeDtypeStruct((layer_count, per_group, rows // t_ways, KVR), jnp.bfloat16)
        for rows in (QR, D)
    )
    rows = (widths[QUERY] // LANES, widths[OUT] // LANES)
    outs = None
    for layer in range(layer_count):
        for shift in range(t_ways):
            part = parts[layer][shift].reshape(blocks, per_group, sum(rows), LANES)
            came_from = lax.rem(me - shift + t_ways, t_ways)
            outs = absorb(layer, came_from, part, matrices, outs, shapes, t_ways, rows)
    return tuple(outs)


def solution(mesh):
    placed = (P(None, ("fsdp", "tp")), P(), P(), P())
    return jax.shard_map(
        per_device,
        mesh=mesh,
        in_specs=placed,
        out_specs=(P(None, "fsdp", "tp", None), P(None, "fsdp", "tp", None)),
        check_vma=False,
    )
```

```python
import functools
import math

import jax
import jax.numpy as jnp
from jax import lax
from jax.experimental import pallas as pl
from jax.experimental.pallas import tpu as pltpu
from jax.sharding import PartitionSpec as P

D = 7168
QR = 1536
KVR = 512
QK_NOPE = 128
V_DIM = 128
LANES = 128
QUERY, KEY, VALUE, OUT = range(4)
VMEM_LIMIT = 48 * 1024 * 1024


def piece_widths(rank_total):
    return (
        QR * QK_NOPE // rank_total,
        QK_NOPE * KVR // rank_total,
        V_DIM * KVR // rank_total,
        D * V_DIM // rank_total,
    )


def pack(table, param_offsets, owner_map, ways, widths, granule, layers, slots, kinds):
    head_count = owner_map.shape[1]
    steps = [widths[kind] // granule for kind in kinds]
    starts = [sum(steps[:i]) for i in range(len(kinds))]
    out = jax.ShapeDtypeStruct(
        (ways, len(layers), len(slots), sum(steps)) + table.shape[2:], table.dtype
    )

    def kernel(offsets, owners, source, target, taken):
        for at, layer in enumerate(layers):
            for way in range(ways):
                taken[way] = 0

            @pl.loop(0, head_count)
            def _(head):
                way = owners[layer, head]
                slot = taken[way]
                taken[way] = slot + 1

                @pl.when(jnp.logical_and(slot >= slots[0], slot <= slots[-1]))
                def _():
                    for kind, step, start in zip(kinds, steps, starts):
                        begin = lax.div(offsets[layer, head, kind], jnp.int32(granule))
                        target[way, at, slot - slots[0], pl.ds(start, step)] = source[
                            layer, pl.ds(begin, step)
                        ]

    return pl.pallas_call(
        kernel,
        out_shape=out,
        in_specs=[
            pl.BlockSpec(memory_space=pltpu.SMEM),
            pl.BlockSpec(memory_space=pltpu.SMEM),
            pl.BlockSpec(memory_space=pltpu.VMEM),
        ],
        out_specs=pl.BlockSpec(memory_space=pltpu.VMEM),
        scratch_shapes=[pltpu.SMEM((ways,), jnp.int32)],
        compiler_params=pltpu.CompilerParams(vmem_limit_bytes=VMEM_LIMIT),
        cost_estimate=pl.CostEstimate(
            flops=0, transcendentals=0, bytes_accessed=2 * 2 * math.prod(out.shape)
        ),
        name="pack",
    )(param_offsets, owner_map, table)


def spread(x, axis, ways, me):
    up, down = [x], [x]
    for _ in range(ways - 1):
        up.append(lax.ppermute(up[-1], axis, [(i, i + 1) for i in range(ways - 1)]))
        down.append(lax.ppermute(down[-1], axis, [(i + 1, i) for i in range(ways - 1)]))
    return [x] + [jnp.where(me >= d, up[d], down[ways - d]) for d in range(1, ways)]


def assemble(me, spread_parts):
    t_ways = len(spread_parts)
    f_ways, layers, heads, kinds, rows, _ = spread_parts[0].shape
    depth = t_ways * f_ways * rows * LANES // KVR
    cuts = KVR // LANES

    def kernel(me_ref, *refs):
        pieces, (out, scratch) = refs[:t_ways], refs[t_ways:]
        for kind in range(kinds):
            for d in range(t_ways):
                t = lax.rem(me_ref[0] - d + t_ways, t_ways)
                for f in range(f_ways):
                    scratch[pl.ds(pl.multiple_of((f * t_ways + t) * rows, rows), rows), :] = pieces[
                        d
                    ][f, 0, 0, kind].astype(jnp.float32)
            for cut in range(cuts):
                out[0, 0, kind, :, pl.ds(cut * LANES, LANES)] = scratch[
                    pl.ds(cut, depth, stride=cuts), :
                ].astype(jnp.bfloat16)

    return pl.pallas_call(
        kernel,
        grid_spec=pltpu.PrefetchScalarGridSpec(
            num_scalar_prefetch=1,
            grid=(layers, heads),
            in_specs=[
                pl.BlockSpec((f_ways, 1, 1, kinds, rows, LANES), lambda l, j, _: (0, l, j, 0, 0, 0))
            ]
            * t_ways,
            out_specs=pl.BlockSpec((1, 1, kinds, depth, KVR), lambda l, j, _: (l, j, 0, 0, 0)),
            scratch_shapes=[pltpu.VMEM((depth * cuts, LANES), jnp.float32)],
        ),
        out_shape=jax.ShapeDtypeStruct((layers, heads, kinds, depth, KVR), spread_parts[0].dtype),
        compiler_params=pltpu.CompilerParams(vmem_limit_bytes=VMEM_LIMIT),
        name="assemble",
    )(me.reshape(1), *spread_parts)


def absorb(where, layer, slots, own, came, matrices, outs, shapes):
    t_ways = len(came) + 1
    blocks = came[0].shape[0]
    q_rows, o_rows = shapes[0].shape[4], shapes[1].shape[4]

    def kernel(at, *refs):
        parts, mats = refs[:t_ways], refs[t_ways]
        q_out, o_out = refs[-2:]
        for d in range(t_ways):
            t = lax.rem(at[0] - d + t_ways, t_ways)
            for f in range(blocks):
                q_out[0, 0, f, t] = jnp.dot(
                    parts[d][f, 0, :q_rows], mats[0, 0, 0], preferred_element_type=jnp.float32
                ).astype(jnp.bfloat16)
                o_out[0, 0, f, t] = jnp.dot(
                    parts[d][f, 0, q_rows:], mats[0, 0, 1], preferred_element_type=jnp.float32
                ).astype(jnp.bfloat16)

    rows = q_rows + o_rows
    in_specs = [pl.BlockSpec((blocks, 1, rows, LANES), lambda j, at: (at[1], j, 0, 0))]
    in_specs += [pl.BlockSpec((blocks, 1, rows, LANES), lambda j, at: (0, j, 0, 0))] * len(came)
    in_specs += [
        pl.BlockSpec((1, 1) + matrices.shape[2:], lambda j, at: (layer, slots[0] + j, 0, 0, 0))
    ]
    args = [own, *came, matrices]
    aliases = {}
    if outs is not None:
        in_specs += [pl.BlockSpec(memory_space=pl.ANY)] * 2
        aliases = {1 + len(args): 0, 2 + len(args): 1}
        args += list(outs)
    work = t_ways * blocks * len(slots) * rows
    return pl.pallas_call(
        kernel,
        grid_spec=pltpu.PrefetchScalarGridSpec(
            num_scalar_prefetch=1,
            grid=(len(slots),),
            in_specs=in_specs,
            out_specs=[
                pl.BlockSpec(
                    (1, 1) + shape.shape[2:], lambda j, at: (layer, slots[0] + j, 0, 0, 0, 0)
                )
                for shape in shapes
            ],
        ),
        out_shape=shapes,
        input_output_aliases=aliases,
        compiler_params=pltpu.CompilerParams(vmem_limit_bytes=VMEM_LIMIT),
        cost_estimate=pl.CostEstimate(
            flops=2 * work * LANES * KVR,
            transcendentals=0,
            bytes_accessed=2 * work * (LANES + KVR),
        ),
        name="absorb",
    )(where, *args)


def absorb_plain(me, own, came, matrices):
    t_ways = len(came) + 1
    order = lax.rem(me - jnp.arange(t_ways, dtype=jnp.int32) + t_ways, jnp.int32(t_ways))
    rows = jnp.take(jnp.stack([own, *came]), order, axis=0).transpose(2, 1, 0, 3, 4)
    cut = rows.shape[3] * QR // (QR + D)
    return tuple(
        jnp.einsum("hrc,hck->hrk", part, mats, preferred_element_type=jnp.float32).astype(jnp.bfloat16)
        for part, mats in (
            (rows[:, :, :, :cut].reshape(rows.shape[0], -1, LANES), matrices[:, 0]),
            (rows[:, :, :, cut:].reshape(rows.shape[0], -1, LANES), matrices[:, 1]),
        )
    )


def per_device(learner_flat, param_offsets, owner_map, slice_map):
    f_ways, t_ways = lax.axis_size("fsdp"), lax.axis_size("tp")
    layer_count = learner_flat.shape[0]
    per_group = owner_map.shape[1] // f_ways
    widths = piece_widths(f_ways * t_ways)
    granule = functools.reduce(math.gcd, widths)
    table = learner_flat.reshape(layer_count, -1, granule // LANES, LANES)
    whole_tiles = granule % (16 * LANES) == 0
    row_counts = [width // LANES for width in widths]
    rows_total = row_counts[QUERY] + row_counts[OUT]

    me = lax.axis_index("tp")
    slice_row = lax.dynamic_index_in_dim(slice_map, lax.axis_index("fsdp"), 0, keepdims=False)
    blocks = f_ways // t_ways

    def packed(layers, slots, kinds):
        return pack(table, param_offsets, owner_map, f_ways, widths, granule, layers, slots, kinds)

    def over_fsdp(x):
        return lax.all_to_all(x, "fsdp", split_axis=0, concat_axis=0, tiled=True)

    pairs = over_fsdp(packed(range(layer_count), range(per_group), (KEY, VALUE)))
    pairs = pairs.reshape(f_ways, layer_count, per_group, 2, row_counts[KEY], LANES)
    pairs = spread(pairs, "tp", t_ways, me)

    half = max(1, per_group // 2)
    chunks = [
        (layer, range(at, at + half)) for layer in range(layer_count) for at in range(0, per_group, half)
    ]
    exchanged = []
    for layer, slots in chunks:
        rows = over_fsdp(packed((layer,), slots, (QUERY, OUT)))
        rows = rows.reshape(f_ways, len(slots), rows_total, LANES)
        came = []
        for shift in range(1, t_ways):
            block = slice_row[lax.rem(me + shift, t_ways)]
            piece = lax.dynamic_slice_in_dim(rows, block * blocks, blocks, 0)
            came.append(lax.ppermute(piece, "tp", [(i, (i + shift) % t_ways) for i in range(t_ways)]))
        exchanged.append((rows, came))

    if not whole_tiles:
        order = lax.rem(me - jnp.arange(t_ways, dtype=jnp.int32) + t_ways, jnp.int32(t_ways))
        matrices = jnp.take(jnp.stack(pairs), order, axis=0).transpose(2, 3, 4, 1, 0, 5, 6)
        matrices = matrices.reshape(layer_count, per_group, 2, -1, KVR)
        done = [
            absorb_plain(
                me,
                lax.dynamic_slice_in_dim(rows, slice_row[me] * blocks, blocks, 0),
                came,
                matrices[layer, slots[0] : slots[-1] + 1],
            )
            for (layer, slots), (rows, came) in zip(chunks, exchanged)
        ]
        return tuple(
            jnp.concatenate(kind).reshape(layer_count, per_group, -1, KVR) for kind in zip(*done)
        )

    matrices = assemble(me, pairs)
    shapes = tuple(
        jax.ShapeDtypeStruct(
            (layer_count, per_group, blocks, t_ways, row_counts[kind], KVR), jnp.bfloat16
        )
        for kind in (QUERY, OUT)
    )
    where = jnp.stack([me, slice_row[me]])
    outs = None
    for (layer, slots), (rows, came) in zip(chunks, exchanged):
        outs = absorb(where, layer, slots, rows, came, matrices, outs, shapes)
    return tuple(out.reshape(layer_count, per_group, -1, KVR) for out in outs)


def solution(mesh):
    placed = (P(None, ("fsdp", "tp")), P(), P(), P())
    return jax.shard_map(
        per_device,
        mesh=mesh,
        in_specs=placed,
        out_specs=(P(None, "fsdp", "tp", None), P(None, "fsdp", "tp", None)),
        check_vma=False,
    )
```

```python
import functools
import math

import jax
import jax.numpy as jnp
from jax import lax
from jax.experimental import pallas as pl
from jax.experimental.pallas import tpu as pltpu
from jax.sharding import PartitionSpec as P

D = 7168
QR = 1536
KVR = 512
QK_NOPE = 128
V_DIM = 128
LANES = 128
QUERY, KEY, VALUE, OUT = range(4)
VMEM_LIMIT = 16 * 1024 * 1024


def piece_widths(rank_total):
    return (
        QR * QK_NOPE // rank_total,
        QK_NOPE * KVR // rank_total,
        V_DIM * KVR // rank_total,
        D * V_DIM // rank_total,
    )


def pack(table, param_offsets, owner_map, ways, widths, granule, chunks, kinds):
    head_count = owner_map.shape[1]
    steps = [widths[kind] // granule for kind in kinds]
    starts = [sum(steps[:i]) for i in range(len(kinds))]
    outs = [
        jax.ShapeDtypeStruct(
            (ways, len(layers), len(slots), sum(steps)) + table.shape[2:], table.dtype
        )
        for layers, slots in chunks
    ]

    def kernel(offsets, owners, source, *refs):
        targets, taken = refs[:-1], refs[-1]
        for layer in sorted({layer for layers, _ in chunks for layer in layers}):
            for way in range(ways):
                taken[way] = 0
            here = [
                (target, layers.index(layer), slots)
                for target, (layers, slots) in zip(targets, chunks)
                if layer in layers
            ]

            def one_head(head):
                way = owners[layer, head]
                slot = taken[way]
                taken[way] = slot + 1
                begins = [lax.div(offsets[layer, head, kind], jnp.int32(granule)) for kind in kinds]
                for target, at, slots in here:

                    @pl.when(jnp.logical_and(slot >= slots[0], slot <= slots[-1]))
                    def _():
                        for begin, step, start in zip(begins, steps, starts):
                            target[way, at, slot - slots[0], pl.ds(start, step)] = source[
                                layer, pl.ds(begin, step)
                            ]

            pl.loop(0, head_count, unroll=min(8, head_count))(one_head)

    return pl.pallas_call(
        kernel,
        out_shape=outs,
        in_specs=[
            pl.BlockSpec(memory_space=pltpu.SMEM),
            pl.BlockSpec(memory_space=pltpu.SMEM),
            pl.BlockSpec(memory_space=pltpu.VMEM),
        ],
        out_specs=[pl.BlockSpec(memory_space=pltpu.VMEM)] * len(outs),
        scratch_shapes=[pltpu.SMEM((ways,), jnp.int32)],
        compiler_params=pltpu.CompilerParams(vmem_limit_bytes=VMEM_LIMIT),
        cost_estimate=pl.CostEstimate(
            flops=0,
            transcendentals=0,
            bytes_accessed=sum(2 * 2 * math.prod(out.shape) for out in outs),
        ),
        name="pack",
    )(param_offsets, owner_map, table)


def line_step(up, down, axis, ways):
    return (
        lax.ppermute(up, axis, [(i, i + 1) for i in range(ways - 1)]),
        lax.ppermute(down, axis, [(i + 1, i) for i in range(ways - 1)]),
    )


def assemble(me, spread_parts):
    t_ways = len(spread_parts)
    f_ways, layers, heads, kinds, rows, _ = spread_parts[0].shape
    depth = t_ways * f_ways * rows * LANES // KVR
    cuts = KVR // LANES

    def kernel(me_ref, *refs):
        pieces, (out, scratch) = refs[:t_ways], refs[t_ways:]
        for kind in range(kinds):
            for d in range(t_ways):
                t = lax.rem(me_ref[0] - d + t_ways, t_ways)
                for f in range(f_ways):
                    scratch[pl.ds(pl.multiple_of((f * t_ways + t) * rows, rows), rows), :] = pieces[
                        d
                    ][f, 0, 0, kind].astype(jnp.float32)
            for cut in range(cuts):
                out[0, 0, kind, :, pl.ds(cut * LANES, LANES)] = scratch[
                    pl.ds(cut, depth, stride=cuts), :
                ].astype(jnp.bfloat16)

    return pl.pallas_call(
        kernel,
        grid_spec=pltpu.PrefetchScalarGridSpec(
            num_scalar_prefetch=1,
            grid=(layers, heads),
            in_specs=[
                pl.BlockSpec((f_ways, 1, 1, kinds, rows, LANES), lambda l, j, _: (0, l, j, 0, 0, 0))
            ]
            * t_ways,
            out_specs=pl.BlockSpec((1, 1, kinds, depth, KVR), lambda l, j, _: (l, j, 0, 0, 0)),
            scratch_shapes=[pltpu.VMEM((depth * cuts, LANES), jnp.float32)],
        ),
        out_shape=jax.ShapeDtypeStruct((layers, heads, kinds, depth, KVR), spread_parts[0].dtype),
        compiler_params=pltpu.CompilerParams(vmem_limit_bytes=VMEM_LIMIT),
        name="assemble",
    )(me.reshape(1), *spread_parts)


def absorb(where, layer, slots, own, came, matrices, outs, shapes):
    t_ways = len(came) + 1
    blocks = came[0].shape[0]
    q_rows, o_rows = shapes[0].shape[4], shapes[1].shape[4]

    def kernel(at, *refs):
        parts, mats = refs[:t_ways], refs[t_ways]
        q_out, o_out = refs[-2:]
        for d in range(t_ways):
            t = lax.rem(at[0] - d + t_ways, t_ways)
            for f in range(blocks):
                q_out[0, 0, f, t] = jnp.dot(
                    parts[d][f, 0, :q_rows], mats[0, 0, 0], preferred_element_type=jnp.float32
                ).astype(jnp.bfloat16)
                o_out[0, 0, f, t] = jnp.dot(
                    parts[d][f, 0, q_rows:], mats[0, 0, 1], preferred_element_type=jnp.float32
                ).astype(jnp.bfloat16)

    rows = q_rows + o_rows
    in_specs = [pl.BlockSpec((blocks, 1, rows, LANES), lambda j, at: (at[1], j, 0, 0))]
    in_specs += [pl.BlockSpec((blocks, 1, rows, LANES), lambda j, at: (0, j, 0, 0))] * len(came)
    in_specs += [
        pl.BlockSpec((1, 1) + matrices.shape[2:], lambda j, at: (layer, slots[0] + j, 0, 0, 0))
    ]
    args = [own, *came, matrices]
    aliases = {}
    if outs is not None:
        in_specs += [pl.BlockSpec(memory_space=pl.ANY)] * 2
        aliases = {1 + len(args): 0, 2 + len(args): 1}
        args += list(outs)
    work = t_ways * blocks * len(slots) * rows
    return pl.pallas_call(
        kernel,
        grid_spec=pltpu.PrefetchScalarGridSpec(
            num_scalar_prefetch=1,
            grid=(len(slots),),
            in_specs=in_specs,
            out_specs=[
                pl.BlockSpec(
                    (1, 1) + shape.shape[2:], lambda j, at: (layer, slots[0] + j, 0, 0, 0, 0)
                )
                for shape in shapes
            ],
        ),
        out_shape=shapes,
        input_output_aliases=aliases,
        compiler_params=pltpu.CompilerParams(vmem_limit_bytes=VMEM_LIMIT),
        cost_estimate=pl.CostEstimate(
            flops=2 * work * LANES * KVR,
            transcendentals=0,
            bytes_accessed=2 * work * (LANES + KVR),
        ),
        name="absorb",
    )(where, *args)


def absorb_plain(me, own, came, matrices):
    t_ways = len(came) + 1
    order = lax.rem(me - jnp.arange(t_ways, dtype=jnp.int32) + t_ways, jnp.int32(t_ways))
    rows = jnp.take(jnp.stack([own, *came]), order, axis=0).transpose(2, 1, 0, 3, 4)
    cut = rows.shape[3] * QR // (QR + D)
    return tuple(
        jnp.einsum("hrc,hck->hrk", part, mats, preferred_element_type=jnp.float32).astype(jnp.bfloat16)
        for part, mats in (
            (rows[:, :, :, :cut].reshape(rows.shape[0], -1, LANES), matrices[:, 0]),
            (rows[:, :, :, cut:].reshape(rows.shape[0], -1, LANES), matrices[:, 1]),
        )
    )


def per_device(learner_flat, param_offsets, owner_map, slice_map):
    f_ways, t_ways = lax.axis_size("fsdp"), lax.axis_size("tp")
    layer_count = learner_flat.shape[0]
    per_group = owner_map.shape[1] // f_ways
    widths = piece_widths(f_ways * t_ways)
    granule = functools.reduce(math.gcd, widths)
    table = learner_flat.reshape(layer_count, -1, granule // LANES, LANES)
    whole_tiles = granule % (16 * LANES) == 0
    row_counts = [width // LANES for width in widths]
    rows_total = row_counts[QUERY] + row_counts[OUT]

    me = lax.axis_index("tp")
    slice_row = lax.dynamic_index_in_dim(slice_map, lax.axis_index("fsdp"), 0, keepdims=False)
    blocks = f_ways // t_ways

    half = max(1, per_group // 2)
    chunks = [
        (layer, range(at, at + half)) for layer in range(layer_count) for at in range(0, per_group, half)
    ]

    def packed(of, kinds):
        return pack(table, param_offsets, owner_map, f_ways, widths, granule, of, kinds)

    def over_fsdp(x):
        return lax.all_to_all(x, "fsdp", split_axis=0, concat_axis=0, tiled=True)

    def over_tp(rows):
        came = []
        for shift in range(1, t_ways):
            block = slice_row[lax.rem(me + shift, t_ways)]
            piece = lax.dynamic_slice_in_dim(rows, block * blocks, blocks, 0)
            came.append(lax.ppermute(piece, "tp", [(i, (i + shift) % t_ways) for i in range(t_ways)]))
        return came

    (pairs,) = packed([(range(layer_count), range(per_group))], (KEY, VALUE))
    to_send = packed([((layer,), slots) for layer, slots in chunks], (QUERY, OUT))
    pairs = over_fsdp(pairs).reshape(f_ways, layer_count, per_group, 2, row_counts[KEY], LANES)

    shapes = tuple(
        jax.ShapeDtypeStruct(
            (layer_count, per_group, blocks, t_ways, row_counts[kind], KVR), jnp.bfloat16
        )
        for kind in (QUERY, OUT)
    )
    where = jnp.stack([me, slice_row[me]])
    up, down = [pairs], [pairs]
    exchanged, came, rows, outs, matrices = [], None, None, None, None
    for stage in range(len(chunks) + 2):
        arriving = over_tp(rows) if rows is not None else None
        for _ in range(2 if stage == 0 else t_ways):
            if len(up) < t_ways:
                above, below = line_step(up[-1], down[-1], "tp", t_ways)
                up.append(above)
                down.append(below)
        following = None
        if stage < len(chunks):
            following = over_fsdp(to_send[stage])
            following = following.reshape(f_ways, len(chunks[stage][1]), rows_total, LANES)
        if came is not None:
            exchanged.append((settled, came))
            if whole_tiles:
                if matrices is None:
                    near = [jnp.where(me >= d, up[d], down[t_ways - d]) for d in range(1, t_ways)]
                    matrices = assemble(me, [pairs] + near)
                layer, slots = chunks[stage - 2]
                outs = absorb(where, layer, slots, settled, came, matrices, outs, shapes)
        arriving, following, up, down, to_send, outs, matrices = lax.optimization_barrier(
            (arriving, following, up, down, to_send, outs, matrices)
        )
        settled, came, rows = rows, arriving, following
    if whole_tiles:
        return tuple(out.reshape(layer_count, per_group, -1, KVR) for out in outs)

    near = [jnp.where(me >= d, up[d], down[t_ways - d]) for d in range(1, t_ways)]
    order = lax.rem(me - jnp.arange(t_ways, dtype=jnp.int32) + t_ways, jnp.int32(t_ways))
    matrices = jnp.take(jnp.stack([pairs] + near), order, axis=0).transpose(2, 3, 4, 1, 0, 5, 6)
    matrices = matrices.reshape(layer_count, per_group, 2, -1, KVR)
    done = [
        absorb_plain(
            me,
            lax.dynamic_slice_in_dim(rows, slice_row[me] * blocks, blocks, 0),
            came,
            matrices[layer, slots[0] : slots[-1] + 1],
        )
        for (layer, slots), (rows, came) in zip(chunks, exchanged)
    ]
    return tuple(jnp.concatenate(kind).reshape(layer_count, per_group, -1, KVR) for kind in zip(*done))


def solution(mesh):
    placed = (P(None, ("fsdp", "tp")), P(), P(), P())
    return jax.shard_map(
        per_device,
        mesh=mesh,
        in_specs=placed,
        out_specs=(P(None, "fsdp", "tp", None), P(None, "fsdp", "tp", None)),
        check_vma=False,
    )
```

```python
import functools
import math

import jax
import jax.numpy as jnp
from jax import lax
from jax.experimental import pallas as pl
from jax.experimental.pallas import tpu as pltpu
from jax.sharding import PartitionSpec as P

D = 7168
QR = 1536
KVR = 512
QK_NOPE = 128
V_DIM = 128
LANES = 128
QUERY, KEY, VALUE, OUT = range(4)
VMEM_LIMIT = 16 * 1024 * 1024


def piece_widths(rank_total):
    return (
        QR * QK_NOPE // rank_total,
        QK_NOPE * KVR // rank_total,
        V_DIM * KVR // rank_total,
        D * V_DIM // rank_total,
    )


def pack(table, param_offsets, owner_map, ways, widths, granule, chunks, kinds, waits=()):
    head_count = owner_map.shape[1]
    steps = [widths[kind] // granule for kind in kinds]
    starts = [sum(steps[:i]) for i in range(len(kinds))]
    outs = [
        jax.ShapeDtypeStruct(
            (ways, len(layers), len(slots), sum(steps)) + table.shape[2:], table.dtype
        )
        for layers, slots in chunks
    ]

    def kernel(offsets, owners, source, *refs):
        targets, taken = refs[len(waits) : -1], refs[-1]
        for layer in sorted({layer for layers, _ in chunks for layer in layers}):
            for way in range(ways):
                taken[way] = 0
            here = [
                (target, layers.index(layer), slots)
                for target, (layers, slots) in zip(targets, chunks)
                if layer in layers
            ]

            def one_head(head):
                way = owners[layer, head]
                slot = taken[way]
                taken[way] = slot + 1
                begins = [lax.div(offsets[layer, head, kind], jnp.int32(granule)) for kind in kinds]
                for target, at, slots in here:

                    @pl.when(jnp.logical_and(slot >= slots[0], slot <= slots[-1]))
                    def _():
                        for begin, step, start in zip(begins, steps, starts):
                            target[way, at, slot - slots[0], pl.ds(start, step)] = source[
                                layer, pl.ds(begin, step)
                            ]

            pl.loop(0, head_count, unroll=min(8, head_count))(one_head)

    return pl.pallas_call(
        kernel,
        out_shape=outs,
        in_specs=[
            pl.BlockSpec(memory_space=pltpu.SMEM),
            pl.BlockSpec(memory_space=pltpu.SMEM),
            pl.BlockSpec(memory_space=pltpu.VMEM),
        ]
        + [pl.BlockSpec(memory_space=pl.ANY)] * len(waits),
        out_specs=[pl.BlockSpec(memory_space=pltpu.VMEM)] * len(outs),
        scratch_shapes=[pltpu.SMEM((ways,), jnp.int32)],
        compiler_params=pltpu.CompilerParams(vmem_limit_bytes=VMEM_LIMIT),
        cost_estimate=pl.CostEstimate(
            flops=0,
            transcendentals=0,
            bytes_accessed=sum(2 * 2 * math.prod(out.shape) for out in outs),
        ),
        name="pack",
    )(param_offsets, owner_map, table, *waits)


def line_step(up, down, axis, ways):
    return (
        lax.ppermute(up, axis, [(i, i + 1) for i in range(ways - 1)]),
        lax.ppermute(down, axis, [(i + 1, i) for i in range(ways - 1)]),
    )


def assemble(me, spread_parts):
    t_ways = len(spread_parts)
    f_ways, layers, heads, kinds, rows, _ = spread_parts[0].shape
    depth = t_ways * f_ways * rows * LANES // KVR
    cuts = KVR // LANES

    def kernel(me_ref, *refs):
        pieces, (out, scratch) = refs[:t_ways], refs[t_ways:]
        for kind in range(kinds):
            for d in range(t_ways):
                t = lax.rem(me_ref[0] - d + t_ways, t_ways)
                for f in range(f_ways):
                    scratch[pl.ds(pl.multiple_of((f * t_ways + t) * rows, rows), rows), :] = pieces[
                        d
                    ][f, 0, 0, kind].astype(jnp.float32)
            for cut in range(cuts):
                out[0, 0, kind, :, pl.ds(cut * LANES, LANES)] = scratch[
                    pl.ds(cut, depth, stride=cuts), :
                ].astype(jnp.bfloat16)

    return pl.pallas_call(
        kernel,
        grid_spec=pltpu.PrefetchScalarGridSpec(
            num_scalar_prefetch=1,
            grid=(layers, heads),
            in_specs=[
                pl.BlockSpec((f_ways, 1, 1, kinds, rows, LANES), lambda l, j, _: (0, l, j, 0, 0, 0))
            ]
            * t_ways,
            out_specs=pl.BlockSpec((1, 1, kinds, depth, KVR), lambda l, j, _: (l, j, 0, 0, 0)),
            scratch_shapes=[pltpu.VMEM((depth * cuts, LANES), jnp.float32)],
        ),
        out_shape=jax.ShapeDtypeStruct((layers, heads, kinds, depth, KVR), spread_parts[0].dtype),
        compiler_params=pltpu.CompilerParams(vmem_limit_bytes=VMEM_LIMIT),
        name="assemble",
    )(me.reshape(1), *spread_parts)


def absorb(where, layer, slots, own, came, matrices, outs, shapes):
    t_ways = len(came) + 1
    blocks = came[0].shape[0]
    q_rows, o_rows = shapes[0].shape[4], shapes[1].shape[4]

    def kernel(at, *refs):
        parts, mats = refs[:t_ways], refs[t_ways]
        q_out, o_out = refs[-2:]
        for d in range(t_ways):
            t = lax.rem(at[0] - d + t_ways, t_ways)
            q_out[0, 0, 0, t] = jnp.dot(
                parts[d][0, 0, :q_rows], mats[0, 0, 0], preferred_element_type=jnp.float32
            ).astype(jnp.bfloat16)
            o_out[0, 0, 0, t] = jnp.dot(
                parts[d][0, 0, q_rows:], mats[0, 0, 1], preferred_element_type=jnp.float32
            ).astype(jnp.bfloat16)

    rows = q_rows + o_rows
    in_specs = [pl.BlockSpec((1, 1, rows, LANES), lambda j, f, at: (at[1] * blocks + f, j, 0, 0))]
    in_specs += [pl.BlockSpec((1, 1, rows, LANES), lambda j, f, at: (f, j, 0, 0))] * len(came)
    in_specs += [
        pl.BlockSpec((1, 1) + matrices.shape[2:], lambda j, f, at: (layer, slots[0] + j, 0, 0, 0))
    ]
    args = [own, *came, matrices]
    aliases = {}
    if outs is not None:
        in_specs += [pl.BlockSpec(memory_space=pl.ANY)] * 2
        aliases = {1 + len(args): 0, 2 + len(args): 1}
        args += list(outs)
    work = t_ways * blocks * len(slots) * rows
    return pl.pallas_call(
        kernel,
        grid_spec=pltpu.PrefetchScalarGridSpec(
            num_scalar_prefetch=1,
            grid=(len(slots), blocks),
            in_specs=in_specs,
            out_specs=[
                pl.BlockSpec(
                    (1, 1, 1) + shape.shape[3:], lambda j, f, at: (layer, slots[0] + j, f, 0, 0, 0)
                )
                for shape in shapes
            ],
        ),
        out_shape=shapes,
        input_output_aliases=aliases,
        compiler_params=pltpu.CompilerParams(vmem_limit_bytes=VMEM_LIMIT),
        cost_estimate=pl.CostEstimate(
            flops=2 * work * LANES * KVR,
            transcendentals=0,
            bytes_accessed=2 * work * (LANES + KVR),
        ),
        name="absorb",
    )(where, *args)


def absorb_plain(me, own, came, matrices):
    t_ways = len(came) + 1
    order = lax.rem(me - jnp.arange(t_ways, dtype=jnp.int32) + t_ways, jnp.int32(t_ways))
    rows = jnp.take(jnp.stack([own, *came]), order, axis=0).transpose(2, 1, 0, 3, 4)
    cut = rows.shape[3] * QR // (QR + D)
    return tuple(
        jnp.einsum("hrc,hck->hrk", part, mats, preferred_element_type=jnp.float32).astype(jnp.bfloat16)
        for part, mats in (
            (rows[:, :, :, :cut].reshape(rows.shape[0], -1, LANES), matrices[:, 0]),
            (rows[:, :, :, cut:].reshape(rows.shape[0], -1, LANES), matrices[:, 1]),
        )
    )


def per_device(learner_flat, param_offsets, owner_map, slice_map):
    f_ways, t_ways = lax.axis_size("fsdp"), lax.axis_size("tp")
    layer_count = learner_flat.shape[0]
    per_group = owner_map.shape[1] // f_ways
    widths = piece_widths(f_ways * t_ways)
    granule = functools.reduce(math.gcd, widths)
    table = learner_flat.reshape(layer_count, -1, granule // LANES, LANES)
    whole_tiles = granule % (16 * LANES) == 0
    row_counts = [width // LANES for width in widths]
    rows_total = row_counts[QUERY] + row_counts[OUT]

    me = lax.axis_index("tp")
    slice_row = lax.dynamic_index_in_dim(slice_map, lax.axis_index("fsdp"), 0, keepdims=False)
    blocks = f_ways // t_ways
    half = max(1, per_group // 2)
    chunks = [
        (layer, range(at, at + half)) for layer in range(layer_count) for at in range(0, per_group, half)
    ]
    shifts = range(1, t_ways)
    early = [shift for shift in shifts if 2 * shift != t_ways]

    def packed(of, kinds, waits=()):
        return pack(table, param_offsets, owner_map, f_ways, widths, granule, of, kinds, waits)

    def over_fsdp(x):
        return lax.all_to_all(x, "fsdp", split_axis=0, concat_axis=0, tiled=True)

    (pairs,) = packed([(range(layer_count), range(per_group))], (KEY, VALUE))
    pairs = over_fsdp(pairs).reshape(f_ways, layer_count, per_group, 2, row_counts[KEY], LANES)
    up, down = [pairs], [pairs]
    for _ in shifts:
        above, below = line_step(up[-1], down[-1], "tp", t_ways)
        up.append(above)
        down.append(below)

    targets = jnp.stack([slice_row[lax.rem(me + shift, t_ways)] for shift in range(t_ways)])
    exchanged, sent = [], []
    for at, (layer, slots) in enumerate(chunks):
        waits = [targets]
        if at >= 1:
            waits += sent[at - 1] + up[1:3] + down[1:3]
        if at >= 2:
            waits += up[3:] + down[3:] + [exchanged[at - 2][1][shift - 1] for shift in early]
        if at >= 3:
            waits += exchanged[at - 3][1]
        (rows,) = packed([((layer,), slots)], (QUERY, OUT), waits)
        rows = over_fsdp(rows).reshape(f_ways, len(slots), rows_total, LANES)
        pieces = [
            lax.dynamic_slice_in_dim(rows, targets[shift] * blocks, blocks, 0) for shift in shifts
        ]
        sent.append(pieces)
        came = [
            lax.ppermute(piece, "tp", [(i, (i + shift) % t_ways) for i in range(t_ways)])
            for shift, piece in zip(shifts, pieces)
        ]
        exchanged.append((rows, came))
    near = [jnp.where(me >= d, up[d], down[t_ways - d]) for d in shifts]

    if whole_tiles:
        shapes = tuple(
            jax.ShapeDtypeStruct(
                (layer_count, per_group, blocks, t_ways, row_counts[kind], KVR), jnp.bfloat16
            )
            for kind in (QUERY, OUT)
        )
        where = jnp.stack([me, targets[0]])
        matrices = assemble(me, [pairs] + near)
        outs = None
        for (layer, slots), (rows, came) in zip(chunks, exchanged):
            outs = absorb(where, layer, slots, rows, came, matrices, outs, shapes)
        return tuple(out.reshape(layer_count, per_group, -1, KVR) for out in outs)

    order = lax.rem(me - jnp.arange(t_ways, dtype=jnp.int32) + t_ways, jnp.int32(t_ways))
    matrices = jnp.take(jnp.stack([pairs] + near), order, axis=0).transpose(2, 3, 4, 1, 0, 5, 6)
    matrices = matrices.reshape(layer_count, per_group, 2, -1, KVR)
    done = [
        absorb_plain(
            me,
            lax.dynamic_slice_in_dim(rows, targets[0] * blocks, blocks, 0),
            came,
            matrices[layer, slots[0] : slots[-1] + 1],
        )
        for (layer, slots), (rows, came) in zip(chunks, exchanged)
    ]
    return tuple(jnp.concatenate(kind).reshape(layer_count, per_group, -1, KVR) for kind in zip(*done))


def solution(mesh):
    placed = (P(None, ("fsdp", "tp")), P(), P(), P())
    return jax.shard_map(
        per_device,
        mesh=mesh,
        in_specs=placed,
        out_specs=(P(None, "fsdp", "tp", None), P(None, "fsdp", "tp", None)),
        check_vma=False,
    )
```

```python
import functools
import math

import jax
import jax.numpy as jnp
from jax import lax
from jax.experimental import pallas as pl
from jax.experimental.pallas import tpu as pltpu
from jax.sharding import PartitionSpec as P

D = 7168
QR = 1536
KVR = 512
QK_NOPE = 128
V_DIM = 128
LANES = 128
QUERY, KEY, VALUE, OUT = range(4)
HOLD_PAIRS = 2
HOLD_CHUNK = 30
VMEM_LIMIT = 16 * 1024 * 1024


def piece_widths(rank_total):
    return (
        QR * QK_NOPE // rank_total,
        QK_NOPE * KVR // rank_total,
        V_DIM * KVR // rank_total,
        D * V_DIM // rank_total,
    )


def pack(table, param_offsets, owner_map, ways, widths, granule, chunks, waits=()):
    layer_count, head_count = owner_map.shape
    per_group = head_count // ways
    steps = [[widths[kind] // granule for kind in kinds] for _, kinds in chunks]
    outs = [
        jax.ShapeDtypeStruct((ways, len(items), sum(step)) + table.shape[2:], table.dtype)
        for (items, _), step in zip(chunks, steps)
    ]

    def kernel(offsets, owners, source, *refs):
        targets, taken = refs[len(waits) : -1], refs[-1]
        for layer in range(layer_count):
            first = layer * per_group
            here = []
            for target, (items, kinds), step in zip(targets, chunks, steps):
                low, high = max(items[0], first), min(items[-1] + 1, first + per_group)
                if low < high:
                    here.append((target, kinds, step, low - first, high - first, first - items[0]))
            if not here:
                continue
            for way in range(ways):
                taken[way] = 0

            def one_head(head):
                way = owners[layer, head]
                slot = taken[way]
                taken[way] = slot + 1

                def move(target, kinds, step, shift):
                    start = 0
                    for kind, size in zip(kinds, step):
                        begin = lax.div(offsets[layer, head, kind], jnp.int32(granule))
                        target[way, slot + shift, pl.ds(start, size)] = source[layer, pl.ds(begin, size)]
                        start += size

                for target, kinds, step, low, high, shift in here:
                    if (low, high) == (0, per_group):
                        move(target, kinds, step, shift)
                    else:
                        pl.when(jnp.logical_and(slot >= low, slot < high))(
                            functools.partial(move, target, kinds, step, shift)
                        )

            pl.loop(0, head_count, unroll=min(8, head_count))(one_head)

    return pl.pallas_call(
        kernel,
        out_shape=outs,
        in_specs=[
            pl.BlockSpec(memory_space=pltpu.SMEM),
            pl.BlockSpec(memory_space=pltpu.SMEM),
            pl.BlockSpec(memory_space=pltpu.VMEM),
        ]
        + [pl.BlockSpec(memory_space=pl.ANY)] * len(waits),
        out_specs=[pl.BlockSpec(memory_space=pltpu.VMEM)] * len(outs),
        scratch_shapes=[pltpu.SMEM((ways,), jnp.int32)],
        compiler_params=pltpu.CompilerParams(vmem_limit_bytes=VMEM_LIMIT),
        cost_estimate=pl.CostEstimate(
            flops=0,
            transcendentals=0,
            bytes_accessed=sum(2 * 2 * math.prod(out.shape) for out in outs),
        ),
        name="pack",
    )(param_offsets, owner_map, table, *waits)


def first_of(x):
    return lax.slice(x, (0,) * x.ndim, (1,) * x.ndim).reshape(1)


def hold(small, waits, micros):
    def kernel(small_in, *refs):
        for i in range(small.shape[0]):
            refs[-1][i] = small_in[i]

    return pl.pallas_call(
        kernel,
        out_shape=jax.ShapeDtypeStruct(small.shape, small.dtype),
        in_specs=[pl.BlockSpec(memory_space=pltpu.SMEM)]
        + [pl.BlockSpec(memory_space=pl.ANY)] * len(waits),
        out_specs=pl.BlockSpec(memory_space=pltpu.SMEM),
        cost_estimate=pl.CostEstimate(
            flops=int(micros * 1.15e9), transcendentals=0, bytes_accessed=0
        ),
        name="hold",
    )(small, *[first_of(x) for x in waits])


def cut(rows, targets, blocks, shifts):
    shape = (blocks,) + rows.shape[1:]

    def kernel(at, source, *pieces):
        for shift, piece in zip(shifts, pieces):
            for f in range(blocks):
                piece[f] = source[at[shift] * blocks + f]

    return pl.pallas_call(
        kernel,
        out_shape=[jax.ShapeDtypeStruct(shape, rows.dtype)] * len(shifts),
        in_specs=[pl.BlockSpec(memory_space=pltpu.SMEM), pl.BlockSpec(memory_space=pltpu.VMEM)],
        out_specs=[pl.BlockSpec(memory_space=pltpu.VMEM)] * len(shifts),
        compiler_params=pltpu.CompilerParams(vmem_limit_bytes=VMEM_LIMIT),
        cost_estimate=pl.CostEstimate(
            flops=0, transcendentals=0, bytes_accessed=4 * len(shifts) * math.prod(shape)
        ),
        name="cut",
    )(targets, rows)


def line_step(up, down, axis, ways):
    return (
        lax.ppermute(up, axis, [(i, i + 1) for i in range(ways - 1)]),
        lax.ppermute(down, axis, [(i + 1, i) for i in range(ways - 1)]),
    )


def assemble(me, spread_parts):
    t_ways = len(spread_parts)
    f_ways, items, kinds, rows, _ = spread_parts[0].shape
    depth = t_ways * f_ways * rows * LANES // KVR
    cuts = KVR // LANES

    def kernel(me_ref, *refs):
        pieces, (out, scratch) = refs[:t_ways], refs[t_ways:]
        for kind in range(kinds):
            for d in range(t_ways):
                t = lax.rem(me_ref[0] - d + t_ways, t_ways)
                for f in range(f_ways):
                    scratch[pl.ds(pl.multiple_of((f * t_ways + t) * rows, rows), rows), :] = pieces[
                        d
                    ][f, 0, kind].astype(jnp.float32)
            for cut in range(cuts):
                out[0, kind, :, pl.ds(cut * LANES, LANES)] = scratch[
                    pl.ds(cut, depth, stride=cuts), :
                ].astype(jnp.bfloat16)

    return pl.pallas_call(
        kernel,
        grid_spec=pltpu.PrefetchScalarGridSpec(
            num_scalar_prefetch=1,
            grid=(items,),
            in_specs=[pl.BlockSpec((f_ways, 1, kinds, rows, LANES), lambda i, _: (0, i, 0, 0, 0))] * t_ways,
            out_specs=pl.BlockSpec((1, kinds, depth, KVR), lambda i, _: (i, 0, 0, 0)),
            scratch_shapes=[pltpu.VMEM((depth * cuts, LANES), jnp.float32)],
        ),
        out_shape=jax.ShapeDtypeStruct((items, kinds, depth, KVR), spread_parts[0].dtype),
        compiler_params=pltpu.CompilerParams(vmem_limit_bytes=VMEM_LIMIT),
        name="assemble",
    )(me.reshape(1), *spread_parts)


def absorb(where, items, own, came, matrices, outs, shapes):
    t_ways = len(came) + 1
    blocks = came[0].shape[0]
    q_rows, o_rows = shapes[0].shape[3], shapes[1].shape[3]
    rows = q_rows + o_rows

    def kernel(at, *refs):
        parts, mats = refs[:t_ways], refs[t_ways]
        q_out, o_out = refs[-2:]
        for d in range(t_ways):
            t = lax.rem(at[0] - d + t_ways, t_ways)
            for f in range(blocks):
                q_out[0, f, t] = jnp.dot(
                    parts[d][f, 0, :q_rows], mats[0, 0], preferred_element_type=jnp.float32
                ).astype(jnp.bfloat16)
                o_out[0, f, t] = jnp.dot(
                    parts[d][f, 0, q_rows:], mats[0, 1], preferred_element_type=jnp.float32
                ).astype(jnp.bfloat16)

    in_specs = [pl.BlockSpec((blocks, 1, rows, LANES), lambda j, at: (at[1], j, 0, 0))]
    in_specs += [pl.BlockSpec((blocks, 1, rows, LANES), lambda j, at: (0, j, 0, 0))] * len(came)
    in_specs += [pl.BlockSpec((1,) + matrices.shape[1:], lambda j, at: (items[0] + j, 0, 0, 0))]
    args = [own, *came, matrices]
    aliases = {}
    if outs is not None:
        in_specs += [pl.BlockSpec(memory_space=pl.ANY)] * 2
        aliases = {1 + len(args): 0, 2 + len(args): 1}
        args += list(outs)
    work = t_ways * blocks * len(items) * rows
    return pl.pallas_call(
        kernel,
        grid_spec=pltpu.PrefetchScalarGridSpec(
            num_scalar_prefetch=1,
            grid=(len(items),),
            in_specs=in_specs,
            out_specs=[
                pl.BlockSpec((1,) + shape.shape[1:], lambda j, at: (items[0] + j, 0, 0, 0, 0))
                for shape in shapes
            ],
        ),
        out_shape=shapes,
        input_output_aliases=aliases,
        compiler_params=pltpu.CompilerParams(vmem_limit_bytes=VMEM_LIMIT),
        cost_estimate=pl.CostEstimate(
            flops=2 * work * LANES * KVR,
            transcendentals=0,
            bytes_accessed=2 * work * (LANES + KVR),
        ),
        name="absorb",
    )(where, *args)


def absorb_plain(me, own, came, matrices):
    t_ways = len(came) + 1
    order = lax.rem(me - jnp.arange(t_ways, dtype=jnp.int32) + t_ways, jnp.int32(t_ways))
    rows = jnp.take(jnp.stack([own, *came]), order, axis=0).transpose(2, 1, 0, 3, 4)
    cut = rows.shape[3] * QR // (QR + D)
    return tuple(
        jnp.einsum("hrc,hck->hrk", part, mats, preferred_element_type=jnp.float32).astype(jnp.bfloat16)
        for part, mats in (
            (rows[:, :, :, :cut].reshape(rows.shape[0], -1, LANES), matrices[:, 0]),
            (rows[:, :, :, cut:].reshape(rows.shape[0], -1, LANES), matrices[:, 1]),
        )
    )


def per_device(learner_flat, param_offsets, owner_map, slice_map):
    f_ways, t_ways = lax.axis_size("fsdp"), lax.axis_size("tp")
    layer_count = learner_flat.shape[0]
    per_group = owner_map.shape[1] // f_ways
    item_count = layer_count * per_group
    widths = piece_widths(f_ways * t_ways)
    granule = functools.reduce(math.gcd, widths)
    table = learner_flat.reshape(layer_count, -1, granule // LANES, LANES)
    whole_tiles = granule % (16 * LANES) == 0
    row_counts = [width // LANES for width in widths]

    me = lax.axis_index("tp")
    slice_row = lax.dynamic_index_in_dim(slice_map, lax.axis_index("fsdp"), 0, keepdims=False)
    blocks = f_ways // t_ways
    shifts = range(1, t_ways)
    cuts = [0, item_count * 2 // 8, item_count * 5 // 8, item_count]
    chunks = [range(low, high) for low, high in zip(cuts, cuts[1:]) if low < high]

    def packed(of, waits=()):
        waits = [first_of(x) for x in waits]
        return pack(table, param_offsets, owner_map, f_ways, widths, granule, of, waits)

    def over_fsdp(x, rows):
        x = lax.all_to_all(x, "fsdp", split_axis=0, concat_axis=0, tiled=True)
        return x.reshape(x.shape[:2] + rows)

    def over_tp(rows, to):
        return [
            lax.ppermute(piece, "tp", [(i, (i + shift) % t_ways) for i in range(t_ways)])
            for shift, piece in zip(shifts, cut(rows, to, blocks, shifts))
        ]

    (pairs,) = packed([(range(item_count), (KEY, VALUE))])
    to_send = packed([(items, (QUERY, OUT)) for items in chunks])
    pairs = over_fsdp(pairs, (2, row_counts[KEY], LANES))
    targets = jnp.stack([slice_row[lax.rem(me + shift, t_ways)] for shift in range(t_ways)])
    up, down = [pairs], [pairs]
    for _ in shifts:
        above, below = line_step(up[-1], down[-1], "tp", t_ways)
        up.append(above)
        down.append(below)

    exchanged = []
    for at, items in enumerate(chunks):
        rows = over_fsdp(to_send[at], (row_counts[QUERY] + row_counts[OUT], LANES))
        waits = exchanged[at - 1][1] + up[3:] + down[3:] if at else up[1:3] + down[1:3]
        exchanged.append((rows, over_tp(rows, hold(targets, waits, HOLD_CHUNK if at else HOLD_PAIRS))))
    near = [jnp.where(me >= d, up[d], down[t_ways - d]) for d in shifts]

    if whole_tiles:
        shapes = tuple(
            jax.ShapeDtypeStruct((item_count, blocks, t_ways, row_counts[kind], KVR), jnp.bfloat16)
            for kind in (QUERY, OUT)
        )
        where = jnp.stack([me, targets[0]])
        matrices = assemble(me, [pairs] + near)
        outs = None
        for items, (rows, came) in zip(chunks, exchanged):
            outs = absorb(where, items, rows, came, matrices, outs, shapes)
        return tuple(out.reshape(layer_count, per_group, -1, KVR) for out in outs)

    order = lax.rem(me - jnp.arange(t_ways, dtype=jnp.int32) + t_ways, jnp.int32(t_ways))
    matrices = jnp.take(jnp.stack([pairs] + near), order, axis=0).transpose(2, 3, 1, 0, 4, 5)
    matrices = matrices.reshape(item_count, 2, -1, KVR)
    done = [
        absorb_plain(
            me,
            lax.dynamic_slice_in_dim(rows, targets[0] * blocks, blocks, 0),
            came,
            matrices[items[0] : items[-1] + 1],
        )
        for items, (rows, came) in zip(chunks, exchanged)
    ]
    return tuple(jnp.concatenate(kind).reshape(layer_count, per_group, -1, KVR) for kind in zip(*done))


def solution(mesh):
    placed = (P(None, ("fsdp", "tp")), P(), P(), P())
    return jax.shard_map(
        per_device,
        mesh=mesh,
        in_specs=placed,
        out_specs=(P(None, "fsdp", "tp", None), P(None, "fsdp", "tp", None)),
        check_vma=False,
    )
```

```python
import functools
import math

import jax
import jax.numpy as jnp
from jax import lax
from jax.experimental import pallas as pl
from jax.experimental.pallas import tpu as pltpu
from jax.sharding import PartitionSpec as P

D = 7168
QR = 1536
KVR = 512
QK_NOPE = 128
V_DIM = 128
LANES = 128
QUERY, KEY, VALUE, OUT = range(4)
CUT_MICROS = 10
VMEM_LIMIT = 16 * 1024 * 1024


def piece_widths(rank_total):
    return (
        QR * QK_NOPE // rank_total,
        QK_NOPE * KVR // rank_total,
        V_DIM * KVR // rank_total,
        D * V_DIM // rank_total,
    )


def pack(table, param_offsets, owner_map, ways, widths, granule, chunks):
    layer_count, head_count = owner_map.shape
    per_group = head_count // ways
    steps = [[widths[kind] // granule for kind in kinds] for _, kinds in chunks]
    outs = [
        jax.ShapeDtypeStruct((ways, len(items), sum(step)) + table.shape[2:], table.dtype)
        for (items, _), step in zip(chunks, steps)
    ]

    def kernel(offsets, owners, source, *refs):
        targets, (taken, head_at) = refs[:-2], refs[-2:]
        for layer in range(layer_count):
            for way in range(ways):
                taken[way] = layer * per_group

            def place(head):
                way = owners[layer, head]
                item = taken[way]
                taken[way] = item + 1
                head_at[item * ways + way] = head

            pl.loop(0, head_count, unroll=min(8, head_count))(place)

        for target, (items, kinds), step in zip(targets, chunks, steps):
            for at, item in enumerate(items):

                def move(way):
                    head = head_at[item * ways + way]
                    start = 0
                    for kind, size in zip(kinds, step):
                        begin = lax.div(offsets[item // per_group, head, kind], jnp.int32(granule))
                        target[way, at, pl.ds(start, size)] = source[item // per_group, pl.ds(begin, size)]
                        start += size

                pl.loop(0, ways, unroll=min(8, ways))(move)

    return pl.pallas_call(
        kernel,
        out_shape=outs,
        in_specs=[
            pl.BlockSpec(memory_space=pltpu.SMEM),
            pl.BlockSpec(memory_space=pltpu.SMEM),
            pl.BlockSpec(memory_space=pltpu.VMEM),
        ],
        out_specs=[pl.BlockSpec(memory_space=pltpu.VMEM)] * len(outs),
        scratch_shapes=[
            pltpu.SMEM((ways,), jnp.int32),
            pltpu.SMEM((layer_count * head_count,), jnp.int32),
        ],
        compiler_params=pltpu.CompilerParams(vmem_limit_bytes=VMEM_LIMIT),
        cost_estimate=pl.CostEstimate(
            flops=0,
            transcendentals=0,
            bytes_accessed=sum(2 * 2 * math.prod(out.shape) for out in outs),
        ),
        name="pack",
    )(param_offsets, owner_map, table)


def cut(rows, slice_map, blocks, shifts, waits, micros):
    shape = (blocks,) + rows.shape[1:]
    t_ways = slice_map.shape[1]

    def kernel(mapped, source, *refs):
        f_me, t_me = lax.axis_index("fsdp"), lax.axis_index("tp")
        for shift, piece in zip(shifts, refs[len(waits) :]):
            block = mapped[f_me, lax.rem(t_me + shift, t_ways)]
            for f in range(blocks):
                piece[f] = source[block * blocks + f]

    def corner(x):
        block = (1,) * (x.ndim - 2) + (min(16, x.shape[-2]), LANES)
        return pl.BlockSpec(block, lambda _: (0,) * x.ndim)

    return pl.pallas_call(
        kernel,
        grid=(1,),
        out_shape=[jax.ShapeDtypeStruct(shape, rows.dtype)] * len(shifts),
        in_specs=[pl.BlockSpec(memory_space=pltpu.SMEM), pl.BlockSpec(memory_space=pltpu.VMEM)]
        + [corner(x) for x in waits],
        out_specs=[pl.BlockSpec(memory_space=pltpu.VMEM)] * len(shifts),
        compiler_params=pltpu.CompilerParams(vmem_limit_bytes=VMEM_LIMIT),
        cost_estimate=pl.CostEstimate(
            flops=int(micros * 1.15e9),
            transcendentals=0,
            bytes_accessed=4 * len(shifts) * math.prod(shape),
        ),
        name="cut",
    )(slice_map, rows, *waits)


def line_step(up, down, axis, ways):
    return (
        lax.ppermute(up, axis, [(i, i + 1) for i in range(ways - 1)]),
        lax.ppermute(down, axis, [(i + 1, i) for i in range(ways - 1)]),
    )


def assemble(me, spread_parts):
    t_ways = len(spread_parts)
    f_ways, items, kinds, rows, _ = spread_parts[0].shape
    depth = t_ways * f_ways * rows * LANES // KVR
    cuts = KVR // LANES

    def kernel(me_ref, *refs):
        pieces, (out, scratch) = refs[:t_ways], refs[t_ways:]
        for kind in range(kinds):
            for d in range(t_ways):
                t = lax.rem(me_ref[0] - d + t_ways, t_ways)
                for f in range(f_ways):
                    scratch[pl.ds(pl.multiple_of((f * t_ways + t) * rows, rows), rows), :] = pieces[
                        d
                    ][f, 0, kind].astype(jnp.float32)
            for cut in range(cuts):
                out[0, kind, :, pl.ds(cut * LANES, LANES)] = scratch[
                    pl.ds(cut, depth, stride=cuts), :
                ].astype(jnp.bfloat16)

    return pl.pallas_call(
        kernel,
        grid_spec=pltpu.PrefetchScalarGridSpec(
            num_scalar_prefetch=1,
            grid=(items,),
            in_specs=[pl.BlockSpec((f_ways, 1, kinds, rows, LANES), lambda i, _: (0, i, 0, 0, 0))] * t_ways,
            out_specs=pl.BlockSpec((1, kinds, depth, KVR), lambda i, _: (i, 0, 0, 0)),
            scratch_shapes=[pltpu.VMEM((depth * cuts, LANES), jnp.float32)],
        ),
        out_shape=jax.ShapeDtypeStruct((items, kinds, depth, KVR), spread_parts[0].dtype),
        compiler_params=pltpu.CompilerParams(vmem_limit_bytes=VMEM_LIMIT),
        name="assemble",
    )(me.reshape(1), *spread_parts)


def absorb(where, items, own, came, matrices, outs, shapes):
    t_ways = len(came) + 1
    blocks = came[0].shape[0]
    q_rows, o_rows = shapes[0].shape[3], shapes[1].shape[3]
    rows = q_rows + o_rows

    def kernel(at, *refs):
        parts, mats = refs[:t_ways], refs[t_ways]
        q_out, o_out = refs[-2:]
        for d in range(t_ways):
            t = lax.rem(at[0] - d + t_ways, t_ways)
            for f in range(blocks):
                q_out[0, f, t] = jnp.dot(
                    parts[d][f, 0, :q_rows], mats[0, 0], preferred_element_type=jnp.float32
                ).astype(jnp.bfloat16)
                o_out[0, f, t] = jnp.dot(
                    parts[d][f, 0, q_rows:], mats[0, 1], preferred_element_type=jnp.float32
                ).astype(jnp.bfloat16)

    in_specs = [pl.BlockSpec((blocks, 1, rows, LANES), lambda j, at: (at[1], j, 0, 0))]
    in_specs += [pl.BlockSpec((blocks, 1, rows, LANES), lambda j, at: (0, j, 0, 0))] * len(came)
    in_specs += [pl.BlockSpec((1,) + matrices.shape[1:], lambda j, at: (items[0] + j, 0, 0, 0))]
    args = [own, *came, matrices]
    aliases = {}
    if outs is not None:
        in_specs += [pl.BlockSpec(memory_space=pl.ANY)] * 2
        aliases = {1 + len(args): 0, 2 + len(args): 1}
        args += list(outs)
    work = t_ways * blocks * len(items) * rows
    return pl.pallas_call(
        kernel,
        grid_spec=pltpu.PrefetchScalarGridSpec(
            num_scalar_prefetch=1,
            grid=(len(items),),
            in_specs=in_specs,
            out_specs=[
                pl.BlockSpec((1,) + shape.shape[1:], lambda j, at: (items[0] + j, 0, 0, 0, 0))
                for shape in shapes
            ],
        ),
        out_shape=shapes,
        input_output_aliases=aliases,
        compiler_params=pltpu.CompilerParams(vmem_limit_bytes=VMEM_LIMIT),
        cost_estimate=pl.CostEstimate(
            flops=2 * work * LANES * KVR,
            transcendentals=0,
            bytes_accessed=2 * work * (LANES + KVR),
        ),
        name="absorb",
    )(where, *args)


def absorb_plain(me, own, came, matrices):
    t_ways = len(came) + 1
    order = lax.rem(me - jnp.arange(t_ways, dtype=jnp.int32) + t_ways, jnp.int32(t_ways))
    rows = jnp.take(jnp.stack([own, *came]), order, axis=0).transpose(2, 1, 0, 3, 4)
    cut = rows.shape[3] * QR // (QR + D)
    return tuple(
        jnp.einsum("hrc,hck->hrk", part, mats, preferred_element_type=jnp.float32).astype(jnp.bfloat16)
        for part, mats in (
            (rows[:, :, :, :cut].reshape(rows.shape[0], -1, LANES), matrices[:, 0]),
            (rows[:, :, :, cut:].reshape(rows.shape[0], -1, LANES), matrices[:, 1]),
        )
    )


def per_device(learner_flat, param_offsets, owner_map, slice_map):
    f_ways, t_ways = lax.axis_size("fsdp"), lax.axis_size("tp")
    layer_count = learner_flat.shape[0]
    per_group = owner_map.shape[1] // f_ways
    item_count = layer_count * per_group
    widths = piece_widths(f_ways * t_ways)
    granule = functools.reduce(math.gcd, widths)
    table = learner_flat.reshape(layer_count, -1, granule // LANES, LANES)
    whole_tiles = granule % (16 * LANES) == 0
    row_counts = [width // LANES for width in widths]

    me = lax.axis_index("tp")
    blocks = f_ways // t_ways
    shifts = range(1, t_ways)
    per_chunk = max(1, item_count // 4)
    chunks = [range(at, min(at + per_chunk, item_count)) for at in range(0, item_count, per_chunk)]

    def over_fsdp(x, rows):
        x = lax.all_to_all(x, "fsdp", split_axis=0, concat_axis=0, tiled=True)
        return x.reshape(x.shape[:2] + rows)

    pairs, *to_send = pack(
        table,
        param_offsets,
        owner_map,
        f_ways,
        widths,
        granule,
        [(range(item_count), (KEY, VALUE))] + [(items, (QUERY, OUT)) for items in chunks],
    )
    pairs = over_fsdp(pairs, (2, row_counts[KEY], LANES))
    up, down = [pairs], [pairs]
    for _ in shifts:
        above, below = line_step(up[-1], down[-1], "tp", t_ways)
        up.append(above)
        down.append(below)

    exchanged = []
    for at in range(len(chunks)):
        rows = over_fsdp(to_send[at], (row_counts[QUERY] + row_counts[OUT], LANES))
        waits = exchanged[at - 2][1] if at >= 2 else [up[2:3] + down[2:3], up[3:] + down[3:]][at]
        pieces = cut(rows, slice_map, blocks, shifts, waits, CUT_MICROS)
        came = [
            lax.ppermute(piece, "tp", [(i, (i + shift) % t_ways) for i in range(t_ways)])
            for shift, piece in zip(shifts, pieces)
        ]
        exchanged.append((rows, came))
    slice_row = lax.dynamic_index_in_dim(slice_map, lax.axis_index("fsdp"), 0, keepdims=False)
    near = [jnp.where(me >= d, up[d], down[t_ways - d]) for d in shifts]

    if whole_tiles:
        shapes = tuple(
            jax.ShapeDtypeStruct((item_count, blocks, t_ways, row_counts[kind], KVR), jnp.bfloat16)
            for kind in (QUERY, OUT)
        )
        where = jnp.stack([me, slice_row[me]])
        matrices = assemble(me, [pairs] + near)
        outs = None
        for items, (rows, came) in zip(chunks, exchanged):
            outs = absorb(where, items, rows, came, matrices, outs, shapes)
        return tuple(out.reshape(layer_count, per_group, -1, KVR) for out in outs)

    order = lax.rem(me - jnp.arange(t_ways, dtype=jnp.int32) + t_ways, jnp.int32(t_ways))
    matrices = jnp.take(jnp.stack([pairs] + near), order, axis=0).transpose(2, 3, 1, 0, 4, 5)
    matrices = matrices.reshape(item_count, 2, -1, KVR)
    done = [
        absorb_plain(
            me,
            lax.dynamic_slice_in_dim(rows, slice_row[me] * blocks, blocks, 0),
            came,
            matrices[items[0] : items[-1] + 1],
        )
        for items, (rows, came) in zip(chunks, exchanged)
    ]
    return tuple(jnp.concatenate(kind).reshape(layer_count, per_group, -1, KVR) for kind in zip(*done))


def solution(mesh):
    placed = (P(None, ("fsdp", "tp")), P(), P(), P())
    return jax.shard_map(
        per_device,
        mesh=mesh,
        in_specs=placed,
        out_specs=(P(None, "fsdp", "tp", None), P(None, "fsdp", "tp", None)),
        check_vma=False,
    )
```

```python
import functools
import math

import jax
import jax.numpy as jnp
from jax import lax
from jax.experimental import pallas as pl
from jax.experimental.pallas import tpu as pltpu
from jax.sharding import PartitionSpec as P

D = 7168
QR = 1536
KVR = 512
QK_NOPE = 128
V_DIM = 128
LANES = 128
QUERY, KEY, VALUE, OUT = range(4)
CUT_MICROS = 10
TOKEN_MICROS = 20
CUTS = (0, 2, 4, 7, 8)
VMEM_LIMIT = 16 * 1024 * 1024


def piece_widths(rank_total):
    return (
        QR * QK_NOPE // rank_total,
        QK_NOPE * KVR // rank_total,
        V_DIM * KVR // rank_total,
        D * V_DIM // rank_total,
    )


def pack(table, param_offsets, owner_map, ways, widths, granule, chunks):
    layer_count, head_count = owner_map.shape
    per_group = head_count // ways
    steps = [[widths[kind] // granule for kind in kinds] for _, kinds in chunks]
    outs = [
        jax.ShapeDtypeStruct((ways, len(items), sum(step)) + table.shape[2:], table.dtype)
        for (items, _), step in zip(chunks, steps)
    ]

    def kernel(offsets, owners, source, *refs):
        targets, (taken, head_at) = refs[:-2], refs[-2:]
        for layer in range(layer_count):
            for way in range(ways):
                taken[way] = layer * per_group

            def place(head):
                way = owners[layer, head]
                item = taken[way]
                taken[way] = item + 1
                head_at[item * ways + way] = head

            pl.loop(0, head_count, unroll=min(8, head_count))(place)

        for target, (items, kinds), step in zip(targets, chunks, steps):
            for at, item in enumerate(items):

                def move(way):
                    head = head_at[item * ways + way]
                    start = 0
                    for kind, size in zip(kinds, step):
                        begin = lax.div(offsets[item // per_group, head, kind], jnp.int32(granule))
                        target[way, at, pl.ds(start, size)] = source[item // per_group, pl.ds(begin, size)]
                        start += size

                pl.loop(0, ways, unroll=min(8, ways))(move)

    return pl.pallas_call(
        kernel,
        out_shape=outs,
        in_specs=[
            pl.BlockSpec(memory_space=pltpu.SMEM),
            pl.BlockSpec(memory_space=pltpu.SMEM),
            pl.BlockSpec(memory_space=pltpu.VMEM),
        ],
        out_specs=[pl.BlockSpec(memory_space=pltpu.VMEM)] * len(outs),
        scratch_shapes=[
            pltpu.SMEM((ways,), jnp.int32),
            pltpu.SMEM((layer_count * head_count,), jnp.int32),
        ],
        compiler_params=pltpu.CompilerParams(vmem_limit_bytes=VMEM_LIMIT),
        cost_estimate=pl.CostEstimate(
            flops=0,
            transcendentals=0,
            bytes_accessed=sum(2 * 2 * math.prod(out.shape) for out in outs),
        ),
        name="pack",
    )(param_offsets, owner_map, table)


def corner(x):
    block = (1,) * (x.ndim - 2) + (min(16, x.shape[-2]), LANES)
    return pl.BlockSpec(block, lambda _: (0,) * x.ndim)


def cut(rows, slice_map, blocks, shifts, waits, micros):
    shape = (blocks,) + rows.shape[1:]
    t_ways = slice_map.shape[1]

    def kernel(mapped, source, *refs):
        f_me, t_me = lax.axis_index("fsdp"), lax.axis_index("tp")
        for shift, piece in zip(shifts, refs[len(waits) :]):
            block = mapped[f_me, lax.rem(t_me + shift, t_ways)]
            for f in range(blocks):
                piece[f] = source[block * blocks + f]

    return pl.pallas_call(
        kernel,
        grid=(1,),
        out_shape=[jax.ShapeDtypeStruct(shape, rows.dtype)] * len(shifts),
        in_specs=[pl.BlockSpec(memory_space=pltpu.SMEM), pl.BlockSpec(memory_space=pltpu.VMEM)]
        + [corner(x) for x in waits],
        out_specs=[pl.BlockSpec(memory_space=pltpu.VMEM)] * len(shifts),
        compiler_params=pltpu.CompilerParams(vmem_limit_bytes=VMEM_LIMIT),
        cost_estimate=pl.CostEstimate(
            flops=int(micros * 1.15e9),
            transcendentals=0,
            bytes_accessed=4 * len(shifts) * math.prod(shape),
        ),
        name="cut",
    )(slice_map, rows, *waits)


def token(waits, micros):
    def kernel(*refs):
        refs[-1][...] = jnp.zeros(refs[-1].shape, refs[-1].dtype)

    return pl.pallas_call(
        kernel,
        grid=(1,),
        out_shape=jax.ShapeDtypeStruct((16, LANES), jnp.bfloat16),
        in_specs=[corner(x) for x in waits],
        cost_estimate=pl.CostEstimate(
            flops=int(micros * 1.15e9), transcendentals=0, bytes_accessed=0
        ),
        name="token",
    )(*waits)


def line_step(up, down, axis, ways):
    return (
        lax.ppermute(up, axis, [(i, i + 1) for i in range(ways - 1)]),
        lax.ppermute(down, axis, [(i + 1, i) for i in range(ways - 1)]),
    )


def assemble(me, spread_parts):
    t_ways = len(spread_parts)
    f_ways, items, kinds, rows, _ = spread_parts[0].shape
    depth = t_ways * f_ways * rows * LANES // KVR
    cuts = KVR // LANES

    def kernel(me_ref, *refs):
        pieces, (out, scratch) = refs[:t_ways], refs[t_ways:]
        for kind in range(kinds):
            for d in range(t_ways):
                t = lax.rem(me_ref[0] - d + t_ways, t_ways)
                for f in range(f_ways):
                    scratch[pl.ds(pl.multiple_of((f * t_ways + t) * rows, rows), rows), :] = pieces[
                        d
                    ][f, 0, kind].astype(jnp.float32)
            for cut in range(cuts):
                out[0, kind, :, pl.ds(cut * LANES, LANES)] = scratch[
                    pl.ds(cut, depth, stride=cuts), :
                ].astype(jnp.bfloat16)

    return pl.pallas_call(
        kernel,
        grid_spec=pltpu.PrefetchScalarGridSpec(
            num_scalar_prefetch=1,
            grid=(items,),
            in_specs=[pl.BlockSpec((f_ways, 1, kinds, rows, LANES), lambda i, _: (0, i, 0, 0, 0))] * t_ways,
            out_specs=pl.BlockSpec((1, kinds, depth, KVR), lambda i, _: (i, 0, 0, 0)),
            scratch_shapes=[pltpu.VMEM((depth * cuts, LANES), jnp.float32)],
        ),
        out_shape=jax.ShapeDtypeStruct((items, kinds, depth, KVR), spread_parts[0].dtype),
        compiler_params=pltpu.CompilerParams(vmem_limit_bytes=VMEM_LIMIT),
        name="assemble",
    )(me.reshape(1), *spread_parts)


def absorb(where, items, own, came, matrices, outs, shapes):
    t_ways = len(came) + 1
    blocks = came[0].shape[0]
    q_rows, o_rows = shapes[0].shape[3], shapes[1].shape[3]
    rows = q_rows + o_rows

    def kernel(at, *refs):
        parts, mats = refs[:t_ways], refs[t_ways]
        q_out, o_out = refs[-2:]
        for d in range(t_ways):
            t = lax.rem(at[0] - d + t_ways, t_ways)
            for f in range(blocks):
                q_out[0, f, t] = jnp.dot(
                    parts[d][f, 0, :q_rows], mats[0, 0], preferred_element_type=jnp.float32
                ).astype(jnp.bfloat16)
                o_out[0, f, t] = jnp.dot(
                    parts[d][f, 0, q_rows:], mats[0, 1], preferred_element_type=jnp.float32
                ).astype(jnp.bfloat16)

    in_specs = [pl.BlockSpec((blocks, 1, rows, LANES), lambda j, at: (at[1], j, 0, 0))]
    in_specs += [pl.BlockSpec((blocks, 1, rows, LANES), lambda j, at: (0, j, 0, 0))] * len(came)
    in_specs += [pl.BlockSpec((1,) + matrices.shape[1:], lambda j, at: (items[0] + j, 0, 0, 0))]
    args = [own, *came, matrices]
    aliases = {}
    if outs is not None:
        in_specs += [pl.BlockSpec(memory_space=pl.ANY)] * 2
        aliases = {1 + len(args): 0, 2 + len(args): 1}
        args += list(outs)
    work = t_ways * blocks * len(items) * rows
    return pl.pallas_call(
        kernel,
        grid_spec=pltpu.PrefetchScalarGridSpec(
            num_scalar_prefetch=1,
            grid=(len(items),),
            in_specs=in_specs,
            out_specs=[
                pl.BlockSpec((1,) + shape.shape[1:], lambda j, at: (items[0] + j, 0, 0, 0, 0))
                for shape in shapes
            ],
        ),
        out_shape=shapes,
        input_output_aliases=aliases,
        compiler_params=pltpu.CompilerParams(vmem_limit_bytes=VMEM_LIMIT),
        cost_estimate=pl.CostEstimate(
            flops=2 * work * LANES * KVR,
            transcendentals=0,
            bytes_accessed=2 * work * (LANES + KVR),
        ),
        name="absorb",
    )(where, *args)


def absorb_plain(me, own, came, matrices):
    t_ways = len(came) + 1
    order = lax.rem(me - jnp.arange(t_ways, dtype=jnp.int32) + t_ways, jnp.int32(t_ways))
    rows = jnp.take(jnp.stack([own, *came]), order, axis=0).transpose(2, 1, 0, 3, 4)
    cut = rows.shape[3] * QR // (QR + D)
    return tuple(
        jnp.einsum("hrc,hck->hrk", part, mats, preferred_element_type=jnp.float32).astype(jnp.bfloat16)
        for part, mats in (
            (rows[:, :, :, :cut].reshape(rows.shape[0], -1, LANES), matrices[:, 0]),
            (rows[:, :, :, cut:].reshape(rows.shape[0], -1, LANES), matrices[:, 1]),
        )
    )


def per_device(learner_flat, param_offsets, owner_map, slice_map):
    f_ways, t_ways = lax.axis_size("fsdp"), lax.axis_size("tp")
    layer_count = learner_flat.shape[0]
    per_group = owner_map.shape[1] // f_ways
    item_count = layer_count * per_group
    widths = piece_widths(f_ways * t_ways)
    granule = functools.reduce(math.gcd, widths)
    table = learner_flat.reshape(layer_count, -1, granule // LANES, LANES)
    whole_tiles = granule % (16 * LANES) == 0
    row_counts = [width // LANES for width in widths]

    me = lax.axis_index("tp")
    blocks = f_ways // t_ways
    shifts = range(1, t_ways)
    cuts = [item_count * eighths // 8 for eighths in CUTS]
    chunks = [range(low, high) for low, high in zip(cuts, cuts[1:]) if low < high]

    def over_fsdp(x, rows):
        x = lax.all_to_all(x, "fsdp", split_axis=0, concat_axis=0, tiled=True)
        return x.reshape(x.shape[:2] + rows)

    pairs, *to_send = pack(
        table,
        param_offsets,
        owner_map,
        f_ways,
        widths,
        granule,
        [(range(item_count), (KEY, VALUE))] + [(items, (QUERY, OUT)) for items in chunks],
    )
    pairs = over_fsdp(pairs, (2, row_counts[KEY], LANES))
    up, down = [pairs], [pairs]
    for _ in shifts:
        above, below = line_step(up[-1], down[-1], "tp", t_ways)
        up.append(above)
        down.append(below)

    exchanged, sent = [], []
    near_pairs = token(up[2:3] + down[2:3], TOKEN_MICROS)
    for at in range(len(chunks)):
        rows = over_fsdp(to_send[at], (row_counts[QUERY] + row_counts[OUT], LANES))
        waits = sent[at - 1][:1] if at else []
        if at == 1:
            waits = waits + up[3:] + down[3:] + [near_pairs]
        elif at:
            waits = waits + exchanged[at - 2][1]
        pieces = cut(rows, slice_map, blocks, shifts, waits, CUT_MICROS)
        came = [
            lax.ppermute(piece, "tp", [(i, (i + shift) % t_ways) for i in range(t_ways)])
            for shift, piece in zip(shifts, pieces)
        ]
        exchanged.append((rows, came))
        sent.append(list(pieces))
    slice_row = lax.dynamic_index_in_dim(slice_map, lax.axis_index("fsdp"), 0, keepdims=False)
    near = [jnp.where(me >= d, up[d], down[t_ways - d]) for d in shifts]

    if whole_tiles:
        shapes = tuple(
            jax.ShapeDtypeStruct((item_count, blocks, t_ways, row_counts[kind], KVR), jnp.bfloat16)
            for kind in (QUERY, OUT)
        )
        where = jnp.stack([me, slice_row[me]])
        matrices = assemble(me, [pairs] + near)
        outs = None
        for items, (rows, came) in zip(chunks, exchanged):
            outs = absorb(where, items, rows, came, matrices, outs, shapes)
        return tuple(out.reshape(layer_count, per_group, -1, KVR) for out in outs)

    order = lax.rem(me - jnp.arange(t_ways, dtype=jnp.int32) + t_ways, jnp.int32(t_ways))
    matrices = jnp.take(jnp.stack([pairs] + near), order, axis=0).transpose(2, 3, 1, 0, 4, 5)
    matrices = matrices.reshape(item_count, 2, -1, KVR)
    done = [
        absorb_plain(
            me,
            lax.dynamic_slice_in_dim(rows, slice_row[me] * blocks, blocks, 0),
            came,
            matrices[items[0] : items[-1] + 1],
        )
        for items, (rows, came) in zip(chunks, exchanged)
    ]
    return tuple(jnp.concatenate(kind).reshape(layer_count, per_group, -1, KVR) for kind in zip(*done))


def solution(mesh):
    placed = (P(None, ("fsdp", "tp")), P(), P(), P())
    return jax.shard_map(
        per_device,
        mesh=mesh,
        in_specs=placed,
        out_specs=(P(None, "fsdp", "tp", None), P(None, "fsdp", "tp", None)),
        check_vma=False,
    )
```

```python
import functools
import math

import jax
import jax.numpy as jnp
from jax import lax
from jax.experimental import pallas as pl
from jax.experimental.pallas import tpu as pltpu
from jax.sharding import PartitionSpec as P

D = 7168
QR = 1536
KVR = 512
QK_NOPE = 128
V_DIM = 128
LANES = 128
QUERY, KEY, VALUE, OUT = range(4)
CUT_MICROS = 10
TOKEN_MICROS = 20
CUTS = (0, 2, 4, 6, 8)
VMEM_LIMIT = 16 * 1024 * 1024


def piece_widths(rank_total):
    return (
        QR * QK_NOPE // rank_total,
        QK_NOPE * KVR // rank_total,
        V_DIM * KVR // rank_total,
        D * V_DIM // rank_total,
    )


def pack(table, param_offsets, owner_map, ways, widths, granule, chunks):
    layer_count, head_count = owner_map.shape
    per_group = head_count // ways
    steps = [[widths[kind] // granule for kind in kinds] for _, kinds in chunks]
    outs = [
        jax.ShapeDtypeStruct((ways, len(items), sum(step)) + table.shape[2:], table.dtype)
        for (items, _), step in zip(chunks, steps)
    ]

    def kernel(offsets, owners, source, *refs):
        targets, (taken, head_at) = refs[:-2], refs[-2:]
        for layer in range(layer_count):
            for way in range(ways):
                taken[way] = layer * per_group

            def place(head):
                way = owners[layer, head]
                item = taken[way]
                taken[way] = item + 1
                head_at[item * ways + way] = head

            pl.loop(0, head_count, unroll=min(8, head_count))(place)

        for target, (items, kinds), step in zip(targets, chunks, steps):
            for at, item in enumerate(items):

                def move(way):
                    head = head_at[item * ways + way]
                    start = 0
                    for kind, size in zip(kinds, step):
                        begin = lax.div(offsets[item // per_group, head, kind], jnp.int32(granule))
                        target[way, at, pl.ds(start, size)] = source[item // per_group, pl.ds(begin, size)]
                        start += size

                pl.loop(0, ways, unroll=min(8, ways))(move)

    return pl.pallas_call(
        kernel,
        out_shape=outs,
        in_specs=[
            pl.BlockSpec(memory_space=pltpu.SMEM),
            pl.BlockSpec(memory_space=pltpu.SMEM),
            pl.BlockSpec(memory_space=pltpu.VMEM),
        ],
        out_specs=[pl.BlockSpec(memory_space=pltpu.VMEM)] * len(outs),
        scratch_shapes=[
            pltpu.SMEM((ways,), jnp.int32),
            pltpu.SMEM((layer_count * head_count,), jnp.int32),
        ],
        compiler_params=pltpu.CompilerParams(vmem_limit_bytes=VMEM_LIMIT),
        cost_estimate=pl.CostEstimate(
            flops=0,
            transcendentals=0,
            bytes_accessed=sum(2 * 2 * math.prod(out.shape) for out in outs),
        ),
        name="pack",
    )(param_offsets, owner_map, table)


def corner_of(x):
    return (1,) * (x.ndim - 2) + (min(16, x.shape[-2]), LANES)


def corner(x):
    return pl.BlockSpec(corner_of(x), lambda _: (0,) * x.ndim)


def cut(rows, slice_map, blocks, shifts, waits, micros):
    shape = (blocks,) + rows.shape[1:]
    t_ways = slice_map.shape[1]

    def kernel(mapped, source, *refs):
        f_me, t_me = lax.axis_index("fsdp"), lax.axis_index("tp")
        for shift, piece in zip(shifts, refs[len(waits) :]):
            block = mapped[f_me, lax.rem(t_me + shift, t_ways)]
            for f in range(blocks):
                piece[f] = source[block * blocks + f]

    return pl.pallas_call(
        kernel,
        grid=(1,),
        out_shape=[jax.ShapeDtypeStruct(shape, rows.dtype)] * len(shifts),
        in_specs=[pl.BlockSpec(memory_space=pltpu.SMEM), pl.BlockSpec(memory_space=pltpu.VMEM)]
        + [corner(x) for x in waits],
        out_specs=[pl.BlockSpec(memory_space=pltpu.VMEM)] * len(shifts),
        compiler_params=pltpu.CompilerParams(vmem_limit_bytes=VMEM_LIMIT),
        cost_estimate=pl.CostEstimate(
            flops=int(micros * 1.15e9),
            transcendentals=0,
            bytes_accessed=4 * len(shifts) * math.prod(shape),
        ),
        name="cut",
    )(slice_map, rows, *waits)


def token(waits, micros):
    def kernel(*refs):
        refs[-1][...] = jnp.zeros(refs[-1].shape, refs[-1].dtype)

    return pl.pallas_call(
        kernel,
        grid=(1,),
        out_shape=jax.ShapeDtypeStruct((16, LANES), jnp.bfloat16),
        in_specs=[corner(x) for x in waits],
        cost_estimate=pl.CostEstimate(
            flops=int(micros * 1.15e9), transcendentals=0, bytes_accessed=0
        ),
        name="token",
    )(*waits)


def neighbours(x, axis, ways):
    return (
        lax.ppermute(x, axis, [(i, i + 1) for i in range(ways - 1)]),
        lax.ppermute(x, axis, [(i + 1, i) for i in range(ways - 1)]),
    )


def pass_on(me, across, up, down, waits):
    def kernel(me_ref, first, above, below, *refs):
        out = refs[-1]
        out[0] = first[...]

        @pl.when(me_ref[0] == 2)
        def _():
            out[1] = above[...]

        @pl.when(me_ref[0] != 2)
        def _():
            out[1] = below[...]

    whole = pl.BlockSpec(across.shape, lambda _, me_ref: (0,) * across.ndim)
    corners = [pl.BlockSpec(corner_of(x), lambda _, me_ref, n=x.ndim: (0,) * n) for x in waits]
    return pl.pallas_call(
        kernel,
        grid_spec=pltpu.PrefetchScalarGridSpec(
            num_scalar_prefetch=1,
            grid=(1,),
            in_specs=[whole] * 3 + corners,
            out_specs=pl.BlockSpec((2,) + across.shape, lambda _, me_ref: (0,) * (across.ndim + 1)),
        ),
        out_shape=jax.ShapeDtypeStruct((2,) + across.shape, across.dtype),
        compiler_params=pltpu.CompilerParams(vmem_limit_bytes=VMEM_LIMIT),
        name="pass_on",
    )(me.reshape(1), across, up, down, *waits)


def assemble(me, spread_parts):
    t_ways = len(spread_parts)
    f_ways, items, kinds, rows, _ = spread_parts[0].shape
    depth = t_ways * f_ways * rows * LANES // KVR
    cuts = KVR // LANES

    def kernel(me_ref, *refs):
        pieces, (out, scratch) = refs[:t_ways], refs[t_ways:]
        for kind in range(kinds):
            for d in range(t_ways):
                t = lax.rem(me_ref[0] - d + t_ways, t_ways)
                for f in range(f_ways):
                    scratch[pl.ds(pl.multiple_of((f * t_ways + t) * rows, rows), rows), :] = pieces[
                        d
                    ][f, 0, kind].astype(jnp.float32)
            for cut in range(cuts):
                out[0, kind, :, pl.ds(cut * LANES, LANES)] = scratch[
                    pl.ds(cut, depth, stride=cuts), :
                ].astype(jnp.bfloat16)

    return pl.pallas_call(
        kernel,
        grid_spec=pltpu.PrefetchScalarGridSpec(
            num_scalar_prefetch=1,
            grid=(items,),
            in_specs=[pl.BlockSpec((f_ways, 1, kinds, rows, LANES), lambda i, _: (0, i, 0, 0, 0))] * t_ways,
            out_specs=pl.BlockSpec((1, kinds, depth, KVR), lambda i, _: (i, 0, 0, 0)),
            scratch_shapes=[pltpu.VMEM((depth * cuts, LANES), jnp.float32)],
        ),
        out_shape=jax.ShapeDtypeStruct((items, kinds, depth, KVR), spread_parts[0].dtype),
        compiler_params=pltpu.CompilerParams(vmem_limit_bytes=VMEM_LIMIT),
        name="assemble",
    )(me.reshape(1), *spread_parts)


def absorb(where, items, own, came, matrices, outs, shapes):
    t_ways = len(came) + 1
    blocks = came[0].shape[0]
    q_rows, o_rows = shapes[0].shape[3], shapes[1].shape[3]
    rows = q_rows + o_rows

    def kernel(at, *refs):
        parts, mats = refs[:t_ways], refs[t_ways]
        q_out, o_out = refs[-2:]
        for d in range(t_ways):
            t = lax.rem(at[0] - d + t_ways, t_ways)
            for f in range(blocks):
                q_out[0, f, t] = jnp.dot(
                    parts[d][f, 0, :q_rows], mats[0, 0], preferred_element_type=jnp.float32
                ).astype(jnp.bfloat16)
                o_out[0, f, t] = jnp.dot(
                    parts[d][f, 0, q_rows:], mats[0, 1], preferred_element_type=jnp.float32
                ).astype(jnp.bfloat16)

    in_specs = [pl.BlockSpec((blocks, 1, rows, LANES), lambda j, at: (at[1], j, 0, 0))]
    in_specs += [pl.BlockSpec((blocks, 1, rows, LANES), lambda j, at: (0, j, 0, 0))] * len(came)
    in_specs += [pl.BlockSpec((1,) + matrices.shape[1:], lambda j, at: (items[0] + j, 0, 0, 0))]
    args = [own, *came, matrices]
    aliases = {}
    if outs is not None:
        in_specs += [pl.BlockSpec(memory_space=pl.ANY)] * 2
        aliases = {1 + len(args): 0, 2 + len(args): 1}
        args += list(outs)
    work = t_ways * blocks * len(items) * rows
    return pl.pallas_call(
        kernel,
        grid_spec=pltpu.PrefetchScalarGridSpec(
            num_scalar_prefetch=1,
            grid=(len(items),),
            in_specs=in_specs,
            out_specs=[
                pl.BlockSpec((1,) + shape.shape[1:], lambda j, at: (items[0] + j, 0, 0, 0, 0))
                for shape in shapes
            ],
        ),
        out_shape=shapes,
        input_output_aliases=aliases,
        compiler_params=pltpu.CompilerParams(vmem_limit_bytes=VMEM_LIMIT),
        cost_estimate=pl.CostEstimate(
            flops=2 * work * LANES * KVR,
            transcendentals=0,
            bytes_accessed=2 * work * (LANES + KVR),
        ),
        name="absorb",
    )(where, *args)


def absorb_plain(me, own, came, matrices):
    t_ways = len(came) + 1
    order = lax.rem(me - jnp.arange(t_ways, dtype=jnp.int32) + t_ways, jnp.int32(t_ways))
    rows = jnp.take(jnp.stack([own, *came]), order, axis=0).transpose(2, 1, 0, 3, 4)
    cut = rows.shape[3] * QR // (QR + D)
    return tuple(
        jnp.einsum("hrc,hck->hrk", part, mats, preferred_element_type=jnp.float32).astype(jnp.bfloat16)
        for part, mats in (
            (rows[:, :, :, :cut].reshape(rows.shape[0], -1, LANES), matrices[:, 0]),
            (rows[:, :, :, cut:].reshape(rows.shape[0], -1, LANES), matrices[:, 1]),
        )
    )


def per_device(learner_flat, param_offsets, owner_map, slice_map):
    f_ways, t_ways = lax.axis_size("fsdp"), lax.axis_size("tp")
    layer_count = learner_flat.shape[0]
    per_group = owner_map.shape[1] // f_ways
    item_count = layer_count * per_group
    widths = piece_widths(f_ways * t_ways)
    granule = functools.reduce(math.gcd, widths)
    table = learner_flat.reshape(layer_count, -1, granule // LANES, LANES)
    whole_tiles = granule % (16 * LANES) == 0
    row_counts = [width // LANES for width in widths]

    me = lax.axis_index("tp")
    blocks = f_ways // t_ways
    shifts = range(1, t_ways)
    cuts = [item_count * eighths // 8 for eighths in CUTS]
    chunks = [range(low, high) for low, high in zip(cuts, cuts[1:]) if low < high]

    def over_fsdp(x, rows):
        x = lax.all_to_all(x, "fsdp", split_axis=0, concat_axis=0, tiled=True)
        return x.reshape(x.shape[:2] + rows)

    pairs, *to_send = pack(
        table,
        param_offsets,
        owner_map,
        f_ways,
        widths,
        granule,
        [(range(item_count), (KEY, VALUE))] + [(items, (QUERY, OUT)) for items in chunks],
    )
    pairs = over_fsdp(pairs, (2, row_counts[KEY], LANES))
    up, down = neighbours(pairs, "tp", t_ways)
    if t_ways == 4:
        across = lax.ppermute(pairs, "tp", [(0, 2), (3, 1)])
        near = token([up, down, across], TOKEN_MICROS)
    else:
        ups, downs = [pairs, up], [pairs, down]
        for _ in range(2, t_ways):
            ups.append(neighbours(ups[-1], "tp", t_ways)[0])
            downs.append(neighbours(downs[-1], "tp", t_ways)[1])

    exchanged, sent = [], []
    for at in range(len(chunks)):
        rows = over_fsdp(to_send[at], (row_counts[QUERY] + row_counts[OUT], LANES))
        waits = sent[at - 1][:1] if at else []
        if at >= 2:
            waits = waits + exchanged[at - 2][1]
        if t_ways == 4 and at == 1:
            waits = waits + [near]
        if t_ways == 4 and at == len(chunks) - 1:
            waits = waits + [far]
        pieces = cut(rows, slice_map, blocks, shifts, waits, CUT_MICROS)
        came = [
            lax.ppermute(piece, "tp", [(i, (i + shift) % t_ways) for i in range(t_ways)])
            for shift, piece in zip(shifts, pieces)
        ]
        exchanged.append((rows, came))
        sent.append(list(pieces))
        if t_ways == 4 and at == 1:
            far = lax.ppermute(
                pass_on(me, across, up, down, sent[1][:1]), "tp", [(1, 0), (2, 3)]
            )
    if t_ways == 4:
        ends = jnp.logical_or(me == 0, me == 3)
        spread = [
            pairs,
            jnp.where(me == 0, far[0], up),
            jnp.where(ends, far[1], across),
            jnp.where(me == 3, far[0], down),
        ]
    else:
        spread = [pairs] + [jnp.where(me >= d, ups[d], downs[t_ways - d]) for d in shifts]
    slice_row = lax.dynamic_index_in_dim(slice_map, lax.axis_index("fsdp"), 0, keepdims=False)
    near = [jnp.where(me >= d, up[d], down[t_ways - d]) for d in shifts]

    if whole_tiles:
        shapes = tuple(
            jax.ShapeDtypeStruct((item_count, blocks, t_ways, row_counts[kind], KVR), jnp.bfloat16)
            for kind in (QUERY, OUT)
        )
        where = jnp.stack([me, slice_row[me]])
        matrices = assemble(me, spread)
        outs = None
        for items, (rows, came) in zip(chunks, exchanged):
            outs = absorb(where, items, rows, came, matrices, outs, shapes)
        return tuple(out.reshape(layer_count, per_group, -1, KVR) for out in outs)

    order = lax.rem(me - jnp.arange(t_ways, dtype=jnp.int32) + t_ways, jnp.int32(t_ways))
    matrices = jnp.take(jnp.stack(spread), order, axis=0).transpose(2, 3, 1, 0, 4, 5)
    matrices = matrices.reshape(item_count, 2, -1, KVR)
    done = [
        absorb_plain(
            me,
            lax.dynamic_slice_in_dim(rows, slice_row[me] * blocks, blocks, 0),
            came,
            matrices[items[0] : items[-1] + 1],
        )
        for items, (rows, came) in zip(chunks, exchanged)
    ]
    return tuple(jnp.concatenate(kind).reshape(layer_count, per_group, -1, KVR) for kind in zip(*done))


def solution(mesh):
    placed = (P(None, ("fsdp", "tp")), P(), P(), P())
    return jax.shard_map(
        per_device,
        mesh=mesh,
        in_specs=placed,
        out_specs=(P(None, "fsdp", "tp", None), P(None, "fsdp", "tp", None)),
        check_vma=False,
    )
```

```python
import functools
import math

import jax
import jax.numpy as jnp
from jax import lax
from jax.experimental import pallas as pl
from jax.experimental.pallas import tpu as pltpu
from jax.sharding import PartitionSpec as P

D = 7168
QR = 1536
KVR = 512
QK_NOPE = 128
V_DIM = 128
LANES = 128
QUERY, KEY, VALUE, OUT = range(4)
CUT_MICROS = 10
TOKEN_MICROS = 20
CUTS = (0, 1, 4, 6, 8)
VMEM_LIMIT = 16 * 1024 * 1024


def piece_widths(rank_total):
    return (
        QR * QK_NOPE // rank_total,
        QK_NOPE * KVR // rank_total,
        V_DIM * KVR // rank_total,
        D * V_DIM // rank_total,
    )


def pack(table, param_offsets, owner_map, ways, widths, granule, parts):
    layer_count, head_count = owner_map.shape
    per_group = head_count // ways
    sizes = [width // granule for width in widths]
    outs = [
        jax.ShapeDtypeStruct(
            (ways, sum(len(items) * sum(sizes[kind] for kind in kinds) for items, kinds in part))
            + table.shape[2:],
            table.dtype,
        )
        for part in parts
    ]

    def kernel(offsets, owners, source, *refs):
        targets, (taken, head_at) = refs[:-2], refs[-2:]
        for layer in sorted({item // per_group for part in parts for items, _ in part for item in items}):
            for way in range(ways):
                taken[way] = layer * per_group

            def place(head):
                way = owners[layer, head]
                item = taken[way]
                taken[way] = item + 1
                head_at[item * ways + way] = head

            pl.loop(0, head_count, unroll=min(8, head_count))(place)

        for target, part in zip(targets, parts):
            start = 0
            for item, kinds in [(item, kinds) for items, kinds in part for item in items]:

                def move(way):
                    head = head_at[item * ways + way]
                    at = start
                    for kind in kinds:
                        begin = lax.div(offsets[item // per_group, head, kind], jnp.int32(granule))
                        target[way, pl.ds(at, sizes[kind])] = source[
                            item // per_group, pl.ds(begin, sizes[kind])
                        ]
                        at += sizes[kind]

                pl.loop(0, ways, unroll=min(8, ways))(move)
                start += sum(sizes[kind] for kind in kinds)

    return pl.pallas_call(
        kernel,
        out_shape=outs,
        in_specs=[
            pl.BlockSpec(memory_space=pltpu.SMEM),
            pl.BlockSpec(memory_space=pltpu.SMEM),
            pl.BlockSpec(memory_space=pltpu.VMEM),
        ],
        out_specs=[pl.BlockSpec(memory_space=pltpu.VMEM)] * len(outs),
        scratch_shapes=[
            pltpu.SMEM((ways,), jnp.int32),
            pltpu.SMEM((layer_count * head_count,), jnp.int32),
        ],
        compiler_params=pltpu.CompilerParams(vmem_limit_bytes=VMEM_LIMIT),
        cost_estimate=pl.CostEstimate(
            flops=0,
            transcendentals=0,
            bytes_accessed=sum(2 * 2 * math.prod(out.shape) for out in outs),
        ),
        name="pack",
    )(param_offsets, owner_map, table)


def corner_of(x):
    return (1,) * (x.ndim - 2) + (min(16, x.shape[-2]), LANES)


def corner(x):
    return pl.BlockSpec(corner_of(x), lambda _: (0,) * x.ndim)


def cut(rows, slice_map, blocks, ahead, item_rows, waits, micros):
    t_ways = slice_map.shape[1]
    first = math.prod(ahead)
    items = (rows.shape[1] - first) // item_rows
    shapes = [(rows.shape[0],) + ahead + rows.shape[2:]] if first else []
    shapes += [(blocks, items, item_rows) + rows.shape[2:]] * t_ways

    def kernel(mapped, source, *refs):
        f_me, t_me = lax.axis_index("fsdp"), lax.axis_index("tp")
        refs = refs[len(waits) :]
        if first:
            for f in range(rows.shape[0]):
                for item in range(ahead[0]):
                    for kind in range(ahead[1]):
                        start = (item * ahead[1] + kind) * ahead[2]
                        refs[0][f, item, kind] = source[f, start : start + ahead[2]]
            refs = refs[1:]
        for shift, piece in enumerate(refs):
            block = mapped[f_me, lax.rem(t_me + shift, t_ways)]
            for f in range(blocks):
                for item in range(items):
                    start = first + item * item_rows
                    piece[f, item] = source[block * blocks + f, start : start + item_rows]

    return pl.pallas_call(
        kernel,
        grid=(1,),
        out_shape=[jax.ShapeDtypeStruct(shape, rows.dtype) for shape in shapes],
        in_specs=[pl.BlockSpec(memory_space=pltpu.SMEM), pl.BlockSpec(memory_space=pltpu.VMEM)]
        + [corner(x) for x in waits],
        out_specs=[pl.BlockSpec(memory_space=pltpu.VMEM)] * len(shapes),
        compiler_params=pltpu.CompilerParams(vmem_limit_bytes=VMEM_LIMIT),
        cost_estimate=pl.CostEstimate(
            flops=int(micros * 1.15e9),
            transcendentals=0,
            bytes_accessed=4 * sum(math.prod(shape) for shape in shapes),
        ),
        name="cut",
    )(slice_map, rows, *waits)


def token(waits, micros):
    def kernel(*refs):
        refs[-1][...] = jnp.zeros(refs[-1].shape, refs[-1].dtype)

    return pl.pallas_call(
        kernel,
        grid=(1,),
        out_shape=jax.ShapeDtypeStruct((16, LANES), jnp.bfloat16),
        in_specs=[corner(x) for x in waits],
        cost_estimate=pl.CostEstimate(
            flops=int(micros * 1.15e9), transcendentals=0, bytes_accessed=0
        ),
        name="token",
    )(*waits)


def neighbours(x, axis, ways):
    return (
        lax.ppermute(x, axis, [(i, i + 1) for i in range(ways - 1)]),
        lax.ppermute(x, axis, [(i + 1, i) for i in range(ways - 1)]),
    )


def pass_on(me, across, up, down, waits):
    def kernel(me_ref, first, above, below, *refs):
        out = refs[-1]
        out[0] = first[...]

        @pl.when(me_ref[0] == 2)
        def _():
            out[1] = above[...]

        @pl.when(me_ref[0] != 2)
        def _():
            out[1] = below[...]

    whole = pl.BlockSpec(across.shape, lambda _, me_ref: (0,) * across.ndim)
    corners = [pl.BlockSpec(corner_of(x), lambda _, me_ref, n=x.ndim: (0,) * n) for x in waits]
    return pl.pallas_call(
        kernel,
        grid_spec=pltpu.PrefetchScalarGridSpec(
            num_scalar_prefetch=1,
            grid=(1,),
            in_specs=[whole] * 3 + corners,
            out_specs=pl.BlockSpec((2,) + across.shape, lambda _, me_ref: (0,) * (across.ndim + 1)),
        ),
        out_shape=jax.ShapeDtypeStruct((2,) + across.shape, across.dtype),
        compiler_params=pltpu.CompilerParams(vmem_limit_bytes=VMEM_LIMIT),
        name="pass_on",
    )(me.reshape(1), across, up, down, *waits)


def assemble(me, spread_parts):
    t_ways = len(spread_parts)
    f_ways, items, kinds, rows, _ = spread_parts[0].shape
    depth = t_ways * f_ways * rows * LANES // KVR
    cuts = KVR // LANES

    def kernel(me_ref, *refs):
        pieces, (out, scratch) = refs[:t_ways], refs[t_ways:]
        for kind in range(kinds):
            for d in range(t_ways):
                t = lax.rem(me_ref[0] - d + t_ways, t_ways)
                for f in range(f_ways):
                    scratch[pl.ds(pl.multiple_of((f * t_ways + t) * rows, rows), rows), :] = pieces[
                        d
                    ][f, 0, kind].astype(jnp.float32)
            for cut in range(cuts):
                out[0, kind, :, pl.ds(cut * LANES, LANES)] = scratch[
                    pl.ds(cut, depth, stride=cuts), :
                ].astype(jnp.bfloat16)

    return pl.pallas_call(
        kernel,
        grid_spec=pltpu.PrefetchScalarGridSpec(
            num_scalar_prefetch=1,
            grid=(items,),
            in_specs=[pl.BlockSpec((f_ways, 1, kinds, rows, LANES), lambda i, _: (0, i, 0, 0, 0))] * t_ways,
            out_specs=pl.BlockSpec((1, kinds, depth, KVR), lambda i, _: (i, 0, 0, 0)),
            scratch_shapes=[pltpu.VMEM((depth * cuts, LANES), jnp.float32)],
        ),
        out_shape=jax.ShapeDtypeStruct((items, kinds, depth, KVR), spread_parts[0].dtype),
        compiler_params=pltpu.CompilerParams(vmem_limit_bytes=VMEM_LIMIT),
        name="assemble",
    )(me.reshape(1), *spread_parts)


def absorb(me, items, parts, matrices, outs, shapes):
    t_ways = len(parts)
    blocks = parts[0].shape[0]
    q_rows, o_rows = shapes[0].shape[3], shapes[1].shape[3]
    rows = q_rows + o_rows

    def kernel(at, *refs):
        parts, mats = refs[:t_ways], refs[t_ways]
        q_out, o_out = refs[-2:]
        for d in range(t_ways):
            t = lax.rem(at[0] - d + t_ways, t_ways)
            for f in range(blocks):
                q_out[0, f, t] = jnp.dot(
                    parts[d][f, 0, :q_rows], mats[0, 0], preferred_element_type=jnp.float32
                ).astype(jnp.bfloat16)
                o_out[0, f, t] = jnp.dot(
                    parts[d][f, 0, q_rows:], mats[0, 1], preferred_element_type=jnp.float32
                ).astype(jnp.bfloat16)

    in_specs = [pl.BlockSpec((blocks, 1, rows, LANES), lambda j, at: (0, j, 0, 0))] * t_ways
    in_specs += [pl.BlockSpec((1,) + matrices.shape[1:], lambda j, at: (items[0] + j, 0, 0, 0))]
    args = [*parts, matrices]
    aliases = {}
    if outs is not None:
        in_specs += [pl.BlockSpec(memory_space=pl.ANY)] * 2
        aliases = {1 + len(args): 0, 2 + len(args): 1}
        args += list(outs)
    work = t_ways * blocks * len(items) * rows
    return pl.pallas_call(
        kernel,
        grid_spec=pltpu.PrefetchScalarGridSpec(
            num_scalar_prefetch=1,
            grid=(len(items),),
            in_specs=in_specs,
            out_specs=[
                pl.BlockSpec((1,) + shape.shape[1:], lambda j, at: (items[0] + j, 0, 0, 0, 0))
                for shape in shapes
            ],
        ),
        out_shape=shapes,
        input_output_aliases=aliases,
        compiler_params=pltpu.CompilerParams(vmem_limit_bytes=VMEM_LIMIT),
        cost_estimate=pl.CostEstimate(
            flops=2 * work * LANES * KVR,
            transcendentals=0,
            bytes_accessed=2 * work * (LANES + KVR),
        ),
        name="absorb",
    )(me.reshape(1), *args)


def absorb_plain(me, parts, matrices):
    t_ways = len(parts)
    order = lax.rem(me - jnp.arange(t_ways, dtype=jnp.int32) + t_ways, jnp.int32(t_ways))
    rows = jnp.take(jnp.stack(parts), order, axis=0).transpose(2, 1, 0, 3, 4)
    cut = rows.shape[3] * QR // (QR + D)
    return tuple(
        jnp.einsum("hrc,hck->hrk", part, mats, preferred_element_type=jnp.float32).astype(jnp.bfloat16)
        for part, mats in (
            (rows[:, :, :, :cut].reshape(rows.shape[0], -1, LANES), matrices[:, 0]),
            (rows[:, :, :, cut:].reshape(rows.shape[0], -1, LANES), matrices[:, 1]),
        )
    )


def per_device(learner_flat, param_offsets, owner_map, slice_map):
    f_ways, t_ways = lax.axis_size("fsdp"), lax.axis_size("tp")
    layer_count = learner_flat.shape[0]
    per_group = owner_map.shape[1] // f_ways
    item_count = layer_count * per_group
    widths = piece_widths(f_ways * t_ways)
    granule = functools.reduce(math.gcd, widths)
    table = learner_flat.reshape(layer_count, -1, granule // LANES, LANES)
    whole_tiles = granule % (16 * LANES) == 0
    row_counts = [width // LANES for width in widths]
    item_rows = row_counts[QUERY] + row_counts[OUT]
    ahead = (item_count, 2, row_counts[KEY])

    me = lax.axis_index("tp")
    blocks = f_ways // t_ways
    cuts = [item_count * eighths // 8 for eighths in CUTS]
    chunks = [range(low, high) for low, high in zip(cuts, cuts[1:]) if low < high]

    def packed(parts):
        return pack(table, param_offsets, owner_map, f_ways, widths, granule, parts)

    def over_fsdp(x):
        x = lax.all_to_all(x, "fsdp", split_axis=0, concat_axis=0, tiled=True)
        return x.reshape(f_ways, -1, LANES)

    first_parts = [[(range(item_count), (KEY, VALUE)), (chunks[0], (QUERY, OUT))]]
    other_parts = [[(items, (QUERY, OUT))] for items in chunks[1:]]
    to_send = packed(first_parts + other_parts)

    exchanged, sent = [], []
    for at in range(len(chunks)):
        rows = over_fsdp(to_send[at])
        waits = sent[at - 1][:1] if at else []
        if at >= 2:
            waits = waits + exchanged[at - 2][1:]
        if at == 1:
            waits = waits + exchanged[0][1:3]
        if t_ways == 4 and at in (1, 2):
            waits = waits + [near if at == 1 else far]
        pieces = list(cut(rows, slice_map, blocks, ahead if at == 0 else (0,), item_rows, waits, CUT_MICROS))
        if at == 0:
            pairs = pieces.pop(0)
            up, down = neighbours(pairs, "tp", t_ways)
            if t_ways == 4:
                across = lax.ppermute(pairs, "tp", [(0, 2), (3, 1)])
                near = token([up, down, across], TOKEN_MICROS)
                far = lax.ppermute(pass_on(me, across, up, down, []), "tp", [(1, 0), (2, 3)])
        sent.append(pieces)
        exchanged.append(
            pieces[:1]
            + [
                lax.ppermute(piece, "tp", [(i, (i + shift) % t_ways) for i in range(t_ways)])
                for shift, piece in enumerate(pieces)
                if shift
            ]
        )

    if t_ways == 4:
        ends = jnp.logical_or(me == 0, me == 3)
        spread = [
            pairs,
            jnp.where(me == 0, far[0], up),
            jnp.where(ends, far[1], across),
            jnp.where(me == 3, far[0], down),
        ]
    else:
        ups, downs = [pairs, up], [pairs, down]
        for _ in range(2, t_ways):
            ups.append(neighbours(ups[-1], "tp", t_ways)[0])
            downs.append(neighbours(downs[-1], "tp", t_ways)[1])
        spread = [pairs] + [jnp.where(me >= d, ups[d], downs[t_ways - d]) for d in range(1, t_ways)]

    if whole_tiles:
        shapes = tuple(
            jax.ShapeDtypeStruct((item_count, blocks, t_ways, row_counts[kind], KVR), jnp.bfloat16)
            for kind in (QUERY, OUT)
        )
        matrices = assemble(me, spread)
        outs = None
        for items, parts in zip(chunks, exchanged):
            outs = absorb(me, items, parts, matrices, outs, shapes)
        return tuple(out.reshape(layer_count, per_group, -1, KVR) for out in outs)

    order = lax.rem(me - jnp.arange(t_ways, dtype=jnp.int32) + t_ways, jnp.int32(t_ways))
    matrices = jnp.take(jnp.stack(spread), order, axis=0).transpose(2, 3, 1, 0, 4, 5)
    matrices = matrices.reshape(item_count, 2, -1, KVR)
    done = [
        absorb_plain(me, parts, matrices[items[0] : items[-1] + 1])
        for items, parts in zip(chunks, exchanged)
    ]
    return tuple(jnp.concatenate(kind).reshape(layer_count, per_group, -1, KVR) for kind in zip(*done))


def solution(mesh):
    placed = (P(None, ("fsdp", "tp")), P(), P(), P())
    return jax.shard_map(
        per_device,
        mesh=mesh,
        in_specs=placed,
        out_specs=(P(None, "fsdp", "tp", None), P(None, "fsdp", "tp", None)),
        check_vma=False,
    )
```

```python
import functools
import math

import jax
import jax.numpy as jnp
from jax import lax
from jax.experimental import pallas as pl
from jax.experimental.pallas import tpu as pltpu
from jax.sharding import PartitionSpec as P

D = 7168
QR = 1536
KVR = 512
QK_NOPE = 128
V_DIM = 128
LANES = 128
QUERY, KEY, VALUE, OUT = range(4)
CUT_MICROS = 30
TOKEN_MICROS = 40
CUTS = (0, 1, 3, 5, 8)
VMEM_LIMIT = 16 * 1024 * 1024


def piece_widths(rank_total):
    return (
        QR * QK_NOPE // rank_total,
        QK_NOPE * KVR // rank_total,
        V_DIM * KVR // rank_total,
        D * V_DIM // rank_total,
    )


def pack(table, param_offsets, owner_map, ways, widths, granule, parts):
    layer_count, head_count = owner_map.shape
    per_group = head_count // ways
    sizes = [width // granule for width in widths]
    outs = [
        jax.ShapeDtypeStruct(
            (ways, sum(len(items) * sum(sizes[kind] for kind in kinds) for items, kinds in part))
            + table.shape[2:],
            table.dtype,
        )
        for part in parts
    ]

    def kernel(offsets, owners, source, *refs):
        targets, (taken, head_at) = refs[:-2], refs[-2:]
        for layer in sorted({item // per_group for part in parts for items, _ in part for item in items}):
            for way in range(ways):
                taken[way] = layer * per_group

            def place(head):
                way = owners[layer, head]
                item = taken[way]
                taken[way] = item + 1
                head_at[item * ways + way] = head

            pl.loop(0, head_count, unroll=min(8, head_count))(place)

        for target, part in zip(targets, parts):
            start = 0
            for item, kinds in [(item, kinds) for items, kinds in part for item in items]:

                def move(way):
                    head = head_at[item * ways + way]
                    at = start
                    for kind in kinds:
                        begin = lax.div(offsets[item // per_group, head, kind], jnp.int32(granule))
                        target[way, pl.ds(at, sizes[kind])] = source[
                            item // per_group, pl.ds(begin, sizes[kind])
                        ]
                        at += sizes[kind]

                pl.loop(0, ways, unroll=min(8, ways))(move)
                start += sum(sizes[kind] for kind in kinds)

    return pl.pallas_call(
        kernel,
        out_shape=outs,
        in_specs=[
            pl.BlockSpec(memory_space=pltpu.SMEM),
            pl.BlockSpec(memory_space=pltpu.SMEM),
            pl.BlockSpec(memory_space=pltpu.VMEM),
        ],
        out_specs=[pl.BlockSpec(memory_space=pltpu.VMEM)] * len(outs),
        scratch_shapes=[
            pltpu.SMEM((ways,), jnp.int32),
            pltpu.SMEM((layer_count * head_count,), jnp.int32),
        ],
        compiler_params=pltpu.CompilerParams(vmem_limit_bytes=VMEM_LIMIT),
        cost_estimate=pl.CostEstimate(
            flops=0,
            transcendentals=0,
            bytes_accessed=sum(2 * 2 * math.prod(out.shape) for out in outs),
        ),
        name="pack",
    )(param_offsets, owner_map, table)


def corner_of(x):
    return (1,) * (x.ndim - 2) + (min(16, x.shape[-2]), LANES)


def corner(x):
    return pl.BlockSpec(corner_of(x), lambda _: (0,) * x.ndim)


def cut(rows, slice_map, blocks, ahead, item_rows, waits, micros):
    t_ways = slice_map.shape[1]
    first = math.prod(ahead)
    items = (rows.shape[1] - first) // item_rows
    shapes = [(rows.shape[0],) + ahead + rows.shape[2:]] if first else []
    shapes += [(blocks, items, item_rows) + rows.shape[2:]] * t_ways

    def kernel(mapped, source, *refs):
        f_me, t_me = lax.axis_index("fsdp"), lax.axis_index("tp")
        refs = refs[len(waits) :]
        if first:
            for f in range(rows.shape[0]):
                for item in range(ahead[0]):
                    for kind in range(ahead[1]):
                        start = (item * ahead[1] + kind) * ahead[2]
                        refs[0][f, item, kind] = source[f, start : start + ahead[2]]
            refs = refs[1:]
        for shift, piece in enumerate(refs):
            block = mapped[f_me, lax.rem(t_me + shift, t_ways)]
            for f in range(blocks):
                for item in range(items):
                    start = first + item * item_rows
                    piece[f, item] = source[block * blocks + f, start : start + item_rows]

    return pl.pallas_call(
        kernel,
        grid=(1,),
        out_shape=[jax.ShapeDtypeStruct(shape, rows.dtype) for shape in shapes],
        in_specs=[pl.BlockSpec(memory_space=pltpu.SMEM), pl.BlockSpec(memory_space=pltpu.VMEM)]
        + [corner(x) for x in waits],
        out_specs=[pl.BlockSpec(memory_space=pltpu.VMEM)] * len(shapes),
        compiler_params=pltpu.CompilerParams(vmem_limit_bytes=VMEM_LIMIT),
        cost_estimate=pl.CostEstimate(
            flops=int(micros * 1.15e9),
            transcendentals=0,
            bytes_accessed=4 * sum(math.prod(shape) for shape in shapes),
        ),
        name="cut",
    )(slice_map, rows, *waits)


def token(waits, micros):
    def kernel(*refs):
        refs[-1][...] = jnp.zeros(refs[-1].shape, refs[-1].dtype)

    return pl.pallas_call(
        kernel,
        grid=(1,),
        out_shape=jax.ShapeDtypeStruct((16, LANES), jnp.bfloat16),
        in_specs=[corner(x) for x in waits],
        cost_estimate=pl.CostEstimate(
            flops=int(micros * 1.15e9), transcendentals=0, bytes_accessed=0
        ),
        name="token",
    )(*waits)


def neighbours(x, axis, ways):
    return (
        lax.ppermute(x, axis, [(i, i + 1) for i in range(ways - 1)]),
        lax.ppermute(x, axis, [(i + 1, i) for i in range(ways - 1)]),
    )


def pass_on(me, across, up, down, waits):
    def kernel(me_ref, first, above, below, *refs):
        out = refs[-1]
        out[0] = first[...]

        @pl.when(me_ref[0] == 2)
        def _():
            out[1] = above[...]

        @pl.when(me_ref[0] != 2)
        def _():
            out[1] = below[...]

    whole = pl.BlockSpec(across.shape, lambda _, me_ref: (0,) * across.ndim)
    corners = [pl.BlockSpec(corner_of(x), lambda _, me_ref, n=x.ndim: (0,) * n) for x in waits]
    return pl.pallas_call(
        kernel,
        grid_spec=pltpu.PrefetchScalarGridSpec(
            num_scalar_prefetch=1,
            grid=(1,),
            in_specs=[whole] * 3 + corners,
            out_specs=pl.BlockSpec((2,) + across.shape, lambda _, me_ref: (0,) * (across.ndim + 1)),
        ),
        out_shape=jax.ShapeDtypeStruct((2,) + across.shape, across.dtype),
        compiler_params=pltpu.CompilerParams(vmem_limit_bytes=VMEM_LIMIT),
        name="pass_on",
    )(me.reshape(1), across, up, down, *waits)


def assemble(me, spread_parts):
    t_ways = len(spread_parts)
    f_ways, items, kinds, rows, _ = spread_parts[0].shape
    depth = t_ways * f_ways * rows * LANES // KVR
    cuts = KVR // LANES

    def kernel(me_ref, *refs):
        pieces, (out, scratch) = refs[:t_ways], refs[t_ways:]
        for kind in range(kinds):
            for d in range(t_ways):
                t = lax.rem(me_ref[0] - d + t_ways, t_ways)
                for f in range(f_ways):
                    scratch[pl.ds(pl.multiple_of((f * t_ways + t) * rows, rows), rows), :] = pieces[
                        d
                    ][f, 0, kind].astype(jnp.float32)
            for cut in range(cuts):
                out[0, kind, :, pl.ds(cut * LANES, LANES)] = scratch[
                    pl.ds(cut, depth, stride=cuts), :
                ].astype(jnp.bfloat16)

    return pl.pallas_call(
        kernel,
        grid_spec=pltpu.PrefetchScalarGridSpec(
            num_scalar_prefetch=1,
            grid=(items,),
            in_specs=[pl.BlockSpec((f_ways, 1, kinds, rows, LANES), lambda i, _: (0, i, 0, 0, 0))] * t_ways,
            out_specs=pl.BlockSpec((1, kinds, depth, KVR), lambda i, _: (i, 0, 0, 0)),
            scratch_shapes=[pltpu.VMEM((depth * cuts, LANES), jnp.float32)],
        ),
        out_shape=jax.ShapeDtypeStruct((items, kinds, depth, KVR), spread_parts[0].dtype),
        compiler_params=pltpu.CompilerParams(vmem_limit_bytes=VMEM_LIMIT),
        name="assemble",
    )(me.reshape(1), *spread_parts)


def absorb(me, items, parts, matrices, outs, shapes):
    t_ways = len(parts)
    blocks = parts[0].shape[0]
    q_rows, o_rows = shapes[0].shape[3], shapes[1].shape[3]
    rows = q_rows + o_rows

    def kernel(at, *refs):
        parts, mats = refs[:t_ways], refs[t_ways]
        q_out, o_out = refs[-2:]
        for d in range(t_ways):
            t = lax.rem(at[0] - d + t_ways, t_ways)
            for f in range(blocks):
                q_out[0, f, t] = jnp.dot(
                    parts[d][f, 0, :q_rows], mats[0, 0], preferred_element_type=jnp.float32
                ).astype(jnp.bfloat16)
                o_out[0, f, t] = jnp.dot(
                    parts[d][f, 0, q_rows:], mats[0, 1], preferred_element_type=jnp.float32
                ).astype(jnp.bfloat16)

    in_specs = [pl.BlockSpec((blocks, 1, rows, LANES), lambda j, at: (0, j, 0, 0))] * t_ways
    in_specs += [pl.BlockSpec((1,) + matrices.shape[1:], lambda j, at: (items[0] + j, 0, 0, 0))]
    args = [*parts, matrices]
    aliases = {}
    if outs is not None:
        in_specs += [pl.BlockSpec(memory_space=pl.ANY)] * 2
        aliases = {1 + len(args): 0, 2 + len(args): 1}
        args += list(outs)
    work = t_ways * blocks * len(items) * rows
    return pl.pallas_call(
        kernel,
        grid_spec=pltpu.PrefetchScalarGridSpec(
            num_scalar_prefetch=1,
            grid=(len(items),),
            in_specs=in_specs,
            out_specs=[
                pl.BlockSpec((1,) + shape.shape[1:], lambda j, at: (items[0] + j, 0, 0, 0, 0))
                for shape in shapes
            ],
        ),
        out_shape=shapes,
        input_output_aliases=aliases,
        compiler_params=pltpu.CompilerParams(vmem_limit_bytes=VMEM_LIMIT),
        cost_estimate=pl.CostEstimate(
            flops=2 * work * LANES * KVR,
            transcendentals=0,
            bytes_accessed=2 * work * (LANES + KVR),
        ),
        name="absorb",
    )(me.reshape(1), *args)


def absorb_plain(me, parts, matrices):
    t_ways = len(parts)
    order = lax.rem(me - jnp.arange(t_ways, dtype=jnp.int32) + t_ways, jnp.int32(t_ways))
    rows = jnp.take(jnp.stack(parts), order, axis=0).transpose(2, 1, 0, 3, 4)
    cut = rows.shape[3] * QR // (QR + D)
    return tuple(
        jnp.einsum("hrc,hck->hrk", part, mats, preferred_element_type=jnp.float32).astype(jnp.bfloat16)
        for part, mats in (
            (rows[:, :, :, :cut].reshape(rows.shape[0], -1, LANES), matrices[:, 0]),
            (rows[:, :, :, cut:].reshape(rows.shape[0], -1, LANES), matrices[:, 1]),
        )
    )


def per_device(learner_flat, param_offsets, owner_map, slice_map):
    f_ways, t_ways = lax.axis_size("fsdp"), lax.axis_size("tp")
    layer_count = learner_flat.shape[0]
    per_group = owner_map.shape[1] // f_ways
    item_count = layer_count * per_group
    widths = piece_widths(f_ways * t_ways)
    granule = functools.reduce(math.gcd, widths)
    table = learner_flat.reshape(layer_count, -1, granule // LANES, LANES)
    whole_tiles = granule % (16 * LANES) == 0
    row_counts = [width // LANES for width in widths]
    item_rows = row_counts[QUERY] + row_counts[OUT]
    ahead = (item_count, 2, row_counts[KEY])

    me = lax.axis_index("tp")
    blocks = f_ways // t_ways
    cuts = [item_count * eighths // 8 for eighths in CUTS]
    chunks = [range(low, high) for low, high in zip(cuts, cuts[1:]) if low < high]

    def packed(parts):
        return pack(table, param_offsets, owner_map, f_ways, widths, granule, parts)

    def over_fsdp(x):
        x = lax.all_to_all(x, "fsdp", split_axis=0, concat_axis=0, tiled=True)
        return x.reshape(f_ways, -1, LANES)

    first_parts = [[(range(item_count), (KEY, VALUE)), (chunks[0], (QUERY, OUT))]]
    other_parts = [[(items, (QUERY, OUT))] for items in chunks[1:]]
    to_send = packed(first_parts + other_parts)

    exchanged, sent = [], []
    for at in range(len(chunks)):
        rows = over_fsdp(to_send[at])
        waits = sent[at - 1][:1] if at else []
        if at >= 2:
            waits = waits + exchanged[at - 2][1:]
        if at == 1:
            waits = waits + exchanged[0][1:3]
        if t_ways == 4 and at in (1, len(chunks) - 1):
            waits = waits + [near if at == 1 else far]
        pieces = list(cut(rows, slice_map, blocks, ahead if at == 0 else (0,), item_rows, waits, CUT_MICROS))
        if at == 0:
            pairs = pieces.pop(0)
            up, down = neighbours(pairs, "tp", t_ways)
            if t_ways == 4:
                across = lax.ppermute(pairs, "tp", [(0, 2), (3, 1)])
                near = token([up, down, across], TOKEN_MICROS)
                far = lax.ppermute(pass_on(me, across, up, down, []), "tp", [(1, 0), (2, 3)])
        sent.append(pieces)
        exchanged.append(
            pieces[:1]
            + [
                lax.ppermute(piece, "tp", [(i, (i + shift) % t_ways) for i in range(t_ways)])
                for shift, piece in enumerate(pieces)
                if shift
            ]
        )

    if t_ways == 4:
        ends = jnp.logical_or(me == 0, me == 3)
        spread = [
            pairs,
            jnp.where(me == 0, far[0], up),
            jnp.where(ends, far[1], across),
            jnp.where(me == 3, far[0], down),
        ]
    else:
        ups, downs = [pairs, up], [pairs, down]
        for _ in range(2, t_ways):
            ups.append(neighbours(ups[-1], "tp", t_ways)[0])
            downs.append(neighbours(downs[-1], "tp", t_ways)[1])
        spread = [pairs] + [jnp.where(me >= d, ups[d], downs[t_ways - d]) for d in range(1, t_ways)]

    if whole_tiles:
        shapes = tuple(
            jax.ShapeDtypeStruct((item_count, blocks, t_ways, row_counts[kind], KVR), jnp.bfloat16)
            for kind in (QUERY, OUT)
        )
        matrices = assemble(me, spread)
        outs = None
        for items, parts in zip(chunks, exchanged):
            outs = absorb(me, items, parts, matrices, outs, shapes)
        return tuple(out.reshape(layer_count, per_group, -1, KVR) for out in outs)

    order = lax.rem(me - jnp.arange(t_ways, dtype=jnp.int32) + t_ways, jnp.int32(t_ways))
    matrices = jnp.take(jnp.stack(spread), order, axis=0).transpose(2, 3, 1, 0, 4, 5)
    matrices = matrices.reshape(item_count, 2, -1, KVR)
    done = [
        absorb_plain(me, parts, matrices[items[0] : items[-1] + 1])
        for items, parts in zip(chunks, exchanged)
    ]
    return tuple(jnp.concatenate(kind).reshape(layer_count, per_group, -1, KVR) for kind in zip(*done))


def solution(mesh):
    placed = (P(None, ("fsdp", "tp")), P(), P(), P())
    return jax.shard_map(
        per_device,
        mesh=mesh,
        in_specs=placed,
        out_specs=(P(None, "fsdp", "tp", None), P(None, "fsdp", "tp", None)),
        check_vma=False,
    )
```

```python
import functools
import math

import jax
import jax.numpy as jnp
from jax import lax
from jax.experimental import pallas as pl
from jax.experimental.pallas import tpu as pltpu
from jax.sharding import PartitionSpec as P

D = 7168
QR = 1536
KVR = 512
QK_NOPE = 128
V_DIM = 128
LANES = 128
QUERY, KEY, VALUE, OUT = range(4)
CUT_MICROS = 10
TOKEN_MICROS = 20
CUTS = (0, 1, 4, 6, 8)
VMEM_LIMIT = 16 * 1024 * 1024


def piece_widths(rank_total):
    return (
        QR * QK_NOPE // rank_total,
        QK_NOPE * KVR // rank_total,
        V_DIM * KVR // rank_total,
        D * V_DIM // rank_total,
    )


def pack(table, param_offsets, owner_map, ways, widths, granule, parts):
    layer_count, head_count = owner_map.shape
    per_group = head_count // ways
    sizes = [width // granule for width in widths]
    outs = [
        jax.ShapeDtypeStruct(
            (ways, sum(len(items) * sum(sizes[kind] for kind in kinds) for items, kinds in part))
            + table.shape[2:],
            table.dtype,
        )
        for part in parts
    ]

    def kernel(offsets, owners, source, *refs):
        targets, (taken, head_at) = refs[:-2], refs[-2:]
        for layer in sorted({item // per_group for part in parts for items, _ in part for item in items}):
            for way in range(ways):
                taken[way] = layer * per_group

            def place(head):
                way = owners[layer, head]
                item = taken[way]
                taken[way] = item + 1
                head_at[item * ways + way] = head

            pl.loop(0, head_count, unroll=min(8, head_count))(place)

        for target, part in zip(targets, parts):
            start = 0
            for item, kinds in [(item, kinds) for items, kinds in part for item in items]:

                def move(way):
                    head = head_at[item * ways + way]
                    at = start
                    for kind in kinds:
                        begin = lax.div(offsets[item // per_group, head, kind], jnp.int32(granule))
                        target[way, pl.ds(at, sizes[kind])] = source[
                            item // per_group, pl.ds(begin, sizes[kind])
                        ]
                        at += sizes[kind]

                pl.loop(0, ways, unroll=min(8, ways))(move)
                start += sum(sizes[kind] for kind in kinds)

    return pl.pallas_call(
        kernel,
        out_shape=outs,
        in_specs=[
            pl.BlockSpec(memory_space=pltpu.SMEM),
            pl.BlockSpec(memory_space=pltpu.SMEM),
            pl.BlockSpec(memory_space=pltpu.VMEM),
        ],
        out_specs=[pl.BlockSpec(memory_space=pltpu.VMEM)] * len(outs),
        scratch_shapes=[
            pltpu.SMEM((ways,), jnp.int32),
            pltpu.SMEM((layer_count * head_count,), jnp.int32),
        ],
        compiler_params=pltpu.CompilerParams(vmem_limit_bytes=VMEM_LIMIT),
        cost_estimate=pl.CostEstimate(
            flops=0,
            transcendentals=0,
            bytes_accessed=sum(2 * 2 * math.prod(out.shape) for out in outs),
        ),
        name="pack",
    )(param_offsets, owner_map, table)


def corner_of(x):
    return (1,) * (x.ndim - 2) + (min(16, x.shape[-2]), LANES)


def corner(x):
    return pl.BlockSpec(corner_of(x), lambda _: (0,) * x.ndim)


def cut(rows, slice_map, blocks, ahead, item_rows, waits, micros):
    t_ways = slice_map.shape[1]
    first = math.prod(ahead)
    items = (rows.shape[1] - first) // item_rows
    shapes = [(rows.shape[0],) + ahead + rows.shape[2:]] if first else []
    shapes += [(blocks, items, item_rows) + rows.shape[2:]] * t_ways

    def kernel(mapped, source, *refs):
        f_me, t_me = lax.axis_index("fsdp"), lax.axis_index("tp")
        refs = refs[len(waits) :]
        if first:
            for f in range(rows.shape[0]):
                for item in range(ahead[0]):
                    for kind in range(ahead[1]):
                        start = (item * ahead[1] + kind) * ahead[2]
                        refs[0][f, item, kind] = source[f, start : start + ahead[2]]
            refs = refs[1:]
        for shift, piece in enumerate(refs):
            block = mapped[f_me, lax.rem(t_me + shift, t_ways)]
            for f in range(blocks):
                for item in range(items):
                    start = first + item * item_rows
                    piece[f, item] = source[block * blocks + f, start : start + item_rows]

    return pl.pallas_call(
        kernel,
        grid=(1,),
        out_shape=[jax.ShapeDtypeStruct(shape, rows.dtype) for shape in shapes],
        in_specs=[pl.BlockSpec(memory_space=pltpu.SMEM), pl.BlockSpec(memory_space=pltpu.VMEM)]
        + [corner(x) for x in waits],
        out_specs=[pl.BlockSpec(memory_space=pltpu.VMEM)] * len(shapes),
        compiler_params=pltpu.CompilerParams(vmem_limit_bytes=VMEM_LIMIT),
        cost_estimate=pl.CostEstimate(
            flops=int(micros * 1.15e9),
            transcendentals=0,
            bytes_accessed=4 * sum(math.prod(shape) for shape in shapes),
        ),
        name="cut",
    )(slice_map, rows, *waits)


def token(waits, micros):
    def kernel(*refs):
        refs[-1][...] = jnp.zeros(refs[-1].shape, refs[-1].dtype)

    return pl.pallas_call(
        kernel,
        grid=(1,),
        out_shape=jax.ShapeDtypeStruct((16, LANES), jnp.bfloat16),
        in_specs=[corner(x) for x in waits],
        cost_estimate=pl.CostEstimate(
            flops=int(micros * 1.15e9), transcendentals=0, bytes_accessed=0
        ),
        name="token",
    )(*waits)


def neighbours(x, axis, ways):
    return (
        lax.ppermute(x, axis, [(i, i + 1) for i in range(ways - 1)]),
        lax.ppermute(x, axis, [(i + 1, i) for i in range(ways - 1)]),
    )


def pass_on(me, across, up, down, waits):
    def kernel(me_ref, first, above, below, *refs):
        out = refs[-1]
        out[0] = first[...]

        @pl.when(me_ref[0] == 2)
        def _():
            out[1] = above[...]

        @pl.when(me_ref[0] != 2)
        def _():
            out[1] = below[...]

    whole = pl.BlockSpec(across.shape, lambda _, me_ref: (0,) * across.ndim)
    corners = [pl.BlockSpec(corner_of(x), lambda _, me_ref, n=x.ndim: (0,) * n) for x in waits]
    return pl.pallas_call(
        kernel,
        grid_spec=pltpu.PrefetchScalarGridSpec(
            num_scalar_prefetch=1,
            grid=(1,),
            in_specs=[whole] * 3 + corners,
            out_specs=pl.BlockSpec((2,) + across.shape, lambda _, me_ref: (0,) * (across.ndim + 1)),
        ),
        out_shape=jax.ShapeDtypeStruct((2,) + across.shape, across.dtype),
        compiler_params=pltpu.CompilerParams(vmem_limit_bytes=VMEM_LIMIT),
        name="pass_on",
    )(me.reshape(1), across, up, down, *waits)


def assemble(me, spread_parts):
    t_ways = len(spread_parts)
    f_ways, items, kinds, rows, _ = spread_parts[0].shape
    depth = t_ways * f_ways * rows * LANES // KVR
    cuts = KVR // LANES

    def kernel(me_ref, *refs):
        pieces, (out, scratch) = refs[:t_ways], refs[t_ways:]
        for kind in range(kinds):
            for d in range(t_ways):
                t = lax.rem(me_ref[0] - d + t_ways, t_ways)
                for f in range(f_ways):
                    scratch[pl.ds(pl.multiple_of((f * t_ways + t) * rows, rows), rows), :] = pieces[
                        d
                    ][f, 0, kind].astype(jnp.float32)
            for cut in range(cuts):
                out[0, kind, :, pl.ds(cut * LANES, LANES)] = scratch[
                    pl.ds(cut, depth, stride=cuts), :
                ].astype(jnp.bfloat16)

    return pl.pallas_call(
        kernel,
        grid_spec=pltpu.PrefetchScalarGridSpec(
            num_scalar_prefetch=1,
            grid=(items,),
            in_specs=[pl.BlockSpec((f_ways, 1, kinds, rows, LANES), lambda i, _: (0, i, 0, 0, 0))] * t_ways,
            out_specs=pl.BlockSpec((1, kinds, depth, KVR), lambda i, _: (i, 0, 0, 0)),
            scratch_shapes=[pltpu.VMEM((depth * cuts, LANES), jnp.float32)],
        ),
        out_shape=jax.ShapeDtypeStruct((items, kinds, depth, KVR), spread_parts[0].dtype),
        compiler_params=pltpu.CompilerParams(vmem_limit_bytes=VMEM_LIMIT),
        name="assemble",
    )(me.reshape(1), *spread_parts)


def absorb(me, items, parts, matrices, outs, shapes):
    t_ways = len(parts)
    blocks = parts[0].shape[0]
    q_rows, o_rows = shapes[0].shape[3], shapes[1].shape[3]
    rows = q_rows + o_rows

    def kernel(at, *refs):
        parts, mats = refs[:t_ways], refs[t_ways]
        q_out, o_out = refs[-2:]
        for d in range(t_ways):
            t = lax.rem(at[0] - d + t_ways, t_ways)
            for f in range(blocks):
                q_out[0, f, t] = jnp.dot(
                    parts[d][f, 0, :q_rows], mats[0, 0], preferred_element_type=jnp.float32
                ).astype(jnp.bfloat16)
                o_out[0, f, t] = jnp.dot(
                    parts[d][f, 0, q_rows:], mats[0, 1], preferred_element_type=jnp.float32
                ).astype(jnp.bfloat16)

    in_specs = [pl.BlockSpec((blocks, 1, rows, LANES), lambda j, at: (0, j, 0, 0))] * t_ways
    in_specs += [pl.BlockSpec((1,) + matrices.shape[1:], lambda j, at: (items[0] + j, 0, 0, 0))]
    args = [*parts, matrices]
    aliases = {}
    if outs is not None:
        in_specs += [pl.BlockSpec(memory_space=pl.ANY)] * 2
        aliases = {1 + len(args): 0, 2 + len(args): 1}
        args += list(outs)
    work = t_ways * blocks * len(items) * rows
    return pl.pallas_call(
        kernel,
        grid_spec=pltpu.PrefetchScalarGridSpec(
            num_scalar_prefetch=1,
            grid=(len(items),),
            in_specs=in_specs,
            out_specs=[
                pl.BlockSpec((1,) + shape.shape[1:], lambda j, at: (items[0] + j, 0, 0, 0, 0))
                for shape in shapes
            ],
        ),
        out_shape=shapes,
        input_output_aliases=aliases,
        compiler_params=pltpu.CompilerParams(vmem_limit_bytes=VMEM_LIMIT),
        cost_estimate=pl.CostEstimate(
            flops=2 * work * LANES * KVR,
            transcendentals=0,
            bytes_accessed=2 * work * (LANES + KVR),
        ),
        name="absorb",
    )(me.reshape(1), *args)


def absorb_plain(me, parts, matrices):
    t_ways = len(parts)
    order = lax.rem(me - jnp.arange(t_ways, dtype=jnp.int32) + t_ways, jnp.int32(t_ways))
    rows = jnp.take(jnp.stack(parts), order, axis=0).transpose(2, 1, 0, 3, 4)
    cut = rows.shape[3] * QR // (QR + D)
    return tuple(
        jnp.einsum("hrc,hck->hrk", part, mats, preferred_element_type=jnp.float32).astype(jnp.bfloat16)
        for part, mats in (
            (rows[:, :, :, :cut].reshape(rows.shape[0], -1, LANES), matrices[:, 0]),
            (rows[:, :, :, cut:].reshape(rows.shape[0], -1, LANES), matrices[:, 1]),
        )
    )


def per_device(learner_flat, param_offsets, owner_map, slice_map):
    f_ways, t_ways = lax.axis_size("fsdp"), lax.axis_size("tp")
    layer_count = learner_flat.shape[0]
    per_group = owner_map.shape[1] // f_ways
    item_count = layer_count * per_group
    widths = piece_widths(f_ways * t_ways)
    granule = functools.reduce(math.gcd, widths)
    table = learner_flat.reshape(layer_count, -1, granule // LANES, LANES)
    whole_tiles = granule % (16 * LANES) == 0
    row_counts = [width // LANES for width in widths]
    item_rows = row_counts[QUERY] + row_counts[OUT]
    ahead = (item_count, 2, row_counts[KEY])

    me = lax.axis_index("tp")
    blocks = f_ways // t_ways
    cuts = [item_count * eighths // 8 for eighths in CUTS]
    chunks = [range(low, high) for low, high in zip(cuts, cuts[1:]) if low < high]

    def packed(parts):
        return pack(table, param_offsets, owner_map, f_ways, widths, granule, parts)

    def over_fsdp(x):
        x = lax.all_to_all(x, "fsdp", split_axis=0, concat_axis=0, tiled=True)
        return x.reshape(f_ways, -1, LANES)

    first_parts = [[(range(item_count), (KEY, VALUE)), (chunks[0], (QUERY, OUT))]]
    other_parts = [[(items, (QUERY, OUT))] for items in chunks[1:]]
    to_send = packed(first_parts + other_parts)

    exchanged, sent = [], []
    for at in range(len(chunks)):
        rows = over_fsdp(to_send[at])
        waits = sent[at - 1][:1] if at else []
        if at >= 2:
            waits = waits + exchanged[at - 2][1:]
        if at == 1:
            waits = waits + exchanged[0][1:3]
        if t_ways == 4 and at == 1:
            waits = waits + [near, passed]
        pieces = list(cut(rows, slice_map, blocks, ahead if at == 0 else (0,), item_rows, waits, CUT_MICROS))
        if at == 0:
            pairs = pieces.pop(0)
            up, down = neighbours(pairs, "tp", t_ways)
            if t_ways == 4:
                across = lax.ppermute(pairs, "tp", [(0, 2), (3, 1)])
                near = token([up, down, across], TOKEN_MICROS)
                passed = pass_on(me, across, up, down, [])
                far = lax.ppermute(passed, "tp", [(1, 0), (2, 3)])
        sent.append(pieces)
        exchanged.append(
            pieces[:1]
            + [
                lax.ppermute(piece, "tp", [(i, (i + shift) % t_ways) for i in range(t_ways)])
                for shift, piece in enumerate(pieces)
                if shift
            ]
        )

    if t_ways == 4:
        ends = jnp.logical_or(me == 0, me == 3)
        spread = [
            pairs,
            jnp.where(me == 0, far[0], up),
            jnp.where(ends, far[1], across),
            jnp.where(me == 3, far[0], down),
        ]
    else:
        ups, downs = [pairs, up], [pairs, down]
        for _ in range(2, t_ways):
            ups.append(neighbours(ups[-1], "tp", t_ways)[0])
            downs.append(neighbours(downs[-1], "tp", t_ways)[1])
        spread = [pairs] + [jnp.where(me >= d, ups[d], downs[t_ways - d]) for d in range(1, t_ways)]

    if whole_tiles:
        shapes = tuple(
            jax.ShapeDtypeStruct((item_count, blocks, t_ways, row_counts[kind], KVR), jnp.bfloat16)
            for kind in (QUERY, OUT)
        )
        matrices = assemble(me, spread)
        outs = None
        for items, parts in zip(chunks, exchanged):
            outs = absorb(me, items, parts, matrices, outs, shapes)
        return tuple(out.reshape(layer_count, per_group, -1, KVR) for out in outs)

    order = lax.rem(me - jnp.arange(t_ways, dtype=jnp.int32) + t_ways, jnp.int32(t_ways))
    matrices = jnp.take(jnp.stack(spread), order, axis=0).transpose(2, 3, 1, 0, 4, 5)
    matrices = matrices.reshape(item_count, 2, -1, KVR)
    done = [
        absorb_plain(me, parts, matrices[items[0] : items[-1] + 1])
        for items, parts in zip(chunks, exchanged)
    ]
    return tuple(jnp.concatenate(kind).reshape(layer_count, per_group, -1, KVR) for kind in zip(*done))


def solution(mesh):
    placed = (P(None, ("fsdp", "tp")), P(), P(), P())
    return jax.shard_map(
        per_device,
        mesh=mesh,
        in_specs=placed,
        out_specs=(P(None, "fsdp", "tp", None), P(None, "fsdp", "tp", None)),
        check_vma=False,
    )
```

```python
import functools
import math

import jax
import jax.numpy as jnp
from jax import lax
from jax.experimental import pallas as pl
from jax.experimental.pallas import tpu as pltpu
from jax.sharding import PartitionSpec as P

D = 7168
QR = 1536
KVR = 512
QK_NOPE = 128
V_DIM = 128
LANES = 128
QUERY, KEY, VALUE, OUT = range(4)
CUT_MICROS = 30
TOKEN_MICROS = 6
CUTS = (0, 1, 4, 6, 8)
GROUPS = (0, 1, 2, 4)
VMEM_LIMIT = 16 * 1024 * 1024


def piece_widths(rank_total):
    return (
        QR * QK_NOPE // rank_total,
        QK_NOPE * KVR // rank_total,
        V_DIM * KVR // rank_total,
        D * V_DIM // rank_total,
    )


def pack(table, param_offsets, owner_map, ways, widths, granule, parts):
    layer_count, head_count = owner_map.shape
    per_group = head_count // ways
    sizes = [width // granule for width in widths]
    outs = [
        jax.ShapeDtypeStruct(
            (ways, sum(len(items) * sum(sizes[kind] for kind in kinds) for items, kinds in part))
            + table.shape[2:],
            table.dtype,
        )
        for part in parts
    ]

    def kernel(offsets, owners, source, *refs):
        targets, (taken, head_at) = refs[:-2], refs[-2:]
        for layer in sorted({item // per_group for part in parts for items, _ in part for item in items}):
            for way in range(ways):
                taken[way] = layer * per_group

            def place(head):
                way = owners[layer, head]
                item = taken[way]
                taken[way] = item + 1
                head_at[item * ways + way] = head

            pl.loop(0, head_count, unroll=min(8, head_count))(place)

        for target, part in zip(targets, parts):
            start = 0
            for item, kinds in [(item, kinds) for items, kinds in part for item in items]:

                def move(way):
                    head = head_at[item * ways + way]
                    at = start
                    for kind in kinds:
                        begin = lax.div(offsets[item // per_group, head, kind], jnp.int32(granule))
                        target[way, pl.ds(at, sizes[kind])] = source[
                            item // per_group, pl.ds(begin, sizes[kind])
                        ]
                        at += sizes[kind]

                pl.loop(0, ways, unroll=min(8, ways))(move)
                start += sum(sizes[kind] for kind in kinds)

    return pl.pallas_call(
        kernel,
        out_shape=outs,
        in_specs=[
            pl.BlockSpec(memory_space=pltpu.SMEM),
            pl.BlockSpec(memory_space=pltpu.SMEM),
            pl.BlockSpec(memory_space=pltpu.VMEM),
        ],
        out_specs=[pl.BlockSpec(memory_space=pltpu.VMEM)] * len(outs),
        scratch_shapes=[
            pltpu.SMEM((ways,), jnp.int32),
            pltpu.SMEM((layer_count * head_count,), jnp.int32),
        ],
        compiler_params=pltpu.CompilerParams(vmem_limit_bytes=VMEM_LIMIT),
        cost_estimate=pl.CostEstimate(
            flops=0,
            transcendentals=0,
            bytes_accessed=sum(2 * 2 * math.prod(out.shape) for out in outs),
        ),
        name="pack",
    )(param_offsets, owner_map, table)


def corner_of(x):
    return (1,) * (x.ndim - 2) + (min(16, x.shape[-2]), LANES)


def corner(x):
    return pl.BlockSpec(corner_of(x), lambda _: (0,) * x.ndim)


def cut(rows, slice_map, blocks, ahead, first, items, item_rows, waits, micros):
    t_ways = slice_map.shape[1]
    shapes = [(rows.shape[0],) + ahead + rows.shape[2:]] if ahead else []
    shapes += [(blocks, items, item_rows) + rows.shape[2:]] * t_ways

    def kernel(mapped, source, *refs):
        f_me, t_me = lax.axis_index("fsdp"), lax.axis_index("tp")
        refs = refs[len(waits) :]
        if ahead:
            for f in range(rows.shape[0]):
                for item in range(ahead[0]):
                    for kind in range(ahead[1]):
                        start = (item * ahead[1] + kind) * ahead[2]
                        refs[0][f, item, kind] = source[f, start : start + ahead[2]]
            refs = refs[1:]
        for shift, piece in enumerate(refs):
            block = mapped[f_me, lax.rem(t_me + shift, t_ways)]
            for f in range(blocks):
                for item in range(items):
                    start = first + item * item_rows
                    piece[f, item] = source[block * blocks + f, start : start + item_rows]

    return pl.pallas_call(
        kernel,
        grid=(1,),
        out_shape=[jax.ShapeDtypeStruct(shape, rows.dtype) for shape in shapes],
        in_specs=[pl.BlockSpec(memory_space=pltpu.SMEM), pl.BlockSpec(memory_space=pltpu.VMEM)]
        + [corner(x) for x in waits],
        out_specs=[pl.BlockSpec(memory_space=pltpu.VMEM)] * len(shapes),
        compiler_params=pltpu.CompilerParams(vmem_limit_bytes=VMEM_LIMIT),
        cost_estimate=pl.CostEstimate(
            flops=int(micros * 1.15e9),
            transcendentals=0,
            bytes_accessed=4 * sum(math.prod(shape) for shape in shapes),
        ),
        name="cut",
    )(slice_map, rows, *waits)


def token(waits, micros):
    def kernel(*refs):
        refs[-1][...] = jnp.zeros(refs[-1].shape, refs[-1].dtype)

    return pl.pallas_call(
        kernel,
        grid=(1,),
        out_shape=jax.ShapeDtypeStruct((16, LANES), jnp.bfloat16),
        in_specs=[corner(x) for x in waits],
        cost_estimate=pl.CostEstimate(
            flops=int(micros * 1.15e9), transcendentals=0, bytes_accessed=0
        ),
        name="token",
    )(*waits)


def neighbours(x, axis, ways):
    return (
        lax.ppermute(x, axis, [(i, i + 1) for i in range(ways - 1)]),
        lax.ppermute(x, axis, [(i + 1, i) for i in range(ways - 1)]),
    )


def pass_on(me, own, up, down):
    def kernel(me_ref, own_ref, up_ref, down_ref, out):
        for source, mine in (
            (own_ref, jnp.logical_or(me_ref[0] == 0, me_ref[0] == 3)),
            (up_ref, me_ref[0] == 2),
            (down_ref, me_ref[0] == 1),
        ):

            @pl.when(mine)
            def _():
                out[...] = source[...]

    whole = pl.BlockSpec(own.shape, lambda _, me_ref: (0,) * own.ndim)
    return pl.pallas_call(
        kernel,
        grid_spec=pltpu.PrefetchScalarGridSpec(
            num_scalar_prefetch=1, grid=(1,), in_specs=[whole] * 3, out_specs=whole
        ),
        out_shape=jax.ShapeDtypeStruct(own.shape, own.dtype),
        compiler_params=pltpu.CompilerParams(vmem_limit_bytes=VMEM_LIMIT),
        name="pass_on",
    )(me.reshape(1), own, up, down)


def assemble(me, spread_parts):
    t_ways = len(spread_parts)
    f_ways, items, kinds, rows, _ = spread_parts[0].shape
    depth = t_ways * f_ways * rows * LANES // KVR
    cuts = KVR // LANES

    def kernel(me_ref, *refs):
        pieces, (out, scratch) = refs[:t_ways], refs[t_ways:]
        for kind in range(kinds):
            for d in range(t_ways):
                t = lax.rem(me_ref[0] - d + t_ways, t_ways)
                for f in range(f_ways):
                    scratch[pl.ds(pl.multiple_of((f * t_ways + t) * rows, rows), rows), :] = pieces[
                        d
                    ][f, 0, kind].astype(jnp.float32)
            for cut in range(cuts):
                out[0, kind, :, pl.ds(cut * LANES, LANES)] = scratch[
                    pl.ds(cut, depth, stride=cuts), :
                ].astype(jnp.bfloat16)

    return pl.pallas_call(
        kernel,
        grid_spec=pltpu.PrefetchScalarGridSpec(
            num_scalar_prefetch=1,
            grid=(items,),
            in_specs=[pl.BlockSpec((f_ways, 1, kinds, rows, LANES), lambda i, _: (0, i, 0, 0, 0))] * t_ways,
            out_specs=pl.BlockSpec((1, kinds, depth, KVR), lambda i, _: (i, 0, 0, 0)),
            scratch_shapes=[pltpu.VMEM((depth * cuts, LANES), jnp.float32)],
        ),
        out_shape=jax.ShapeDtypeStruct((items, kinds, depth, KVR), spread_parts[0].dtype),
        compiler_params=pltpu.CompilerParams(vmem_limit_bytes=VMEM_LIMIT),
        name="assemble",
    )(me.reshape(1), *spread_parts)


def absorb(me, items, parts, matrices, outs, shapes):
    t_ways = len(parts)
    blocks = parts[0].shape[0]
    q_rows, o_rows = shapes[0].shape[3], shapes[1].shape[3]
    rows = q_rows + o_rows

    def kernel(at, *refs):
        parts, mats = refs[:t_ways], refs[t_ways]
        q_out, o_out = refs[-2:]
        for d in range(t_ways):
            t = lax.rem(at[0] - d + t_ways, t_ways)
            for f in range(blocks):
                q_out[0, f, t] = jnp.dot(
                    parts[d][f, 0, :q_rows], mats[0, 0], preferred_element_type=jnp.float32
                ).astype(jnp.bfloat16)
                o_out[0, f, t] = jnp.dot(
                    parts[d][f, 0, q_rows:], mats[0, 1], preferred_element_type=jnp.float32
                ).astype(jnp.bfloat16)

    in_specs = [pl.BlockSpec((blocks, 1, rows, LANES), lambda j, at: (0, j, 0, 0))] * t_ways
    in_specs += [pl.BlockSpec((1,) + matrices.shape[1:], lambda j, at: (items[0] + j, 0, 0, 0))]
    args = [*parts, matrices]
    aliases = {}
    if outs is not None:
        in_specs += [pl.BlockSpec(memory_space=pl.ANY)] * 2
        aliases = {1 + len(args): 0, 2 + len(args): 1}
        args += list(outs)
    work = t_ways * blocks * len(items) * rows
    return pl.pallas_call(
        kernel,
        grid_spec=pltpu.PrefetchScalarGridSpec(
            num_scalar_prefetch=1,
            grid=(len(items),),
            in_specs=in_specs,
            out_specs=[
                pl.BlockSpec((1,) + shape.shape[1:], lambda j, at: (items[0] + j, 0, 0, 0, 0))
                for shape in shapes
            ],
        ),
        out_shape=shapes,
        input_output_aliases=aliases,
        compiler_params=pltpu.CompilerParams(vmem_limit_bytes=VMEM_LIMIT),
        cost_estimate=pl.CostEstimate(
            flops=2 * work * LANES * KVR,
            transcendentals=0,
            bytes_accessed=2 * work * (LANES + KVR),
        ),
        name="absorb",
    )(me.reshape(1), *args)


def absorb_plain(me, parts, matrices):
    t_ways = len(parts)
    order = lax.rem(me - jnp.arange(t_ways, dtype=jnp.int32) + t_ways, jnp.int32(t_ways))
    rows = jnp.take(jnp.stack(parts), order, axis=0).transpose(2, 1, 0, 3, 4)
    cut = rows.shape[3] * QR // (QR + D)
    return tuple(
        jnp.einsum("hrc,hck->hrk", part, mats, preferred_element_type=jnp.float32).astype(jnp.bfloat16)
        for part, mats in (
            (rows[:, :, :, :cut].reshape(rows.shape[0], -1, LANES), matrices[:, 0]),
            (rows[:, :, :, cut:].reshape(rows.shape[0], -1, LANES), matrices[:, 1]),
        )
    )


def per_device(learner_flat, param_offsets, owner_map, slice_map):
    f_ways, t_ways = lax.axis_size("fsdp"), lax.axis_size("tp")
    layer_count = learner_flat.shape[0]
    per_group = owner_map.shape[1] // f_ways
    item_count = layer_count * per_group
    widths = piece_widths(f_ways * t_ways)
    granule = functools.reduce(math.gcd, widths)
    table = learner_flat.reshape(layer_count, -1, granule // LANES, LANES)
    whole_tiles = granule % (16 * LANES) == 0
    row_counts = [width // LANES for width in widths]
    item_rows = row_counts[QUERY] + row_counts[OUT]
    ahead = (item_count, 2, row_counts[KEY])

    me = lax.axis_index("tp")
    blocks = f_ways // t_ways
    cuts = [item_count * eighths // 8 for eighths in CUTS]
    chunks = [range(low, high) for low, high in zip(cuts, cuts[1:]) if low < high]

    def over_fsdp(x):
        x = lax.all_to_all(x, "fsdp", split_axis=0, concat_axis=0, tiled=True)
        return x.reshape(f_ways, -1, LANES)

    groups = [chunks[low:high] for low, high in zip(GROUPS, GROUPS[1:]) if chunks[low:high]]
    to_send = pack(
        table,
        param_offsets,
        owner_map,
        f_ways,
        widths,
        granule,
        [
            ([] if at else [(range(item_count), (KEY, VALUE))])
            + [(items, (QUERY, OUT)) for items in group]
            for at, group in enumerate(groups)
        ],
    )

    exchanged, sent = [], []
    for at in range(len(chunks)):
        group = [at in range(low, high) for low, high in zip(GROUPS, GROUPS[1:])].index(True)
        if at == GROUPS[group]:
            rows, first = over_fsdp(to_send[group]), 0 if at else math.prod(ahead)
        waits = sent[at - 1][:1] if at else []
        if at >= 2:
            waits = waits + exchanged[at - 2][1:]
        if at == 1:
            waits = waits + exchanged[0][1:3]
        if t_ways == 4 and at == 1:
            waits = waits + [near]
        pieces = list(
            cut(
                rows,
                slice_map,
                blocks,
                () if at else ahead,
                first,
                len(chunks[at]),
                item_rows,
                waits,
                CUT_MICROS,
            )
        )
        first += len(chunks[at]) * item_rows
        if at == 0:
            pairs = pieces.pop(0)
            up, down = neighbours(pairs, "tp", t_ways)
            if t_ways == 4:
                second = lax.ppermute(
                    pass_on(me, pairs, up, down), "tp", [(0, 2), (1, 0), (2, 3), (3, 1)]
                )
                third = lax.ppermute(second, "tp", [(1, 0), (2, 3)])
                near = token([up, down, second], TOKEN_MICROS)
        sent.append(pieces)
        exchanged.append(
            pieces[:1]
            + [
                lax.ppermute(piece, "tp", [(i, (i + shift) % t_ways) for i in range(t_ways)])
                for shift, piece in enumerate(pieces)
                if shift
            ]
        )

    if t_ways == 4:
        spread = [
            pairs,
            jnp.where(me == 0, third, up),
            second,
            jnp.where(me == 3, third, down),
        ]
    else:
        ups, downs = [pairs, up], [pairs, down]
        for _ in range(2, t_ways):
            ups.append(neighbours(ups[-1], "tp", t_ways)[0])
            downs.append(neighbours(downs[-1], "tp", t_ways)[1])
        spread = [pairs] + [jnp.where(me >= d, ups[d], downs[t_ways - d]) for d in range(1, t_ways)]

    if whole_tiles:
        shapes = tuple(
            jax.ShapeDtypeStruct((item_count, blocks, t_ways, row_counts[kind], KVR), jnp.bfloat16)
            for kind in (QUERY, OUT)
        )
        matrices = assemble(me, spread)
        outs = None
        for items, parts in zip(chunks, exchanged):
            outs = absorb(me, items, parts, matrices, outs, shapes)
        return tuple(out.reshape(layer_count, per_group, -1, KVR) for out in outs)

    order = lax.rem(me - jnp.arange(t_ways, dtype=jnp.int32) + t_ways, jnp.int32(t_ways))
    matrices = jnp.take(jnp.stack(spread), order, axis=0).transpose(2, 3, 1, 0, 4, 5)
    matrices = matrices.reshape(item_count, 2, -1, KVR)
    done = [
        absorb_plain(me, parts, matrices[items[0] : items[-1] + 1])
        for items, parts in zip(chunks, exchanged)
    ]
    return tuple(jnp.concatenate(kind).reshape(layer_count, per_group, -1, KVR) for kind in zip(*done))


def solution(mesh):
    placed = (P(None, ("fsdp", "tp")), P(), P(), P())
    return jax.shard_map(
        per_device,
        mesh=mesh,
        in_specs=placed,
        out_specs=(P(None, "fsdp", "tp", None), P(None, "fsdp", "tp", None)),
        check_vma=False,
    )
```

```python
import functools
import math

import jax
import jax.numpy as jnp
from jax import lax
from jax.experimental import pallas as pl
from jax.experimental.pallas import tpu as pltpu
from jax.sharding import PartitionSpec as P

D = 7168
QR = 1536
KVR = 512
QK_NOPE = 128
V_DIM = 128
LANES = 128
QUERY, KEY, VALUE, OUT = range(4)
CUT_MICROS = 30
TOKEN_MICROS = 6
CUTS = (0, 1, 4, 6, 8)
GROUPS = (0, 1, 2, 4)
VMEM_LIMIT = 16 * 1024 * 1024


def piece_widths(rank_total):
    return (
        QR * QK_NOPE // rank_total,
        QK_NOPE * KVR // rank_total,
        V_DIM * KVR // rank_total,
        D * V_DIM // rank_total,
    )


def pack(table, param_offsets, owner_map, ways, widths, granule, parts):
    layer_count, head_count = owner_map.shape
    per_group = head_count // ways
    sizes = [width // granule for width in widths]
    outs = [
        jax.ShapeDtypeStruct(
            (ways, sum(len(items) * sum(sizes[kind] for kind in kinds) for items, kinds in part))
            + table.shape[2:],
            table.dtype,
        )
        for part in parts
    ]

    def kernel(offsets, owners, source, *refs):
        targets, (taken, head_at) = refs[:-2], refs[-2:]
        for layer in sorted({item // per_group for part in parts for items, _ in part for item in items}):
            for way in range(ways):
                taken[way] = layer * per_group

            def place(head):
                way = owners[layer, head]
                item = taken[way]
                taken[way] = item + 1
                head_at[item * ways + way] = head

            pl.loop(0, head_count, unroll=min(8, head_count))(place)

        for target, part in zip(targets, parts):
            start = 0
            for item, kinds in [(item, kinds) for items, kinds in part for item in items]:

                def move(way):
                    head = head_at[item * ways + way]
                    at = start
                    for kind in kinds:
                        begin = lax.div(offsets[item // per_group, head, kind], jnp.int32(granule))
                        target[way, pl.ds(at, sizes[kind])] = source[
                            item // per_group, pl.ds(begin, sizes[kind])
                        ]
                        at += sizes[kind]

                pl.loop(0, ways, unroll=min(8, ways))(move)
                start += sum(sizes[kind] for kind in kinds)

    return pl.pallas_call(
        kernel,
        out_shape=outs,
        in_specs=[
            pl.BlockSpec(memory_space=pltpu.SMEM),
            pl.BlockSpec(memory_space=pltpu.SMEM),
            pl.BlockSpec(memory_space=pltpu.VMEM),
        ],
        out_specs=[pl.BlockSpec(memory_space=pltpu.VMEM)] * len(outs),
        scratch_shapes=[
            pltpu.SMEM((ways,), jnp.int32),
            pltpu.SMEM((layer_count * head_count,), jnp.int32),
        ],
        compiler_params=pltpu.CompilerParams(vmem_limit_bytes=VMEM_LIMIT),
        cost_estimate=pl.CostEstimate(
            flops=0,
            transcendentals=0,
            bytes_accessed=sum(2 * 2 * math.prod(out.shape) for out in outs),
        ),
        name="pack",
    )(param_offsets, owner_map, table)


def corner_of(x):
    return (1,) * (x.ndim - 2) + (min(16, x.shape[-2]), LANES)


def corner(x):
    return pl.BlockSpec(corner_of(x), lambda _: (0,) * x.ndim)


def cut(rows, slice_map, blocks, ahead, first, items, item_rows, waits, micros):
    t_ways = slice_map.shape[1]
    shapes = [(rows.shape[0],) + ahead + rows.shape[2:]] if ahead else []
    shapes += [(blocks, items, item_rows) + rows.shape[2:]] * t_ways

    def kernel(mapped, source, *refs):
        f_me, t_me = lax.axis_index("fsdp"), lax.axis_index("tp")
        refs = refs[len(waits) :]
        if ahead:
            for f in range(rows.shape[0]):
                for item in range(ahead[0]):
                    for kind in range(ahead[1]):
                        start = (item * ahead[1] + kind) * ahead[2]
                        refs[0][f, item, kind] = source[f, start : start + ahead[2]]
            refs = refs[1:]
        for shift, piece in enumerate(refs):
            block = mapped[f_me, lax.rem(t_me + shift, t_ways)]
            for f in range(blocks):
                for item in range(items):
                    start = first + item * item_rows
                    piece[f, item] = source[block * blocks + f, start : start + item_rows]

    return pl.pallas_call(
        kernel,
        grid=(1,),
        out_shape=[jax.ShapeDtypeStruct(shape, rows.dtype) for shape in shapes],
        in_specs=[pl.BlockSpec(memory_space=pltpu.SMEM), pl.BlockSpec(memory_space=pltpu.VMEM)]
        + [corner(x) for x in waits],
        out_specs=[pl.BlockSpec(memory_space=pltpu.VMEM)] * len(shapes),
        compiler_params=pltpu.CompilerParams(vmem_limit_bytes=VMEM_LIMIT),
        cost_estimate=pl.CostEstimate(
            flops=int(micros * 1.15e9),
            transcendentals=0,
            bytes_accessed=4 * sum(math.prod(shape) for shape in shapes),
        ),
        name="cut",
    )(slice_map, rows, *waits)


def token(waits, micros):
    def kernel(*refs):
        refs[-1][...] = jnp.zeros(refs[-1].shape, refs[-1].dtype)

    return pl.pallas_call(
        kernel,
        grid=(1,),
        out_shape=jax.ShapeDtypeStruct((16, LANES), jnp.bfloat16),
        in_specs=[corner(x) for x in waits],
        cost_estimate=pl.CostEstimate(
            flops=int(micros * 1.15e9), transcendentals=0, bytes_accessed=0
        ),
        name="token",
    )(*waits)


def neighbours(x, axis, ways):
    return (
        lax.ppermute(x, axis, [(i, i + 1) for i in range(ways - 1)]),
        lax.ppermute(x, axis, [(i + 1, i) for i in range(ways - 1)]),
    )


def pass_on(me, own, up, down):
    def kernel(me_ref, own_ref, up_ref, down_ref, out):
        for source, mine in (
            (own_ref, jnp.logical_or(me_ref[0] == 0, me_ref[0] == 3)),
            (up_ref, me_ref[0] == 2),
            (down_ref, me_ref[0] == 1),
        ):

            @pl.when(mine)
            def _():
                out[...] = source[...]

    whole = pl.BlockSpec(own.shape, lambda _, me_ref: (0,) * own.ndim)
    return pl.pallas_call(
        kernel,
        grid_spec=pltpu.PrefetchScalarGridSpec(
            num_scalar_prefetch=1, grid=(1,), in_specs=[whole] * 3, out_specs=whole
        ),
        out_shape=jax.ShapeDtypeStruct(own.shape, own.dtype),
        compiler_params=pltpu.CompilerParams(vmem_limit_bytes=VMEM_LIMIT),
        name="pass_on",
    )(me.reshape(1), own, up, down)


def assemble(me, spread_parts):
    t_ways = len(spread_parts)
    f_ways, items, kinds, rows, _ = spread_parts[0].shape
    depth = t_ways * f_ways * rows * LANES // KVR
    cuts = KVR // LANES

    def kernel(me_ref, *refs):
        pieces, (out, scratch) = refs[:t_ways], refs[t_ways:]
        for kind in range(kinds):
            for d in range(t_ways):
                t = lax.rem(me_ref[0] - d + t_ways, t_ways)
                for f in range(f_ways):
                    scratch[pl.ds(pl.multiple_of((f * t_ways + t) * rows, rows), rows), :] = pieces[
                        d
                    ][f, 0, kind].astype(jnp.float32)
            for cut in range(cuts):
                out[0, kind, :, pl.ds(cut * LANES, LANES)] = scratch[
                    pl.ds(cut, depth, stride=cuts), :
                ].astype(jnp.bfloat16)

    return pl.pallas_call(
        kernel,
        grid_spec=pltpu.PrefetchScalarGridSpec(
            num_scalar_prefetch=1,
            grid=(items,),
            in_specs=[pl.BlockSpec((f_ways, 1, kinds, rows, LANES), lambda i, _: (0, i, 0, 0, 0))] * t_ways,
            out_specs=pl.BlockSpec((1, kinds, depth, KVR), lambda i, _: (i, 0, 0, 0)),
            scratch_shapes=[pltpu.VMEM((depth * cuts, LANES), jnp.float32)],
        ),
        out_shape=jax.ShapeDtypeStruct((items, kinds, depth, KVR), spread_parts[0].dtype),
        compiler_params=pltpu.CompilerParams(vmem_limit_bytes=VMEM_LIMIT),
        name="assemble",
    )(me.reshape(1), *spread_parts)


def absorb(me, items, parts, matrices, outs, shapes):
    t_ways = len(parts)
    blocks = parts[0].shape[0]
    q_rows, o_rows = shapes[0].shape[3], shapes[1].shape[3]
    rows = q_rows + o_rows

    def kernel(at, *refs):
        parts, mats = refs[:t_ways], refs[t_ways]
        q_out, o_out = refs[-2:]
        for d in range(t_ways):
            t = lax.rem(at[0] - d + t_ways, t_ways)
            for f in range(blocks):
                q_out[0, f, t] = jnp.dot(
                    parts[d][f, 0, :q_rows], mats[0, 0], preferred_element_type=jnp.float32
                ).astype(jnp.bfloat16)
                o_out[0, f, t] = jnp.dot(
                    parts[d][f, 0, q_rows:], mats[0, 1], preferred_element_type=jnp.float32
                ).astype(jnp.bfloat16)

    in_specs = [pl.BlockSpec((blocks, 1, rows, LANES), lambda j, at: (0, j, 0, 0))] * t_ways
    in_specs += [pl.BlockSpec((1,) + matrices.shape[1:], lambda j, at: (items[0] + j, 0, 0, 0))]
    args = [*parts, matrices]
    aliases = {}
    if outs is not None:
        in_specs += [pl.BlockSpec(memory_space=pl.ANY)] * 2
        aliases = {1 + len(args): 0, 2 + len(args): 1}
        args += list(outs)
    work = t_ways * blocks * len(items) * rows
    return pl.pallas_call(
        kernel,
        grid_spec=pltpu.PrefetchScalarGridSpec(
            num_scalar_prefetch=1,
            grid=(len(items),),
            in_specs=in_specs,
            out_specs=[
                pl.BlockSpec((1,) + shape.shape[1:], lambda j, at: (items[0] + j, 0, 0, 0, 0))
                for shape in shapes
            ],
        ),
        out_shape=shapes,
        input_output_aliases=aliases,
        compiler_params=pltpu.CompilerParams(vmem_limit_bytes=VMEM_LIMIT),
        cost_estimate=pl.CostEstimate(
            flops=2 * work * LANES * KVR,
            transcendentals=0,
            bytes_accessed=2 * work * (LANES + KVR),
        ),
        name="absorb",
    )(me.reshape(1), *args)


def absorb_plain(me, parts, matrices):
    t_ways = len(parts)
    order = lax.rem(me - jnp.arange(t_ways, dtype=jnp.int32) + t_ways, jnp.int32(t_ways))
    rows = jnp.take(jnp.stack(parts), order, axis=0).transpose(2, 1, 0, 3, 4)
    cut = rows.shape[3] * QR // (QR + D)
    return tuple(
        jnp.einsum("hrc,hck->hrk", part, mats, preferred_element_type=jnp.float32).astype(jnp.bfloat16)
        for part, mats in (
            (rows[:, :, :, :cut].reshape(rows.shape[0], -1, LANES), matrices[:, 0]),
            (rows[:, :, :, cut:].reshape(rows.shape[0], -1, LANES), matrices[:, 1]),
        )
    )


def per_device(learner_flat, param_offsets, owner_map, slice_map):
    f_ways, t_ways = lax.axis_size("fsdp"), lax.axis_size("tp")
    layer_count = learner_flat.shape[0]
    per_group = owner_map.shape[1] // f_ways
    item_count = layer_count * per_group
    widths = piece_widths(f_ways * t_ways)
    granule = functools.reduce(math.gcd, widths)
    table = learner_flat.reshape(layer_count, -1, granule // LANES, LANES)
    whole_tiles = granule % (16 * LANES) == 0
    row_counts = [width // LANES for width in widths]
    item_rows = row_counts[QUERY] + row_counts[OUT]
    ahead = (item_count, 2, row_counts[KEY])

    me = lax.axis_index("tp")
    blocks = f_ways // t_ways
    cuts = [item_count * eighths // 8 for eighths in CUTS]
    chunks = [range(low, high) for low, high in zip(cuts, cuts[1:]) if low < high]

    def over_fsdp(x):
        x = lax.all_to_all(x, "fsdp", split_axis=0, concat_axis=0, tiled=True)
        return x.reshape(f_ways, -1, LANES)

    groups = [chunks[low:high] for low, high in zip(GROUPS, GROUPS[1:]) if chunks[low:high]]
    to_send = pack(
        table,
        param_offsets,
        owner_map,
        f_ways,
        widths,
        granule,
        [
            ([] if at else [(range(item_count), (KEY, VALUE))])
            + [(items, (QUERY, OUT)) for items in group]
            for at, group in enumerate(groups)
        ],
    )

    exchanged, sent = [], []
    for at in range(len(chunks)):
        group = [at in range(low, high) for low, high in zip(GROUPS, GROUPS[1:])].index(True)
        if at == GROUPS[group]:
            rows, first = over_fsdp(to_send[group]), 0 if at else math.prod(ahead)
        waits = sent[at - 1][:1] if at else []
        if at >= 2:
            waits = waits + exchanged[at - 2][1:]
        if at == 1:
            waits = waits + exchanged[0][1:3]
        if t_ways == 4 and at in (1, len(chunks) - 1):
            waits = waits + [near if at == 1 else third]
        pieces = list(
            cut(
                rows,
                slice_map,
                blocks,
                () if at else ahead,
                first,
                len(chunks[at]),
                item_rows,
                waits,
                CUT_MICROS,
            )
        )
        first += len(chunks[at]) * item_rows
        if at == 0:
            pairs = pieces.pop(0)
            up, down = neighbours(pairs, "tp", t_ways)
            if t_ways == 4:
                second = lax.ppermute(
                    pass_on(me, pairs, up, down), "tp", [(0, 2), (1, 0), (2, 3), (3, 1)]
                )
                third = lax.ppermute(second, "tp", [(1, 0), (2, 3)])
                near = token([up, down, second], TOKEN_MICROS)
        sent.append(pieces)
        exchanged.append(
            pieces[:1]
            + [
                lax.ppermute(piece, "tp", [(i, (i + shift) % t_ways) for i in range(t_ways)])
                for shift, piece in enumerate(pieces)
                if shift
            ]
        )

    if t_ways == 4:
        spread = [
            pairs,
            jnp.where(me == 0, third, up),
            second,
            jnp.where(me == 3, third, down),
        ]
    else:
        ups, downs = [pairs, up], [pairs, down]
        for _ in range(2, t_ways):
            ups.append(neighbours(ups[-1], "tp", t_ways)[0])
            downs.append(neighbours(downs[-1], "tp", t_ways)[1])
        spread = [pairs] + [jnp.where(me >= d, ups[d], downs[t_ways - d]) for d in range(1, t_ways)]

    if whole_tiles:
        shapes = tuple(
            jax.ShapeDtypeStruct((item_count, blocks, t_ways, row_counts[kind], KVR), jnp.bfloat16)
            for kind in (QUERY, OUT)
        )
        matrices = assemble(me, spread)
        outs = None
        for items, parts in zip(chunks, exchanged):
            outs = absorb(me, items, parts, matrices, outs, shapes)
        return tuple(out.reshape(layer_count, per_group, -1, KVR) for out in outs)

    order = lax.rem(me - jnp.arange(t_ways, dtype=jnp.int32) + t_ways, jnp.int32(t_ways))
    matrices = jnp.take(jnp.stack(spread), order, axis=0).transpose(2, 3, 1, 0, 4, 5)
    matrices = matrices.reshape(item_count, 2, -1, KVR)
    done = [
        absorb_plain(me, parts, matrices[items[0] : items[-1] + 1])
        for items, parts in zip(chunks, exchanged)
    ]
    return tuple(jnp.concatenate(kind).reshape(layer_count, per_group, -1, KVR) for kind in zip(*done))


def solution(mesh):
    placed = (P(None, ("fsdp", "tp")), P(), P(), P())
    return jax.shard_map(
        per_device,
        mesh=mesh,
        in_specs=placed,
        out_specs=(P(None, "fsdp", "tp", None), P(None, "fsdp", "tp", None)),
        check_vma=False,
    )
```

```python
import functools
import math

import jax
import jax.numpy as jnp
from jax import lax
from jax.experimental import pallas as pl
from jax.experimental.pallas import tpu as pltpu
from jax.sharding import PartitionSpec as P

D = 7168
QR = 1536
KVR = 512
QK_NOPE = 128
V_DIM = 128
LANES = 128
QUERY, KEY, VALUE, OUT = range(4)
CUT_MICROS = 30
TOKEN_MICROS = 40
CUTS = (0, 2, 5, 8)
GROUPS = (0, 1, 2, 3)
VMEM_LIMIT = 16 * 1024 * 1024


def piece_widths(rank_total):
    return (
        QR * QK_NOPE // rank_total,
        QK_NOPE * KVR // rank_total,
        V_DIM * KVR // rank_total,
        D * V_DIM // rank_total,
    )


def pack(table, param_offsets, owner_map, ways, widths, granule, parts):
    layer_count, head_count = owner_map.shape
    per_group = head_count // ways
    sizes = [width // granule for width in widths]
    outs = [
        jax.ShapeDtypeStruct(
            (ways, sum(len(items) * sum(sizes[kind] for kind in kinds) for items, kinds in part))
            + table.shape[2:],
            table.dtype,
        )
        for part in parts
    ]

    def kernel(offsets, owners, source, *refs):
        targets, (taken, head_at) = refs[:-2], refs[-2:]
        for layer in sorted({item // per_group for part in parts for items, _ in part for item in items}):
            for way in range(ways):
                taken[way] = layer * per_group

            def place(head):
                way = owners[layer, head]
                item = taken[way]
                taken[way] = item + 1
                head_at[item * ways + way] = head

            pl.loop(0, head_count, unroll=min(8, head_count))(place)

        for target, part in zip(targets, parts):
            start = 0
            for item, kinds in [(item, kinds) for items, kinds in part for item in items]:

                def move(way):
                    head = head_at[item * ways + way]
                    at = start
                    for kind in kinds:
                        begin = lax.div(offsets[item // per_group, head, kind], jnp.int32(granule))
                        target[way, pl.ds(at, sizes[kind])] = source[
                            item // per_group, pl.ds(begin, sizes[kind])
                        ]
                        at += sizes[kind]

                pl.loop(0, ways, unroll=min(8, ways))(move)
                start += sum(sizes[kind] for kind in kinds)

    return pl.pallas_call(
        kernel,
        out_shape=outs,
        in_specs=[
            pl.BlockSpec(memory_space=pltpu.SMEM),
            pl.BlockSpec(memory_space=pltpu.SMEM),
            pl.BlockSpec(memory_space=pltpu.VMEM),
        ],
        out_specs=[pl.BlockSpec(memory_space=pltpu.VMEM)] * len(outs),
        scratch_shapes=[
            pltpu.SMEM((ways,), jnp.int32),
            pltpu.SMEM((layer_count * head_count,), jnp.int32),
        ],
        compiler_params=pltpu.CompilerParams(vmem_limit_bytes=VMEM_LIMIT),
        cost_estimate=pl.CostEstimate(
            flops=0,
            transcendentals=0,
            bytes_accessed=sum(2 * 2 * math.prod(out.shape) for out in outs),
        ),
        name="pack",
    )(param_offsets, owner_map, table)


def corner_of(x):
    return (1,) * (x.ndim - 2) + (min(16, x.shape[-2]), LANES)


def corner(x):
    return pl.BlockSpec(corner_of(x), lambda _: (0,) * x.ndim)


def cut(rows, slice_map, blocks, ahead, first, items, item_rows, waits, micros):
    t_ways = slice_map.shape[1]
    shapes = [(rows.shape[0],) + ahead + rows.shape[2:]] if ahead else []
    shapes += [(blocks, items, item_rows) + rows.shape[2:]] * t_ways

    def kernel(mapped, source, *refs):
        f_me, t_me = lax.axis_index("fsdp"), lax.axis_index("tp")
        refs = refs[len(waits) :]
        if ahead:
            for f in range(rows.shape[0]):
                for item in range(ahead[0]):
                    for kind in range(ahead[1]):
                        start = (item * ahead[1] + kind) * ahead[2]
                        refs[0][f, item, kind] = source[f, start : start + ahead[2]]
            refs = refs[1:]
        for shift, piece in enumerate(refs):
            block = mapped[f_me, lax.rem(t_me + shift, t_ways)]
            for f in range(blocks):
                for item in range(items):
                    start = first + item * item_rows
                    piece[f, item] = source[block * blocks + f, start : start + item_rows]

    return pl.pallas_call(
        kernel,
        grid=(1,),
        out_shape=[jax.ShapeDtypeStruct(shape, rows.dtype) for shape in shapes],
        in_specs=[pl.BlockSpec(memory_space=pltpu.SMEM), pl.BlockSpec(memory_space=pltpu.VMEM)]
        + [corner(x) for x in waits],
        out_specs=[pl.BlockSpec(memory_space=pltpu.VMEM)] * len(shapes),
        compiler_params=pltpu.CompilerParams(vmem_limit_bytes=VMEM_LIMIT),
        cost_estimate=pl.CostEstimate(
            flops=int(micros * 1.15e9),
            transcendentals=0,
            bytes_accessed=4 * sum(math.prod(shape) for shape in shapes),
        ),
        name="cut",
    )(slice_map, rows, *waits)


def token(waits, micros):
    def kernel(*refs):
        refs[-1][...] = jnp.zeros(refs[-1].shape, refs[-1].dtype)

    return pl.pallas_call(
        kernel,
        grid=(1,),
        out_shape=jax.ShapeDtypeStruct((16, LANES), jnp.bfloat16),
        in_specs=[corner(x) for x in waits],
        cost_estimate=pl.CostEstimate(
            flops=int(micros * 1.15e9), transcendentals=0, bytes_accessed=0
        ),
        name="token",
    )(*waits)


def neighbours(x, axis, ways):
    return (
        lax.ppermute(x, axis, [(i, i + 1) for i in range(ways - 1)]),
        lax.ppermute(x, axis, [(i + 1, i) for i in range(ways - 1)]),
    )


def pass_on(me, across, up, down, waits):
    def kernel(me_ref, first, above, below, *refs):
        out = refs[-1]
        out[0] = first[...]

        @pl.when(me_ref[0] == 2)
        def _():
            out[1] = above[...]

        @pl.when(me_ref[0] != 2)
        def _():
            out[1] = below[...]

    whole = pl.BlockSpec(across.shape, lambda _, me_ref: (0,) * across.ndim)
    corners = [pl.BlockSpec(corner_of(x), lambda _, me_ref, n=x.ndim: (0,) * n) for x in waits]
    return pl.pallas_call(
        kernel,
        grid_spec=pltpu.PrefetchScalarGridSpec(
            num_scalar_prefetch=1,
            grid=(1,),
            in_specs=[whole] * 3 + corners,
            out_specs=pl.BlockSpec((2,) + across.shape, lambda _, me_ref: (0,) * (across.ndim + 1)),
        ),
        out_shape=jax.ShapeDtypeStruct((2,) + across.shape, across.dtype),
        compiler_params=pltpu.CompilerParams(vmem_limit_bytes=VMEM_LIMIT),
        name="pass_on",
    )(me.reshape(1), across, up, down, *waits)


def assemble(me, spread_parts):
    t_ways = len(spread_parts)
    f_ways, items, kinds, rows, _ = spread_parts[0].shape
    depth = t_ways * f_ways * rows * LANES // KVR
    cuts = KVR // LANES

    def kernel(me_ref, *refs):
        pieces, (out, scratch) = refs[:t_ways], refs[t_ways:]
        for kind in range(kinds):
            for d in range(t_ways):
                t = lax.rem(me_ref[0] - d + t_ways, t_ways)
                for f in range(f_ways):
                    scratch[pl.ds(pl.multiple_of((f * t_ways + t) * rows, rows), rows), :] = pieces[
                        d
                    ][f, 0, kind].astype(jnp.float32)
            for cut in range(cuts):
                out[0, kind, :, pl.ds(cut * LANES, LANES)] = scratch[
                    pl.ds(cut, depth, stride=cuts), :
                ].astype(jnp.bfloat16)

    return pl.pallas_call(
        kernel,
        grid_spec=pltpu.PrefetchScalarGridSpec(
            num_scalar_prefetch=1,
            grid=(items,),
            in_specs=[pl.BlockSpec((f_ways, 1, kinds, rows, LANES), lambda i, _: (0, i, 0, 0, 0))] * t_ways,
            out_specs=pl.BlockSpec((1, kinds, depth, KVR), lambda i, _: (i, 0, 0, 0)),
            scratch_shapes=[pltpu.VMEM((depth * cuts, LANES), jnp.float32)],
        ),
        out_shape=jax.ShapeDtypeStruct((items, kinds, depth, KVR), spread_parts[0].dtype),
        compiler_params=pltpu.CompilerParams(vmem_limit_bytes=VMEM_LIMIT),
        name="assemble",
    )(me.reshape(1), *spread_parts)


def absorb(me, items, parts, matrices, outs, shapes):
    t_ways = len(parts)
    blocks = parts[0].shape[0]
    q_rows, o_rows = shapes[0].shape[3], shapes[1].shape[3]
    rows = q_rows + o_rows

    def kernel(at, *refs):
        parts, mats = refs[:t_ways], refs[t_ways]
        q_out, o_out = refs[-2:]
        for d in range(t_ways):
            t = lax.rem(at[0] - d + t_ways, t_ways)
            for f in range(blocks):
                q_out[0, f, t] = jnp.dot(
                    parts[d][f, 0, :q_rows], mats[0, 0], preferred_element_type=jnp.float32
                ).astype(jnp.bfloat16)
                o_out[0, f, t] = jnp.dot(
                    parts[d][f, 0, q_rows:], mats[0, 1], preferred_element_type=jnp.float32
                ).astype(jnp.bfloat16)

    in_specs = [pl.BlockSpec((blocks, 1, rows, LANES), lambda j, at: (0, j, 0, 0))] * t_ways
    in_specs += [pl.BlockSpec((1,) + matrices.shape[1:], lambda j, at: (items[0] + j, 0, 0, 0))]
    args = [*parts, matrices]
    aliases = {}
    if outs is not None:
        in_specs += [pl.BlockSpec(memory_space=pl.ANY)] * 2
        aliases = {1 + len(args): 0, 2 + len(args): 1}
        args += list(outs)
    work = t_ways * blocks * len(items) * rows
    return pl.pallas_call(
        kernel,
        grid_spec=pltpu.PrefetchScalarGridSpec(
            num_scalar_prefetch=1,
            grid=(len(items),),
            in_specs=in_specs,
            out_specs=[
                pl.BlockSpec((1,) + shape.shape[1:], lambda j, at: (items[0] + j, 0, 0, 0, 0))
                for shape in shapes
            ],
        ),
        out_shape=shapes,
        input_output_aliases=aliases,
        compiler_params=pltpu.CompilerParams(vmem_limit_bytes=VMEM_LIMIT),
        cost_estimate=pl.CostEstimate(
            flops=2 * work * LANES * KVR,
            transcendentals=0,
            bytes_accessed=2 * work * (LANES + KVR),
        ),
        name="absorb",
    )(me.reshape(1), *args)


def absorb_plain(me, parts, matrices):
    t_ways = len(parts)
    order = lax.rem(me - jnp.arange(t_ways, dtype=jnp.int32) + t_ways, jnp.int32(t_ways))
    rows = jnp.take(jnp.stack(parts), order, axis=0).transpose(2, 1, 0, 3, 4)
    cut = rows.shape[3] * QR // (QR + D)
    return tuple(
        jnp.einsum("hrc,hck->hrk", part, mats, preferred_element_type=jnp.float32).astype(jnp.bfloat16)
        for part, mats in (
            (rows[:, :, :, :cut].reshape(rows.shape[0], -1, LANES), matrices[:, 0]),
            (rows[:, :, :, cut:].reshape(rows.shape[0], -1, LANES), matrices[:, 1]),
        )
    )


def per_device(learner_flat, param_offsets, owner_map, slice_map):
    f_ways, t_ways = lax.axis_size("fsdp"), lax.axis_size("tp")
    layer_count = learner_flat.shape[0]
    per_group = owner_map.shape[1] // f_ways
    item_count = layer_count * per_group
    widths = piece_widths(f_ways * t_ways)
    granule = functools.reduce(math.gcd, widths)
    table = learner_flat.reshape(layer_count, -1, granule // LANES, LANES)
    whole_tiles = granule % (16 * LANES) == 0
    row_counts = [width // LANES for width in widths]
    item_rows = row_counts[QUERY] + row_counts[OUT]
    ahead = (item_count, 2, row_counts[KEY])

    me = lax.axis_index("tp")
    blocks = f_ways // t_ways
    cuts = [item_count * eighths // 8 for eighths in CUTS]
    chunks = [range(low, high) for low, high in zip(cuts, cuts[1:]) if low < high]

    def over_fsdp(x):
        x = lax.all_to_all(x, "fsdp", split_axis=0, concat_axis=0, tiled=True)
        return x.reshape(f_ways, -1, LANES)

    groups = [chunks[low:high] for low, high in zip(GROUPS, GROUPS[1:]) if chunks[low:high]]
    to_send = pack(
        table,
        param_offsets,
        owner_map,
        f_ways,
        widths,
        granule,
        [
            ([] if at else [(range(item_count), (KEY, VALUE))])
            + [(items, (QUERY, OUT)) for items in group]
            for at, group in enumerate(groups)
        ],
    )

    exchanged, sent = [], []
    for at in range(len(chunks)):
        group = [at in range(low, high) for low, high in zip(GROUPS, GROUPS[1:])].index(True)
        if at == GROUPS[group]:
            rows, first = over_fsdp(to_send[group]), 0 if at else math.prod(ahead)
        waits = sent[at - 1][:1] if at else []
        if at >= 2:
            waits = waits + exchanged[at - 2][1:]
        if t_ways == 4 and at == 1:
            waits = waits + [near, passed]
        pieces = list(
            cut(
                rows,
                slice_map,
                blocks,
                () if at else ahead,
                first,
                len(chunks[at]),
                item_rows,
                waits,
                CUT_MICROS,
            )
        )
        first += len(chunks[at]) * item_rows
        if at == 0:
            pairs = pieces.pop(0)
            up, down = neighbours(pairs, "tp", t_ways)
            if t_ways == 4:
                across = lax.ppermute(pairs, "tp", [(0, 2), (3, 1)])
                near = token([up, down, across], TOKEN_MICROS)
                passed = pass_on(me, across, up, down, [])
                far = lax.ppermute(passed, "tp", [(1, 0), (2, 3)])
        sent.append(pieces)
        exchanged.append(
            pieces[:1]
            + [
                lax.ppermute(piece, "tp", [(i, (i + shift) % t_ways) for i in range(t_ways)])
                for shift, piece in enumerate(pieces)
                if shift
            ]
        )

    if t_ways == 4:
        ends = jnp.logical_or(me == 0, me == 3)
        spread = [
            pairs,
            jnp.where(me == 0, far[0], up),
            jnp.where(ends, far[1], across),
            jnp.where(me == 3, far[0], down),
        ]
    else:
        ups, downs = [pairs, up], [pairs, down]
        for _ in range(2, t_ways):
            ups.append(neighbours(ups[-1], "tp", t_ways)[0])
            downs.append(neighbours(downs[-1], "tp", t_ways)[1])
        spread = [pairs] + [jnp.where(me >= d, ups[d], downs[t_ways - d]) for d in range(1, t_ways)]

    if whole_tiles:
        shapes = tuple(
            jax.ShapeDtypeStruct((item_count, blocks, t_ways, row_counts[kind], KVR), jnp.bfloat16)
            for kind in (QUERY, OUT)
        )
        matrices = assemble(me, spread)
        outs = None
        for items, parts in zip(chunks, exchanged):
            outs = absorb(me, items, parts, matrices, outs, shapes)
        return tuple(out.reshape(layer_count, per_group, -1, KVR) for out in outs)

    order = lax.rem(me - jnp.arange(t_ways, dtype=jnp.int32) + t_ways, jnp.int32(t_ways))
    matrices = jnp.take(jnp.stack(spread), order, axis=0).transpose(2, 3, 1, 0, 4, 5)
    matrices = matrices.reshape(item_count, 2, -1, KVR)
    done = [
        absorb_plain(me, parts, matrices[items[0] : items[-1] + 1])
        for items, parts in zip(chunks, exchanged)
    ]
    return tuple(jnp.concatenate(kind).reshape(layer_count, per_group, -1, KVR) for kind in zip(*done))


def solution(mesh):
    placed = (P(None, ("fsdp", "tp")), P(), P(), P())
    return jax.shard_map(
        per_device,
        mesh=mesh,
        in_specs=placed,
        out_specs=(P(None, "fsdp", "tp", None), P(None, "fsdp", "tp", None)),
        check_vma=False,
    )
```

```python
import functools
import math

import jax
import jax.numpy as jnp
from jax import lax
from jax.experimental import pallas as pl
from jax.experimental.pallas import tpu as pltpu
from jax.sharding import PartitionSpec as P

D = 7168
QR = 1536
KVR = 512
QK_NOPE = 128
V_DIM = 128
LANES = 128
QUERY, KEY, VALUE, OUT = range(4)
CUT_MICROS = 30
TOKEN_MICROS = 40
CUTS = (0, 2, 5, 8)
VMEM_LIMIT = 16 * 1024 * 1024


def piece_widths(rank_total):
    return (
        QR * QK_NOPE // rank_total,
        QK_NOPE * KVR // rank_total,
        V_DIM * KVR // rank_total,
        D * V_DIM // rank_total,
    )


def pack(table, param_offsets, owner_map, ways, widths, granule, parts):
    layer_count, head_count = owner_map.shape
    per_group = head_count // ways
    sizes = [width // granule for width in widths]
    outs = [
        jax.ShapeDtypeStruct(
            (ways, sum(len(items) * sum(sizes[kind] for kind in kinds) for items, kinds in part))
            + table.shape[2:],
            table.dtype,
        )
        for part in parts
    ]

    def kernel(offsets, owners, source, *refs):
        targets, (taken, head_at) = refs[:-2], refs[-2:]
        for layer in sorted({item // per_group for part in parts for items, _ in part for item in items}):
            for way in range(ways):
                taken[way] = layer * per_group

            def place(head):
                way = owners[layer, head]
                item = taken[way]
                taken[way] = item + 1
                head_at[item * ways + way] = head

            pl.loop(0, head_count, unroll=min(8, head_count))(place)

        for target, part in zip(targets, parts):
            start = 0
            for item, kinds in [(item, kinds) for items, kinds in part for item in items]:

                def move(way):
                    head = head_at[item * ways + way]
                    at = start
                    for kind in kinds:
                        begin = lax.div(offsets[item // per_group, head, kind], jnp.int32(granule))
                        target[way, pl.ds(at, sizes[kind])] = source[
                            item // per_group, pl.ds(begin, sizes[kind])
                        ]
                        at += sizes[kind]

                pl.loop(0, ways, unroll=min(8, ways))(move)
                start += sum(sizes[kind] for kind in kinds)

    return pl.pallas_call(
        kernel,
        out_shape=outs,
        in_specs=[
            pl.BlockSpec(memory_space=pltpu.SMEM),
            pl.BlockSpec(memory_space=pltpu.SMEM),
            pl.BlockSpec(memory_space=pltpu.VMEM),
        ],
        out_specs=[pl.BlockSpec(memory_space=pltpu.VMEM)] * len(outs),
        scratch_shapes=[
            pltpu.SMEM((ways,), jnp.int32),
            pltpu.SMEM((layer_count * head_count,), jnp.int32),
        ],
        compiler_params=pltpu.CompilerParams(vmem_limit_bytes=VMEM_LIMIT),
        cost_estimate=pl.CostEstimate(
            flops=0,
            transcendentals=0,
            bytes_accessed=sum(2 * 2 * math.prod(out.shape) for out in outs),
        ),
        name="pack",
    )(param_offsets, owner_map, table)


def corner_of(x):
    return (1,) * (x.ndim - 2) + (min(16, x.shape[-2]), LANES)


def corner(x):
    return pl.BlockSpec(corner_of(x), lambda _: (0,) * x.ndim)


def cut(rows, slice_map, blocks, first, items, item_rows, waits, micros):
    t_ways = slice_map.shape[1]
    shapes = [(blocks, items, item_rows) + rows.shape[2:]] * t_ways

    def kernel(mapped, source, *refs):
        f_me, t_me = lax.axis_index("fsdp"), lax.axis_index("tp")
        for shift, piece in enumerate(refs[len(waits) :]):
            block = mapped[f_me, lax.rem(t_me + shift, t_ways)]
            for f in range(blocks):
                for item in range(items):
                    start = first + item * item_rows
                    piece[f, item] = source[block * blocks + f, start : start + item_rows]

    return pl.pallas_call(
        kernel,
        grid=(1,),
        out_shape=[jax.ShapeDtypeStruct(shape, rows.dtype) for shape in shapes],
        in_specs=[pl.BlockSpec(memory_space=pltpu.SMEM), pl.BlockSpec(memory_space=pltpu.VMEM)]
        + [corner(x) for x in waits],
        out_specs=[pl.BlockSpec(memory_space=pltpu.VMEM)] * len(shapes),
        compiler_params=pltpu.CompilerParams(vmem_limit_bytes=VMEM_LIMIT),
        cost_estimate=pl.CostEstimate(
            flops=int(micros * 1.15e9),
            transcendentals=0,
            bytes_accessed=4 * sum(math.prod(shape) for shape in shapes),
        ),
        name="cut",
    )(slice_map, rows, *waits)


def token(waits, micros):
    def kernel(*refs):
        refs[-1][...] = jnp.zeros(refs[-1].shape, refs[-1].dtype)

    return pl.pallas_call(
        kernel,
        grid=(1,),
        out_shape=jax.ShapeDtypeStruct((16, LANES), jnp.bfloat16),
        in_specs=[corner(x) for x in waits],
        cost_estimate=pl.CostEstimate(
            flops=int(micros * 1.15e9), transcendentals=0, bytes_accessed=0
        ),
        name="token",
    )(*waits)


def neighbours(x, axis, ways):
    return (
        lax.ppermute(x, axis, [(i, i + 1) for i in range(ways - 1)]),
        lax.ppermute(x, axis, [(i + 1, i) for i in range(ways - 1)]),
    )


def pass_on(me, across, up, down, waits):
    def kernel(me_ref, first, above, below, *refs):
        out = refs[-1]
        out[0] = first[...]

        @pl.when(me_ref[0] == 2)
        def _():
            out[1] = above[...]

        @pl.when(me_ref[0] != 2)
        def _():
            out[1] = below[...]

    whole = pl.BlockSpec(across.shape, lambda _, me_ref: (0,) * across.ndim)
    corners = [pl.BlockSpec(corner_of(x), lambda _, me_ref, n=x.ndim: (0,) * n) for x in waits]
    return pl.pallas_call(
        kernel,
        grid_spec=pltpu.PrefetchScalarGridSpec(
            num_scalar_prefetch=1,
            grid=(1,),
            in_specs=[whole] * 3 + corners,
            out_specs=pl.BlockSpec((2,) + across.shape, lambda _, me_ref: (0,) * (across.ndim + 1)),
        ),
        out_shape=jax.ShapeDtypeStruct((2,) + across.shape, across.dtype),
        compiler_params=pltpu.CompilerParams(vmem_limit_bytes=VMEM_LIMIT),
        name="pass_on",
    )(me.reshape(1), across, up, down, *waits)


def join(me, own, up, down, across, far, waits):
    def kernel(me_ref, own_ref, up_ref, down_ref, across_ref, far_ref, *refs):
        out = refs[-1]
        first, last = me_ref[0] == 0, me_ref[0] == 3

        def pick(d, end, far_at, other):
            @pl.when(end)
            def _():
                out[0, d] = far_ref[far_at, 0]

            @pl.when(jnp.logical_not(end))
            def _():
                out[0, d] = other[0]

        out[0, 0] = own_ref[0]
        pick(1, first, 0, up_ref)
        pick(2, jnp.logical_or(first, last), 1, across_ref)
        pick(3, last, 0, down_ref)

    inner = own.shape[1:]
    zeros = (0,) * len(inner)
    one = pl.BlockSpec((1,) + inner, lambda f, me_ref: (f,) + zeros)
    corners = [pl.BlockSpec(corner_of(x), lambda f, me_ref, n=x.ndim: (0,) * n) for x in waits]
    return pl.pallas_call(
        kernel,
        grid_spec=pltpu.PrefetchScalarGridSpec(
            num_scalar_prefetch=1,
            grid=own.shape[:1],
            in_specs=[one] * 4
            + [pl.BlockSpec((2, 1) + inner, lambda f, me_ref: (0, f) + zeros)]
            + corners,
            out_specs=pl.BlockSpec((1, 4) + inner, lambda f, me_ref: (f, 0) + zeros),
        ),
        out_shape=jax.ShapeDtypeStruct(own.shape[:1] + (4,) + inner, own.dtype),
        compiler_params=pltpu.CompilerParams(vmem_limit_bytes=VMEM_LIMIT),
        name="join",
    )(me.reshape(1), own, up, down, across, far, *waits)


def assemble(me, joined, waits):
    f_ways, t_ways, items, kinds, rows, _ = joined.shape
    depth = t_ways * f_ways * rows * LANES // KVR
    cuts = KVR // LANES

    def kernel(me_ref, pieces, *refs):
        out, scratch = refs[-2:]
        for kind in range(kinds):
            for d in range(t_ways):
                t = lax.rem(me_ref[0] - d + t_ways, t_ways)
                for f in range(f_ways):
                    scratch[pl.ds(pl.multiple_of((f * t_ways + t) * rows, rows), rows), :] = pieces[
                        f, d, 0, kind
                    ].astype(jnp.float32)
            for cut in range(cuts):
                out[0, kind, :, pl.ds(cut * LANES, LANES)] = scratch[
                    pl.ds(cut, depth, stride=cuts), :
                ].astype(jnp.bfloat16)

    return pl.pallas_call(
        kernel,
        grid_spec=pltpu.PrefetchScalarGridSpec(
            num_scalar_prefetch=1,
            grid=(items,),
            in_specs=[
                pl.BlockSpec(
                    (f_ways, t_ways, 1, kinds, rows, LANES), lambda i, _: (0, 0, i, 0, 0, 0)
                )
            ]
            + [pl.BlockSpec(corner_of(x), lambda i, _, n=x.ndim: (0,) * n) for x in waits],
            out_specs=pl.BlockSpec((1, kinds, depth, KVR), lambda i, _: (i, 0, 0, 0)),
            scratch_shapes=[pltpu.VMEM((depth * cuts, LANES), jnp.float32)],
        ),
        out_shape=jax.ShapeDtypeStruct((items, kinds, depth, KVR), joined.dtype),
        compiler_params=pltpu.CompilerParams(vmem_limit_bytes=VMEM_LIMIT),
        name="assemble",
    )(me.reshape(1), joined, *waits)


def absorb(me, items, parts, matrices, outs, shapes):
    t_ways = len(parts)
    blocks = parts[0].shape[0]
    q_rows, o_rows = shapes[0].shape[3], shapes[1].shape[3]
    rows = q_rows + o_rows

    def kernel(at, *refs):
        parts, mats = refs[:t_ways], refs[t_ways]
        q_out, o_out = refs[-2:]
        for d in range(t_ways):
            t = lax.rem(at[0] - d + t_ways, t_ways)
            for f in range(blocks):
                q_out[0, f, t] = jnp.dot(
                    parts[d][f, 0, :q_rows], mats[0, 0], preferred_element_type=jnp.float32
                ).astype(jnp.bfloat16)
                o_out[0, f, t] = jnp.dot(
                    parts[d][f, 0, q_rows:], mats[0, 1], preferred_element_type=jnp.float32
                ).astype(jnp.bfloat16)

    in_specs = [pl.BlockSpec((blocks, 1, rows, LANES), lambda j, at: (0, j, 0, 0))] * t_ways
    in_specs += [pl.BlockSpec((1,) + matrices.shape[1:], lambda j, at: (items[0] + j, 0, 0, 0))]
    args = [*parts, matrices]
    aliases = {}
    if outs is not None:
        in_specs += [pl.BlockSpec(memory_space=pl.ANY)] * 2
        aliases = {1 + len(args): 0, 2 + len(args): 1}
        args += list(outs)
    work = t_ways * blocks * len(items) * rows
    return pl.pallas_call(
        kernel,
        grid_spec=pltpu.PrefetchScalarGridSpec(
            num_scalar_prefetch=1,
            grid=(len(items),),
            in_specs=in_specs,
            out_specs=[
                pl.BlockSpec((1,) + shape.shape[1:], lambda j, at: (items[0] + j, 0, 0, 0, 0))
                for shape in shapes
            ],
        ),
        out_shape=shapes,
        input_output_aliases=aliases,
        compiler_params=pltpu.CompilerParams(vmem_limit_bytes=VMEM_LIMIT),
        cost_estimate=pl.CostEstimate(
            flops=2 * work * LANES * KVR,
            transcendentals=0,
            bytes_accessed=2 * work * (LANES + KVR),
        ),
        name="absorb",
    )(me.reshape(1), *args)


def absorb_plain(me, parts, matrices):
    t_ways = len(parts)
    order = lax.rem(me - jnp.arange(t_ways, dtype=jnp.int32) + t_ways, jnp.int32(t_ways))
    rows = jnp.take(jnp.stack(parts), order, axis=0).transpose(2, 1, 0, 3, 4)
    cut = rows.shape[3] * QR // (QR + D)
    return tuple(
        jnp.einsum("hrc,hck->hrk", part, mats, preferred_element_type=jnp.float32).astype(jnp.bfloat16)
        for part, mats in (
            (rows[:, :, :, :cut].reshape(rows.shape[0], -1, LANES), matrices[:, 0]),
            (rows[:, :, :, cut:].reshape(rows.shape[0], -1, LANES), matrices[:, 1]),
        )
    )


def per_device(learner_flat, param_offsets, owner_map, slice_map):
    f_ways, t_ways = lax.axis_size("fsdp"), lax.axis_size("tp")
    layer_count = learner_flat.shape[0]
    per_group = owner_map.shape[1] // f_ways
    item_count = layer_count * per_group
    widths = piece_widths(f_ways * t_ways)
    granule = functools.reduce(math.gcd, widths)
    table = learner_flat.reshape(layer_count, -1, granule // LANES, LANES)
    whole_tiles = granule % (16 * LANES) == 0
    row_counts = [width // LANES for width in widths]
    item_rows = row_counts[QUERY] + row_counts[OUT]

    me = lax.axis_index("tp")
    blocks = f_ways // t_ways
    cuts = [item_count * eighths // 8 for eighths in CUTS]
    chunks = [range(low, high) for low, high in zip(cuts, cuts[1:]) if low < high]

    def over_fsdp(x):
        x = lax.all_to_all(x, "fsdp", split_axis=0, concat_axis=0, tiled=True)
        return x.reshape(f_ways, -1, LANES)

    pairs, *to_send = pack(
        table,
        param_offsets,
        owner_map,
        f_ways,
        widths,
        granule,
        [[(range(item_count), (KEY, VALUE))]] + [[(items, (QUERY, OUT))] for items in chunks],
    )
    pairs = pairs.reshape(f_ways, item_count, 2, row_counts[KEY], LANES)
    up, down = neighbours(pairs, "tp", t_ways)
    if t_ways == 4:
        across = lax.ppermute(pairs, "tp", [(0, 2), (3, 1)])
        near = token([up, down, across], TOKEN_MICROS)
        passed = pass_on(me, across, up, down, [])
        far = lax.ppermute(passed, "tp", [(1, 0), (2, 3)])

    exchanged, sent = [], []
    for at, items in enumerate(chunks):
        rows = over_fsdp(to_send[at])
        waits = sent[at - 1][:1] if at else []
        if at >= 2:
            waits = waits + exchanged[at - 2][1:]
        if t_ways == 4:
            waits = waits + [[near], [passed], [far]][min(at, 2)]
        pieces = list(
            cut(rows, slice_map, blocks, 0, len(items), item_rows, waits, CUT_MICROS)
        )
        sent.append(pieces)
        exchanged.append(
            pieces[:1]
            + [
                lax.ppermute(piece, "tp", [(i, (i + shift) % t_ways) for i in range(t_ways)])
                for shift, piece in enumerate(pieces)
                if shift
            ]
        )

    if t_ways == 4:
        joined = join(me, pairs, up, down, across, far, sent[-1][:1])
    else:
        ups, downs = [pairs, up], [pairs, down]
        for _ in range(2, t_ways):
            ups.append(neighbours(ups[-1], "tp", t_ways)[0])
            downs.append(neighbours(downs[-1], "tp", t_ways)[1])
        joined = jnp.stack(
            [pairs] + [jnp.where(me >= d, ups[d], downs[t_ways - d]) for d in range(1, t_ways)], axis=1
        )
    joined = over_fsdp(joined).reshape(joined.shape)

    if whole_tiles:
        shapes = tuple(
            jax.ShapeDtypeStruct((item_count, blocks, t_ways, row_counts[kind], KVR), jnp.bfloat16)
            for kind in (QUERY, OUT)
        )
        matrices = assemble(me, joined, [token(exchanged[-2][1:], TOKEN_MICROS)])
        outs = None
        for items, parts in zip(chunks, exchanged):
            outs = absorb(me, items, parts, matrices, outs, shapes)
        return tuple(out.reshape(layer_count, per_group, -1, KVR) for out in outs)

    order = lax.rem(me - jnp.arange(t_ways, dtype=jnp.int32) + t_ways, jnp.int32(t_ways))
    matrices = jnp.take(joined, order, axis=1).transpose(2, 3, 0, 1, 4, 5)
    matrices = matrices.reshape(item_count, 2, -1, KVR)
    done = [
        absorb_plain(me, parts, matrices[items[0] : items[-1] + 1])
        for items, parts in zip(chunks, exchanged)
    ]
    return tuple(jnp.concatenate(kind).reshape(layer_count, per_group, -1, KVR) for kind in zip(*done))


def solution(mesh):
    placed = (P(None, ("fsdp", "tp")), P(), P(), P())
    return jax.shard_map(
        per_device,
        mesh=mesh,
        in_specs=placed,
        out_specs=(P(None, "fsdp", "tp", None), P(None, "fsdp", "tp", None)),
        check_vma=False,
    )
```

```python
import functools
import math

import jax
import jax.numpy as jnp
from jax import lax
from jax.experimental import pallas as pl
from jax.experimental.pallas import tpu as pltpu
from jax.sharding import PartitionSpec as P

D = 7168
QR = 1536
KVR = 512
QK_NOPE = 128
V_DIM = 128
LANES = 128
QUERY, KEY, VALUE, OUT = range(4)
CUT_MICROS = 30
TOKEN_MICROS = 40
CUTS = (0, 2, 5, 8)
VMEM_LIMIT = 16 * 1024 * 1024


def piece_widths(rank_total):
    return (
        QR * QK_NOPE // rank_total,
        QK_NOPE * KVR // rank_total,
        V_DIM * KVR // rank_total,
        D * V_DIM // rank_total,
    )


def pack(table, param_offsets, owner_map, ways, widths, granule, parts):
    layer_count, head_count = owner_map.shape
    per_group = head_count // ways
    sizes = [width // granule for width in widths]
    outs = [
        jax.ShapeDtypeStruct(
            (ways, sum(len(items) * sum(sizes[kind] for kind in kinds) for items, kinds in part))
            + table.shape[2:],
            table.dtype,
        )
        for part in parts
    ]

    def kernel(offsets, owners, source, *refs):
        targets, (taken, head_at) = refs[:-2], refs[-2:]
        for layer in sorted({item // per_group for part in parts for items, _ in part for item in items}):
            for way in range(ways):
                taken[way] = layer * per_group

            def place(head):
                way = owners[layer, head]
                item = taken[way]
                taken[way] = item + 1
                head_at[item * ways + way] = head

            pl.loop(0, head_count, unroll=min(8, head_count))(place)

        for target, part in zip(targets, parts):
            start = 0
            for item, kinds in [(item, kinds) for items, kinds in part for item in items]:

                def move(way):
                    head = head_at[item * ways + way]
                    at = start
                    for kind in kinds:
                        begin = lax.div(offsets[item // per_group, head, kind], jnp.int32(granule))
                        target[way, pl.ds(at, sizes[kind])] = source[
                            item // per_group, pl.ds(begin, sizes[kind])
                        ]
                        at += sizes[kind]

                pl.loop(0, ways, unroll=min(8, ways))(move)
                start += sum(sizes[kind] for kind in kinds)

    return pl.pallas_call(
        kernel,
        out_shape=outs,
        in_specs=[
            pl.BlockSpec(memory_space=pltpu.SMEM),
            pl.BlockSpec(memory_space=pltpu.SMEM),
            pl.BlockSpec(memory_space=pltpu.VMEM),
        ],
        out_specs=[pl.BlockSpec(memory_space=pltpu.VMEM)] * len(outs),
        scratch_shapes=[
            pltpu.SMEM((ways,), jnp.int32),
            pltpu.SMEM((layer_count * head_count,), jnp.int32),
        ],
        compiler_params=pltpu.CompilerParams(vmem_limit_bytes=VMEM_LIMIT),
        cost_estimate=pl.CostEstimate(
            flops=0,
            transcendentals=0,
            bytes_accessed=sum(2 * 2 * math.prod(out.shape) for out in outs),
        ),
        name="pack",
    )(param_offsets, owner_map, table)


def corner_of(x):
    return (1,) * (x.ndim - 2) + (min(16, x.shape[-2]), LANES)


def corner(x):
    return pl.BlockSpec(corner_of(x), lambda _: (0,) * x.ndim)


def cut(rows, slice_map, blocks, first, items, item_rows, waits, micros):
    t_ways = slice_map.shape[1]
    shapes = [(blocks, items, item_rows) + rows.shape[2:]] * t_ways

    def kernel(mapped, source, *refs):
        f_me, t_me = lax.axis_index("fsdp"), lax.axis_index("tp")
        for shift, piece in enumerate(refs[len(waits) :]):
            block = mapped[f_me, lax.rem(t_me + shift, t_ways)]
            for f in range(blocks):
                for item in range(items):
                    start = first + item * item_rows
                    piece[f, item] = source[block * blocks + f, start : start + item_rows]

    return pl.pallas_call(
        kernel,
        grid=(1,),
        out_shape=[jax.ShapeDtypeStruct(shape, rows.dtype) for shape in shapes],
        in_specs=[pl.BlockSpec(memory_space=pltpu.SMEM), pl.BlockSpec(memory_space=pltpu.VMEM)]
        + [corner(x) for x in waits],
        out_specs=[pl.BlockSpec(memory_space=pltpu.VMEM)] * len(shapes),
        compiler_params=pltpu.CompilerParams(vmem_limit_bytes=VMEM_LIMIT),
        cost_estimate=pl.CostEstimate(
            flops=int(micros * 1.15e9),
            transcendentals=0,
            bytes_accessed=4 * sum(math.prod(shape) for shape in shapes),
        ),
        name="cut",
    )(slice_map, rows, *waits)


def token(waits, micros):
    def kernel(*refs):
        refs[-1][...] = jnp.zeros(refs[-1].shape, refs[-1].dtype)

    return pl.pallas_call(
        kernel,
        grid=(1,),
        out_shape=jax.ShapeDtypeStruct((16, LANES), jnp.bfloat16),
        in_specs=[corner(x) for x in waits],
        cost_estimate=pl.CostEstimate(
            flops=int(micros * 1.15e9), transcendentals=0, bytes_accessed=0
        ),
        name="token",
    )(*waits)


def neighbours(x, axis, ways):
    return (
        lax.ppermute(x, axis, [(i, i + 1) for i in range(ways - 1)]),
        lax.ppermute(x, axis, [(i + 1, i) for i in range(ways - 1)]),
    )


def pass_on(me, across, up, down, waits):
    def kernel(me_ref, first, above, below, *refs):
        out = refs[-1]
        out[0] = first[...]

        @pl.when(me_ref[0] == 2)
        def _():
            out[1] = above[...]

        @pl.when(me_ref[0] != 2)
        def _():
            out[1] = below[...]

    whole = pl.BlockSpec(across.shape, lambda _, me_ref: (0,) * across.ndim)
    corners = [pl.BlockSpec(corner_of(x), lambda _, me_ref, n=x.ndim: (0,) * n) for x in waits]
    return pl.pallas_call(
        kernel,
        grid_spec=pltpu.PrefetchScalarGridSpec(
            num_scalar_prefetch=1,
            grid=(1,),
            in_specs=[whole] * 3 + corners,
            out_specs=pl.BlockSpec((2,) + across.shape, lambda _, me_ref: (0,) * (across.ndim + 1)),
        ),
        out_shape=jax.ShapeDtypeStruct((2,) + across.shape, across.dtype),
        compiler_params=pltpu.CompilerParams(vmem_limit_bytes=VMEM_LIMIT),
        name="pass_on",
    )(me.reshape(1), across, up, down, *waits)


def join(me, own, up, down, across, far, waits):
    def kernel(me_ref, own_ref, up_ref, down_ref, across_ref, far_ref, *refs):
        out = refs[-1]
        first, last = me_ref[0] == 0, me_ref[0] == 3

        def pick(d, end, far_at, other):
            @pl.when(end)
            def _():
                out[:, d] = far_ref[far_at]

            @pl.when(jnp.logical_not(end))
            def _():
                out[:, d] = other[...]

        out[:, 0] = own_ref[...]
        pick(1, first, 0, up_ref)
        pick(2, jnp.logical_or(first, last), 1, across_ref)
        pick(3, last, 0, down_ref)

    inner = own.shape[1:]
    step = max(1, own.shape[0] // 2)
    zeros = (0,) * len(inner)
    one = pl.BlockSpec((step,) + inner, lambda f, me_ref: (f,) + zeros)
    corners = [pl.BlockSpec(corner_of(x), lambda f, me_ref, n=x.ndim: (0,) * n) for x in waits]
    return pl.pallas_call(
        kernel,
        grid_spec=pltpu.PrefetchScalarGridSpec(
            num_scalar_prefetch=1,
            grid=(own.shape[0] // step,),
            in_specs=[one] * 4
            + [pl.BlockSpec((2, step) + inner, lambda f, me_ref: (0, f) + zeros)]
            + corners,
            out_specs=pl.BlockSpec((step, 4) + inner, lambda f, me_ref: (f, 0) + zeros),
        ),
        out_shape=jax.ShapeDtypeStruct(own.shape[:1] + (4,) + inner, own.dtype),
        compiler_params=pltpu.CompilerParams(vmem_limit_bytes=VMEM_LIMIT),
        name="join",
    )(me.reshape(1), own, up, down, across, far, *waits)


def assemble(me, joined, waits):
    f_ways, t_ways, items, kinds, rows, _ = joined.shape
    depth = t_ways * f_ways * rows * LANES // KVR
    cuts = KVR // LANES

    def kernel(me_ref, pieces, *refs):
        out, scratch = refs[-2:]
        for kind in range(kinds):
            for d in range(t_ways):
                t = lax.rem(me_ref[0] - d + t_ways, t_ways)
                for f in range(f_ways):
                    scratch[pl.ds(pl.multiple_of((f * t_ways + t) * rows, rows), rows), :] = pieces[
                        f, d, 0, kind
                    ].astype(jnp.float32)
            for cut in range(cuts):
                out[0, kind, :, pl.ds(cut * LANES, LANES)] = scratch[
                    pl.ds(cut, depth, stride=cuts), :
                ].astype(jnp.bfloat16)

    return pl.pallas_call(
        kernel,
        grid_spec=pltpu.PrefetchScalarGridSpec(
            num_scalar_prefetch=1,
            grid=(items,),
            in_specs=[
                pl.BlockSpec(
                    (f_ways, t_ways, 1, kinds, rows, LANES), lambda i, _: (0, 0, i, 0, 0, 0)
                )
            ]
            + [pl.BlockSpec(corner_of(x), lambda i, _, n=x.ndim: (0,) * n) for x in waits],
            out_specs=pl.BlockSpec((1, kinds, depth, KVR), lambda i, _: (i, 0, 0, 0)),
            scratch_shapes=[pltpu.VMEM((depth * cuts, LANES), jnp.float32)],
        ),
        out_shape=jax.ShapeDtypeStruct((items, kinds, depth, KVR), joined.dtype),
        compiler_params=pltpu.CompilerParams(vmem_limit_bytes=VMEM_LIMIT),
        name="assemble",
    )(me.reshape(1), joined, *waits)


def absorb(me, items, parts, matrices, outs, shapes):
    t_ways = len(parts)
    blocks = parts[0].shape[0]
    q_rows, o_rows = shapes[0].shape[3], shapes[1].shape[3]
    rows = q_rows + o_rows

    def kernel(at, *refs):
        parts, mats = refs[:t_ways], refs[t_ways]
        q_out, o_out = refs[-2:]
        for d in range(t_ways):
            t = lax.rem(at[0] - d + t_ways, t_ways)
            for f in range(blocks):
                q_out[0, f, t] = jnp.dot(
                    parts[d][f, 0, :q_rows], mats[0, 0], preferred_element_type=jnp.float32
                ).astype(jnp.bfloat16)
                o_out[0, f, t] = jnp.dot(
                    parts[d][f, 0, q_rows:], mats[0, 1], preferred_element_type=jnp.float32
                ).astype(jnp.bfloat16)

    in_specs = [pl.BlockSpec((blocks, 1, rows, LANES), lambda j, at: (0, j, 0, 0))] * t_ways
    in_specs += [pl.BlockSpec((1,) + matrices.shape[1:], lambda j, at: (items[0] + j, 0, 0, 0))]
    args = [*parts, matrices]
    aliases = {}
    if outs is not None:
        in_specs += [pl.BlockSpec(memory_space=pl.ANY)] * 2
        aliases = {1 + len(args): 0, 2 + len(args): 1}
        args += list(outs)
    work = t_ways * blocks * len(items) * rows
    return pl.pallas_call(
        kernel,
        grid_spec=pltpu.PrefetchScalarGridSpec(
            num_scalar_prefetch=1,
            grid=(len(items),),
            in_specs=in_specs,
            out_specs=[
                pl.BlockSpec((1,) + shape.shape[1:], lambda j, at: (items[0] + j, 0, 0, 0, 0))
                for shape in shapes
            ],
        ),
        out_shape=shapes,
        input_output_aliases=aliases,
        compiler_params=pltpu.CompilerParams(vmem_limit_bytes=VMEM_LIMIT),
        cost_estimate=pl.CostEstimate(
            flops=2 * work * LANES * KVR,
            transcendentals=0,
            bytes_accessed=2 * work * (LANES + KVR),
        ),
        name="absorb",
    )(me.reshape(1), *args)


def absorb_plain(me, parts, matrices):
    t_ways = len(parts)
    order = lax.rem(me - jnp.arange(t_ways, dtype=jnp.int32) + t_ways, jnp.int32(t_ways))
    rows = jnp.take(jnp.stack(parts), order, axis=0).transpose(2, 1, 0, 3, 4)
    cut = rows.shape[3] * QR // (QR + D)
    return tuple(
        jnp.einsum("hrc,hck->hrk", part, mats, preferred_element_type=jnp.float32).astype(jnp.bfloat16)
        for part, mats in (
            (rows[:, :, :, :cut].reshape(rows.shape[0], -1, LANES), matrices[:, 0]),
            (rows[:, :, :, cut:].reshape(rows.shape[0], -1, LANES), matrices[:, 1]),
        )
    )


def per_device(learner_flat, param_offsets, owner_map, slice_map):
    f_ways, t_ways = lax.axis_size("fsdp"), lax.axis_size("tp")
    layer_count = learner_flat.shape[0]
    per_group = owner_map.shape[1] // f_ways
    item_count = layer_count * per_group
    widths = piece_widths(f_ways * t_ways)
    granule = functools.reduce(math.gcd, widths)
    table = learner_flat.reshape(layer_count, -1, granule // LANES, LANES)
    whole_tiles = granule % (16 * LANES) == 0
    row_counts = [width // LANES for width in widths]
    item_rows = row_counts[QUERY] + row_counts[OUT]

    me = lax.axis_index("tp")
    blocks = f_ways // t_ways
    cuts = [item_count * eighths // 8 for eighths in CUTS]
    chunks = [range(low, high) for low, high in zip(cuts, cuts[1:]) if low < high]

    def over_fsdp(x):
        x = lax.all_to_all(x, "fsdp", split_axis=0, concat_axis=0, tiled=True)
        return x.reshape(f_ways, -1, LANES)

    pairs, *to_send = pack(
        table,
        param_offsets,
        owner_map,
        f_ways,
        widths,
        granule,
        [[(range(item_count), (KEY, VALUE))]] + [[(items, (QUERY, OUT))] for items in chunks],
    )
    pairs = pairs.reshape(f_ways, item_count, 2, row_counts[KEY], LANES)
    up, down = neighbours(pairs, "tp", t_ways)
    if t_ways == 4:
        across = lax.ppermute(pairs, "tp", [(0, 2), (3, 1)])

    exchanged, sent = [], []
    for at, items in enumerate(chunks):
        rows = over_fsdp(to_send[at])
        waits = sent[at - 1][:1] if at else []
        if at >= 2:
            waits = waits + exchanged[at - 2][1:]
        if t_ways == 4 and at:
            waits = waits + ([passed] if at == 1 else [far])
        pieces = list(
            cut(rows, slice_map, blocks, 0, len(items), item_rows, waits, CUT_MICROS)
        )
        sent.append(pieces)
        if t_ways == 4 and at == 0:
            passed = pass_on(me, across, up, down, pieces[:1])
            far = lax.ppermute(passed, "tp", [(1, 0), (2, 3)])
        exchanged.append(
            pieces[:1]
            + [
                lax.ppermute(piece, "tp", [(i, (i + shift) % t_ways) for i in range(t_ways)])
                for shift, piece in enumerate(pieces)
                if shift
            ]
        )

    if t_ways == 4:
        joined = join(me, pairs, up, down, across, far, sent[-1][:1])
    else:
        ups, downs = [pairs, up], [pairs, down]
        for _ in range(2, t_ways):
            ups.append(neighbours(ups[-1], "tp", t_ways)[0])
            downs.append(neighbours(downs[-1], "tp", t_ways)[1])
        joined = jnp.stack(
            [pairs] + [jnp.where(me >= d, ups[d], downs[t_ways - d]) for d in range(1, t_ways)], axis=1
        )
    joined = over_fsdp(joined).reshape(joined.shape)

    if whole_tiles:
        shapes = tuple(
            jax.ShapeDtypeStruct((item_count, blocks, t_ways, row_counts[kind], KVR), jnp.bfloat16)
            for kind in (QUERY, OUT)
        )
        matrices = assemble(me, joined, [token(exchanged[-2][1:], TOKEN_MICROS)])
        outs = None
        for items, parts in zip(chunks, exchanged):
            outs = absorb(me, items, parts, matrices, outs, shapes)
        return tuple(out.reshape(layer_count, per_group, -1, KVR) for out in outs)

    order = lax.rem(me - jnp.arange(t_ways, dtype=jnp.int32) + t_ways, jnp.int32(t_ways))
    matrices = jnp.take(joined, order, axis=1).transpose(2, 3, 0, 1, 4, 5)
    matrices = matrices.reshape(item_count, 2, -1, KVR)
    done = [
        absorb_plain(me, parts, matrices[items[0] : items[-1] + 1])
        for items, parts in zip(chunks, exchanged)
    ]
    return tuple(jnp.concatenate(kind).reshape(layer_count, per_group, -1, KVR) for kind in zip(*done))


def solution(mesh):
    placed = (P(None, ("fsdp", "tp")), P(), P(), P())
    return jax.shard_map(
        per_device,
        mesh=mesh,
        in_specs=placed,
        out_specs=(P(None, "fsdp", "tp", None), P(None, "fsdp", "tp", None)),
        check_vma=False,
    )
```

```python
import functools
import math

import jax
import jax.numpy as jnp
from jax import lax
from jax.experimental import pallas as pl
from jax.experimental.pallas import tpu as pltpu
from jax.sharding import PartitionSpec as P

D = 7168
QR = 1536
KVR = 512
QK_NOPE = 128
V_DIM = 128
LANES = 128
QUERY, KEY, VALUE, OUT = range(4)
CUT_MICROS = 30
TOKEN_MICROS = 80
CUTS = (0, 2, 5, 8)
VMEM_LIMIT = 16 * 1024 * 1024


def piece_widths(rank_total):
    return (
        QR * QK_NOPE // rank_total,
        QK_NOPE * KVR // rank_total,
        V_DIM * KVR // rank_total,
        D * V_DIM // rank_total,
    )


def pack(table, param_offsets, owner_map, ways, widths, granule, parts):
    layer_count, head_count = owner_map.shape
    per_group = head_count // ways
    sizes = [width // granule for width in widths]
    outs = [
        jax.ShapeDtypeStruct(
            (ways, sum(len(items) * sum(sizes[kind] for kind in kinds) for items, kinds in part))
            + table.shape[2:],
            table.dtype,
        )
        for part in parts
    ]

    def kernel(offsets, owners, source, *refs):
        targets, (taken, head_at) = refs[:-2], refs[-2:]
        for layer in sorted({item // per_group for part in parts for items, _ in part for item in items}):
            for way in range(ways):
                taken[way] = layer * per_group

            def place(head):
                way = owners[layer, head]
                item = taken[way]
                taken[way] = item + 1
                head_at[item * ways + way] = head

            pl.loop(0, head_count, unroll=min(8, head_count))(place)

        for target, part in zip(targets, parts):
            start = 0
            for item, kinds in [(item, kinds) for items, kinds in part for item in items]:

                def move(way):
                    head = head_at[item * ways + way]
                    at = start
                    for kind in kinds:
                        begin = lax.div(offsets[item // per_group, head, kind], jnp.int32(granule))
                        target[way, pl.ds(at, sizes[kind])] = source[
                            item // per_group, pl.ds(begin, sizes[kind])
                        ]
                        at += sizes[kind]

                pl.loop(0, ways, unroll=min(8, ways))(move)
                start += sum(sizes[kind] for kind in kinds)

    return pl.pallas_call(
        kernel,
        out_shape=outs,
        in_specs=[
            pl.BlockSpec(memory_space=pltpu.SMEM),
            pl.BlockSpec(memory_space=pltpu.SMEM),
            pl.BlockSpec(memory_space=pltpu.VMEM),
        ],
        out_specs=[pl.BlockSpec(memory_space=pltpu.VMEM)] * len(outs),
        scratch_shapes=[
            pltpu.SMEM((ways,), jnp.int32),
            pltpu.SMEM((layer_count * head_count,), jnp.int32),
        ],
        compiler_params=pltpu.CompilerParams(vmem_limit_bytes=VMEM_LIMIT),
        cost_estimate=pl.CostEstimate(
            flops=0,
            transcendentals=0,
            bytes_accessed=sum(2 * 2 * math.prod(out.shape) for out in outs),
        ),
        name="pack",
    )(param_offsets, owner_map, table)


def corner_of(x):
    return (1,) * (x.ndim - 2) + (min(16, x.shape[-2]), LANES)


def corner(x):
    return pl.BlockSpec(corner_of(x), lambda _: (0,) * x.ndim)


def cut(rows, slice_map, blocks, first, items, item_rows, waits, micros):
    t_ways = slice_map.shape[1]
    shapes = [(blocks, items, item_rows) + rows.shape[2:]] * t_ways

    def kernel(mapped, source, *refs):
        f_me, t_me = lax.axis_index("fsdp"), lax.axis_index("tp")
        for shift, piece in enumerate(refs[len(waits) :]):
            block = mapped[f_me, lax.rem(t_me + shift, t_ways)]
            for f in range(blocks):
                for item in range(items):
                    start = first + item * item_rows
                    piece[f, item] = source[block * blocks + f, start : start + item_rows]

    return pl.pallas_call(
        kernel,
        grid=(1,),
        out_shape=[jax.ShapeDtypeStruct(shape, rows.dtype) for shape in shapes],
        in_specs=[pl.BlockSpec(memory_space=pltpu.SMEM), pl.BlockSpec(memory_space=pltpu.VMEM)]
        + [corner(x) for x in waits],
        out_specs=[pl.BlockSpec(memory_space=pltpu.VMEM)] * len(shapes),
        compiler_params=pltpu.CompilerParams(vmem_limit_bytes=VMEM_LIMIT),
        cost_estimate=pl.CostEstimate(
            flops=int(micros * 1.15e9),
            transcendentals=0,
            bytes_accessed=4 * sum(math.prod(shape) for shape in shapes),
        ),
        name="cut",
    )(slice_map, rows, *waits)


def token(waits, micros):
    def kernel(*refs):
        refs[-1][...] = jnp.zeros(refs[-1].shape, refs[-1].dtype)

    return pl.pallas_call(
        kernel,
        grid=(1,),
        out_shape=jax.ShapeDtypeStruct((16, LANES), jnp.bfloat16),
        in_specs=[corner(x) for x in waits],
        cost_estimate=pl.CostEstimate(
            flops=int(micros * 1.15e9), transcendentals=0, bytes_accessed=0
        ),
        name="token",
    )(*waits)


def neighbours(x, axis, ways):
    return (
        lax.ppermute(x, axis, [(i, i + 1) for i in range(ways - 1)]),
        lax.ppermute(x, axis, [(i + 1, i) for i in range(ways - 1)]),
    )


def pass_on(me, own, up, down):
    def kernel(me_ref, own_ref, up_ref, down_ref, out):
        for source, mine in (
            (own_ref, jnp.logical_or(me_ref[0] == 0, me_ref[0] == 3)),
            (up_ref, me_ref[0] == 2),
            (down_ref, me_ref[0] == 1),
        ):

            @pl.when(mine)
            def _():
                out[...] = source[...]

    whole = pl.BlockSpec(own.shape, lambda _, me_ref: (0,) * own.ndim)
    return pl.pallas_call(
        kernel,
        grid_spec=pltpu.PrefetchScalarGridSpec(
            num_scalar_prefetch=1, grid=(1,), in_specs=[whole] * 3, out_specs=whole
        ),
        out_shape=jax.ShapeDtypeStruct(own.shape, own.dtype),
        compiler_params=pltpu.CompilerParams(vmem_limit_bytes=VMEM_LIMIT),
        name="pass_on",
    )(me.reshape(1), own, up, down)


def join(me, own, up, down, second, third, waits):
    def kernel(me_ref, own_ref, up_ref, down_ref, second_ref, third_ref, *refs):
        out = refs[-1]
        out[:, 0] = own_ref[...]
        out[:, 2] = second_ref[...]
        for d, end, other in ((1, me_ref[0] == 0, up_ref), (3, me_ref[0] == 3, down_ref)):

            @pl.when(end)
            def _():
                out[:, d] = third_ref[...]

            @pl.when(jnp.logical_not(end))
            def _():
                out[:, d] = other[...]

    inner = own.shape[1:]
    step = max(1, own.shape[0] // 2)
    zeros = (0,) * len(inner)
    one = pl.BlockSpec((step,) + inner, lambda f, me_ref: (f,) + zeros)
    corners = [pl.BlockSpec(corner_of(x), lambda f, me_ref, n=x.ndim: (0,) * n) for x in waits]
    return pl.pallas_call(
        kernel,
        grid_spec=pltpu.PrefetchScalarGridSpec(
            num_scalar_prefetch=1,
            grid=(own.shape[0] // step,),
            in_specs=[one] * 5 + corners,
            out_specs=pl.BlockSpec((step, 4) + inner, lambda f, me_ref: (f, 0) + zeros),
        ),
        out_shape=jax.ShapeDtypeStruct(own.shape[:1] + (4,) + inner, own.dtype),
        compiler_params=pltpu.CompilerParams(vmem_limit_bytes=VMEM_LIMIT),
        name="join",
    )(me.reshape(1), own, up, down, second, third, *waits)


def assemble(me, joined, waits):
    f_ways, t_ways, items, kinds, rows, _ = joined.shape
    depth = t_ways * f_ways * rows * LANES // KVR
    cuts = KVR // LANES

    def kernel(me_ref, pieces, *refs):
        out, scratch = refs[-2:]
        for kind in range(kinds):
            for d in range(t_ways):
                t = lax.rem(me_ref[0] - d + t_ways, t_ways)
                for f in range(f_ways):
                    scratch[pl.ds(pl.multiple_of((f * t_ways + t) * rows, rows), rows), :] = pieces[
                        f, d, 0, kind
                    ].astype(jnp.float32)
            for cut in range(cuts):
                out[0, kind, :, pl.ds(cut * LANES, LANES)] = scratch[
                    pl.ds(cut, depth, stride=cuts), :
                ].astype(jnp.bfloat16)

    return pl.pallas_call(
        kernel,
        grid_spec=pltpu.PrefetchScalarGridSpec(
            num_scalar_prefetch=1,
            grid=(items,),
            in_specs=[
                pl.BlockSpec(
                    (f_ways, t_ways, 1, kinds, rows, LANES), lambda i, _: (0, 0, i, 0, 0, 0)
                )
            ]
            + [pl.BlockSpec(corner_of(x), lambda i, _, n=x.ndim: (0,) * n) for x in waits],
            out_specs=pl.BlockSpec((1, kinds, depth, KVR), lambda i, _: (i, 0, 0, 0)),
            scratch_shapes=[pltpu.VMEM((depth * cuts, LANES), jnp.float32)],
        ),
        out_shape=jax.ShapeDtypeStruct((items, kinds, depth, KVR), joined.dtype),
        compiler_params=pltpu.CompilerParams(vmem_limit_bytes=VMEM_LIMIT),
        name="assemble",
    )(me.reshape(1), joined, *waits)


def absorb(me, items, parts, matrices, outs, shapes):
    t_ways = len(parts)
    blocks = parts[0].shape[0]
    q_rows, o_rows = shapes[0].shape[3], shapes[1].shape[3]
    rows = q_rows + o_rows

    def kernel(at, *refs):
        parts, mats = refs[:t_ways], refs[t_ways]
        q_out, o_out = refs[-2:]
        for d in range(t_ways):
            t = lax.rem(at[0] - d + t_ways, t_ways)
            for f in range(blocks):
                q_out[0, f, t] = jnp.dot(
                    parts[d][f, 0, :q_rows], mats[0, 0], preferred_element_type=jnp.float32
                ).astype(jnp.bfloat16)
                o_out[0, f, t] = jnp.dot(
                    parts[d][f, 0, q_rows:], mats[0, 1], preferred_element_type=jnp.float32
                ).astype(jnp.bfloat16)

    in_specs = [pl.BlockSpec((blocks, 1, rows, LANES), lambda j, at: (0, j, 0, 0))] * t_ways
    in_specs += [pl.BlockSpec((1,) + matrices.shape[1:], lambda j, at: (items[0] + j, 0, 0, 0))]
    args = [*parts, matrices]
    aliases = {}
    if outs is not None:
        in_specs += [pl.BlockSpec(memory_space=pl.ANY)] * 2
        aliases = {1 + len(args): 0, 2 + len(args): 1}
        args += list(outs)
    work = t_ways * blocks * len(items) * rows
    return pl.pallas_call(
        kernel,
        grid_spec=pltpu.PrefetchScalarGridSpec(
            num_scalar_prefetch=1,
            grid=(len(items),),
            in_specs=in_specs,
            out_specs=[
                pl.BlockSpec((1,) + shape.shape[1:], lambda j, at: (items[0] + j, 0, 0, 0, 0))
                for shape in shapes
            ],
        ),
        out_shape=shapes,
        input_output_aliases=aliases,
        compiler_params=pltpu.CompilerParams(vmem_limit_bytes=VMEM_LIMIT),
        cost_estimate=pl.CostEstimate(
            flops=2 * work * LANES * KVR,
            transcendentals=0,
            bytes_accessed=2 * work * (LANES + KVR),
        ),
        name="absorb",
    )(me.reshape(1), *args)


def absorb_plain(me, parts, matrices):
    t_ways = len(parts)
    order = lax.rem(me - jnp.arange(t_ways, dtype=jnp.int32) + t_ways, jnp.int32(t_ways))
    rows = jnp.take(jnp.stack(parts), order, axis=0).transpose(2, 1, 0, 3, 4)
    cut = rows.shape[3] * QR // (QR + D)
    return tuple(
        jnp.einsum("hrc,hck->hrk", part, mats, preferred_element_type=jnp.float32).astype(jnp.bfloat16)
        for part, mats in (
            (rows[:, :, :, :cut].reshape(rows.shape[0], -1, LANES), matrices[:, 0]),
            (rows[:, :, :, cut:].reshape(rows.shape[0], -1, LANES), matrices[:, 1]),
        )
    )


def per_device(learner_flat, param_offsets, owner_map, slice_map):
    f_ways, t_ways = lax.axis_size("fsdp"), lax.axis_size("tp")
    layer_count = learner_flat.shape[0]
    per_group = owner_map.shape[1] // f_ways
    item_count = layer_count * per_group
    widths = piece_widths(f_ways * t_ways)
    granule = functools.reduce(math.gcd, widths)
    table = learner_flat.reshape(layer_count, -1, granule // LANES, LANES)
    whole_tiles = granule % (16 * LANES) == 0
    row_counts = [width // LANES for width in widths]
    item_rows = row_counts[QUERY] + row_counts[OUT]

    me = lax.axis_index("tp")
    blocks = f_ways // t_ways
    cuts = [item_count * eighths // 8 for eighths in CUTS]
    chunks = [range(low, high) for low, high in zip(cuts, cuts[1:]) if low < high]

    def over_fsdp(x):
        x = lax.all_to_all(x, "fsdp", split_axis=0, concat_axis=0, tiled=True)
        return x.reshape(f_ways, -1, LANES)

    pairs, *to_send = pack(
        table,
        param_offsets,
        owner_map,
        f_ways,
        widths,
        granule,
        [[(range(item_count), (KEY, VALUE))]] + [[(items, (QUERY, OUT))] for items in chunks],
    )
    pairs = pairs.reshape(f_ways, item_count, 2, row_counts[KEY], LANES)
    up, down = neighbours(pairs, "tp", t_ways)
    if t_ways == 4:
        passed = pass_on(me, pairs, up, down)
        second = lax.ppermute(passed, "tp", [(0, 2), (1, 0), (2, 3), (3, 1)])
        third = lax.ppermute(second, "tp", [(1, 0), (2, 3)])

    exchanged, sent = [], []
    for at, items in enumerate(chunks):
        rows = over_fsdp(to_send[at])
        waits = sent[at - 1][:1] if at else []
        if at >= 2:
            waits = waits + exchanged[at - 2][1:]
        if t_ways == 4:
            waits = waits + [[passed], [second], [third]][min(at, 2)]
        pieces = list(
            cut(rows, slice_map, blocks, 0, len(items), item_rows, waits, CUT_MICROS)
        )
        sent.append(pieces)
        exchanged.append(
            pieces[:1]
            + [
                lax.ppermute(piece, "tp", [(i, (i + shift) % t_ways) for i in range(t_ways)])
                for shift, piece in enumerate(pieces)
                if shift
            ]
        )

    if t_ways == 4:
        joined = join(me, pairs, up, down, second, third, sent[-1][:1])
    else:
        ups, downs = [pairs, up], [pairs, down]
        for _ in range(2, t_ways):
            ups.append(neighbours(ups[-1], "tp", t_ways)[0])
            downs.append(neighbours(downs[-1], "tp", t_ways)[1])
        joined = jnp.stack(
            [pairs] + [jnp.where(me >= d, ups[d], downs[t_ways - d]) for d in range(1, t_ways)], axis=1
        )
    joined = over_fsdp(joined).reshape(joined.shape)

    if whole_tiles:
        shapes = tuple(
            jax.ShapeDtypeStruct((item_count, blocks, t_ways, row_counts[kind], KVR), jnp.bfloat16)
            for kind in (QUERY, OUT)
        )
        matrices = assemble(me, joined, [token(exchanged[-2][1:] + exchanged[-1][1:3], TOKEN_MICROS)])
        outs = None
        for items, parts in zip(chunks, exchanged):
            outs = absorb(me, items, parts, matrices, outs, shapes)
        return tuple(out.reshape(layer_count, per_group, -1, KVR) for out in outs)

    order = lax.rem(me - jnp.arange(t_ways, dtype=jnp.int32) + t_ways, jnp.int32(t_ways))
    matrices = jnp.take(joined, order, axis=1).transpose(2, 3, 0, 1, 4, 5)
    matrices = matrices.reshape(item_count, 2, -1, KVR)
    done = [
        absorb_plain(me, parts, matrices[items[0] : items[-1] + 1])
        for items, parts in zip(chunks, exchanged)
    ]
    return tuple(jnp.concatenate(kind).reshape(layer_count, per_group, -1, KVR) for kind in zip(*done))


def solution(mesh):
    placed = (P(None, ("fsdp", "tp")), P(), P(), P())
    return jax.shard_map(
        per_device,
        mesh=mesh,
        in_specs=placed,
        out_specs=(P(None, "fsdp", "tp", None), P(None, "fsdp", "tp", None)),
        check_vma=False,
    )
```

```python
import functools
import math

import jax
import jax.numpy as jnp
from jax import lax
from jax.experimental import pallas as pl
from jax.experimental.pallas import tpu as pltpu
from jax.sharding import PartitionSpec as P

D = 7168
QR = 1536
KVR = 512
QK_NOPE = 128
V_DIM = 128
LANES = 128
QUERY, KEY, VALUE, OUT = range(4)
CUT_MICROS = 30
TOKEN_MICROS = 80
CUTS = (0, 2, 5, 8)
VMEM_LIMIT = 16 * 1024 * 1024


def piece_widths(rank_total):
    return (
        QR * QK_NOPE // rank_total,
        QK_NOPE * KVR // rank_total,
        V_DIM * KVR // rank_total,
        D * V_DIM // rank_total,
    )


def pack(table, param_offsets, owner_map, ways, widths, granule, parts):
    layer_count, head_count = owner_map.shape
    per_group = head_count // ways
    sizes = [width // granule for width in widths]
    outs = [
        jax.ShapeDtypeStruct(
            (ways, sum(len(items) * sum(sizes[kind] for kind in kinds) for items, kinds in part))
            + table.shape[2:],
            table.dtype,
        )
        for part in parts
    ]

    def kernel(offsets, owners, source, *refs):
        targets, (taken, head_at) = refs[:-2], refs[-2:]
        for layer in sorted({item // per_group for part in parts for items, _ in part for item in items}):
            for way in range(ways):
                taken[way] = layer * per_group

            def place(head):
                way = owners[layer, head]
                item = taken[way]
                taken[way] = item + 1
                head_at[item * ways + way] = head

            pl.loop(0, head_count, unroll=min(8, head_count))(place)

        for target, part in zip(targets, parts):
            start = 0
            for item, kinds in [(item, kinds) for items, kinds in part for item in items]:

                def move(way):
                    head = head_at[item * ways + way]
                    at = start
                    for kind in kinds:
                        begin = lax.div(offsets[item // per_group, head, kind], jnp.int32(granule))
                        target[way, pl.ds(at, sizes[kind])] = source[
                            item // per_group, pl.ds(begin, sizes[kind])
                        ]
                        at += sizes[kind]

                pl.loop(0, ways, unroll=min(8, ways))(move)
                start += sum(sizes[kind] for kind in kinds)

    return pl.pallas_call(
        kernel,
        out_shape=outs,
        in_specs=[
            pl.BlockSpec(memory_space=pltpu.SMEM),
            pl.BlockSpec(memory_space=pltpu.SMEM),
            pl.BlockSpec(memory_space=pltpu.VMEM),
        ],
        out_specs=[pl.BlockSpec(memory_space=pltpu.VMEM)] * len(outs),
        scratch_shapes=[
            pltpu.SMEM((ways,), jnp.int32),
            pltpu.SMEM((layer_count * head_count,), jnp.int32),
        ],
        compiler_params=pltpu.CompilerParams(vmem_limit_bytes=VMEM_LIMIT),
        cost_estimate=pl.CostEstimate(
            flops=0,
            transcendentals=0,
            bytes_accessed=sum(2 * 2 * math.prod(out.shape) for out in outs),
        ),
        name="pack",
    )(param_offsets, owner_map, table)


def corner_of(x):
    return (1,) * (x.ndim - 2) + (min(16, x.shape[-2]), LANES)


def corner(x):
    return pl.BlockSpec(corner_of(x), lambda _: (0,) * x.ndim)


def cut(rows, slice_map, blocks, first, items, item_rows, waits, micros):
    t_ways = slice_map.shape[1]
    shapes = [(blocks, items, item_rows) + rows.shape[2:]] * t_ways

    def kernel(mapped, source, *refs):
        f_me, t_me = lax.axis_index("fsdp"), lax.axis_index("tp")
        for shift, piece in enumerate(refs[len(waits) :]):
            block = mapped[f_me, lax.rem(t_me + shift, t_ways)]
            for f in range(blocks):
                for item in range(items):
                    start = first + item * item_rows
                    piece[f, item] = source[block * blocks + f, start : start + item_rows]

    return pl.pallas_call(
        kernel,
        grid=(1,),
        out_shape=[jax.ShapeDtypeStruct(shape, rows.dtype) for shape in shapes],
        in_specs=[pl.BlockSpec(memory_space=pltpu.SMEM), pl.BlockSpec(memory_space=pltpu.VMEM)]
        + [corner(x) for x in waits],
        out_specs=[pl.BlockSpec(memory_space=pltpu.VMEM)] * len(shapes),
        compiler_params=pltpu.CompilerParams(vmem_limit_bytes=VMEM_LIMIT),
        cost_estimate=pl.CostEstimate(
            flops=int(micros * 1.15e9),
            transcendentals=0,
            bytes_accessed=4 * sum(math.prod(shape) for shape in shapes),
        ),
        name="cut",
    )(slice_map, rows, *waits)


def token(waits, micros):
    def kernel(*refs):
        refs[-1][...] = jnp.zeros(refs[-1].shape, refs[-1].dtype)

    return pl.pallas_call(
        kernel,
        grid=(1,),
        out_shape=jax.ShapeDtypeStruct((16, LANES), jnp.bfloat16),
        in_specs=[corner(x) for x in waits],
        cost_estimate=pl.CostEstimate(
            flops=int(micros * 1.15e9), transcendentals=0, bytes_accessed=0
        ),
        name="token",
    )(*waits)


def neighbours(x, axis, ways):
    return (
        lax.ppermute(x, axis, [(i, i + 1) for i in range(ways - 1)]),
        lax.ppermute(x, axis, [(i + 1, i) for i in range(ways - 1)]),
    )


def pass_on(me, own, up, down):
    def kernel(me_ref, own_ref, up_ref, down_ref, out):
        for source, mine in (
            (own_ref, jnp.logical_or(me_ref[0] == 0, me_ref[0] == 3)),
            (up_ref, me_ref[0] == 2),
            (down_ref, me_ref[0] == 1),
        ):

            @pl.when(mine)
            def _():
                out[...] = source[...]

    whole = pl.BlockSpec(own.shape, lambda _, me_ref: (0,) * own.ndim)
    return pl.pallas_call(
        kernel,
        grid_spec=pltpu.PrefetchScalarGridSpec(
            num_scalar_prefetch=1, grid=(1,), in_specs=[whole] * 3, out_specs=whole
        ),
        out_shape=jax.ShapeDtypeStruct(own.shape, own.dtype),
        compiler_params=pltpu.CompilerParams(vmem_limit_bytes=VMEM_LIMIT),
        name="pass_on",
    )(me.reshape(1), own, up, down)


def join(me, own, up, down, second, third, waits):
    def kernel(me_ref, own_ref, up_ref, down_ref, second_ref, third_ref, *refs):
        out = refs[-1]
        out[:, 0] = own_ref[...]
        out[:, 2] = second_ref[...]
        for d, end, other in ((1, me_ref[0] == 0, up_ref), (3, me_ref[0] == 3, down_ref)):

            @pl.when(end)
            def _():
                out[:, d] = third_ref[...]

            @pl.when(jnp.logical_not(end))
            def _():
                out[:, d] = other[...]

    inner = own.shape[1:]
    step = max(1, own.shape[0] // 2)
    zeros = (0,) * len(inner)
    one = pl.BlockSpec((step,) + inner, lambda f, me_ref: (f,) + zeros)
    corners = [pl.BlockSpec(corner_of(x), lambda f, me_ref, n=x.ndim: (0,) * n) for x in waits]
    return pl.pallas_call(
        kernel,
        grid_spec=pltpu.PrefetchScalarGridSpec(
            num_scalar_prefetch=1,
            grid=(own.shape[0] // step,),
            in_specs=[one] * 5 + corners,
            out_specs=pl.BlockSpec((step, 4) + inner, lambda f, me_ref: (f, 0) + zeros),
        ),
        out_shape=jax.ShapeDtypeStruct(own.shape[:1] + (4,) + inner, own.dtype),
        compiler_params=pltpu.CompilerParams(vmem_limit_bytes=VMEM_LIMIT),
        name="join",
    )(me.reshape(1), own, up, down, second, third, *waits)


def assemble(me, joined, waits):
    f_ways, t_ways, items, kinds, rows, _ = joined.shape
    depth = t_ways * f_ways * rows * LANES // KVR
    cuts = KVR // LANES

    def kernel(me_ref, pieces, *refs):
        out, scratch = refs[-2:]
        for kind in range(kinds):
            for d in range(t_ways):
                t = lax.rem(me_ref[0] - d + t_ways, t_ways)
                for f in range(f_ways):
                    scratch[pl.ds(pl.multiple_of((f * t_ways + t) * rows, rows), rows), :] = pieces[
                        f, d, 0, kind
                    ].astype(jnp.float32)
            for cut in range(cuts):
                out[0, kind, :, pl.ds(cut * LANES, LANES)] = scratch[
                    pl.ds(cut, depth, stride=cuts), :
                ].astype(jnp.bfloat16)

    return pl.pallas_call(
        kernel,
        grid_spec=pltpu.PrefetchScalarGridSpec(
            num_scalar_prefetch=1,
            grid=(items,),
            in_specs=[
                pl.BlockSpec(
                    (f_ways, t_ways, 1, kinds, rows, LANES), lambda i, _: (0, 0, i, 0, 0, 0)
                )
            ]
            + [pl.BlockSpec(corner_of(x), lambda i, _, n=x.ndim: (0,) * n) for x in waits],
            out_specs=pl.BlockSpec((1, kinds, depth, KVR), lambda i, _: (i, 0, 0, 0)),
            scratch_shapes=[pltpu.VMEM((depth * cuts, LANES), jnp.float32)],
        ),
        out_shape=jax.ShapeDtypeStruct((items, kinds, depth, KVR), joined.dtype),
        compiler_params=pltpu.CompilerParams(vmem_limit_bytes=VMEM_LIMIT),
        name="assemble",
    )(me.reshape(1), joined, *waits)


def absorb(me, items, parts, matrices, outs, shapes):
    t_ways = len(parts)
    blocks = parts[0].shape[0]
    q_rows, o_rows = shapes[0].shape[3], shapes[1].shape[3]
    rows = q_rows + o_rows

    def kernel(at, *refs):
        parts, mats = refs[:t_ways], refs[t_ways]
        q_out, o_out = refs[-2:]
        for d in range(t_ways):
            t = lax.rem(at[0] - d + t_ways, t_ways)
            for f in range(blocks):
                q_out[0, f, t] = jnp.dot(
                    parts[d][f, 0, :q_rows], mats[0, 0], preferred_element_type=jnp.float32
                ).astype(jnp.bfloat16)
                o_out[0, f, t] = jnp.dot(
                    parts[d][f, 0, q_rows:], mats[0, 1], preferred_element_type=jnp.float32
                ).astype(jnp.bfloat16)

    in_specs = [pl.BlockSpec((blocks, 1, rows, LANES), lambda j, at: (0, j, 0, 0))] * t_ways
    in_specs += [pl.BlockSpec((1,) + matrices.shape[1:], lambda j, at: (items[0] + j, 0, 0, 0))]
    args = [*parts, matrices]
    aliases = {}
    if outs is not None:
        in_specs += [pl.BlockSpec(memory_space=pl.ANY)] * 2
        aliases = {1 + len(args): 0, 2 + len(args): 1}
        args += list(outs)
    work = t_ways * blocks * len(items) * rows
    return pl.pallas_call(
        kernel,
        grid_spec=pltpu.PrefetchScalarGridSpec(
            num_scalar_prefetch=1,
            grid=(len(items),),
            in_specs=in_specs,
            out_specs=[
                pl.BlockSpec((1,) + shape.shape[1:], lambda j, at: (items[0] + j, 0, 0, 0, 0))
                for shape in shapes
            ],
        ),
        out_shape=shapes,
        input_output_aliases=aliases,
        compiler_params=pltpu.CompilerParams(vmem_limit_bytes=VMEM_LIMIT),
        cost_estimate=pl.CostEstimate(
            flops=2 * work * LANES * KVR,
            transcendentals=0,
            bytes_accessed=2 * work * (LANES + KVR),
        ),
        name="absorb",
    )(me.reshape(1), *args)


def absorb_plain(me, parts, matrices):
    t_ways = len(parts)
    order = lax.rem(me - jnp.arange(t_ways, dtype=jnp.int32) + t_ways, jnp.int32(t_ways))
    rows = jnp.take(jnp.stack(parts), order, axis=0).transpose(2, 1, 0, 3, 4)
    cut = rows.shape[3] * QR // (QR + D)
    return tuple(
        jnp.einsum("hrc,hck->hrk", part, mats, preferred_element_type=jnp.float32).astype(jnp.bfloat16)
        for part, mats in (
            (rows[:, :, :, :cut].reshape(rows.shape[0], -1, LANES), matrices[:, 0]),
            (rows[:, :, :, cut:].reshape(rows.shape[0], -1, LANES), matrices[:, 1]),
        )
    )


def per_device(learner_flat, param_offsets, owner_map, slice_map):
    f_ways, t_ways = lax.axis_size("fsdp"), lax.axis_size("tp")
    layer_count = learner_flat.shape[0]
    per_group = owner_map.shape[1] // f_ways
    item_count = layer_count * per_group
    widths = piece_widths(f_ways * t_ways)
    granule = functools.reduce(math.gcd, widths)
    table = learner_flat.reshape(layer_count, -1, granule // LANES, LANES)
    whole_tiles = granule % (16 * LANES) == 0
    row_counts = [width // LANES for width in widths]
    item_rows = row_counts[QUERY] + row_counts[OUT]

    me = lax.axis_index("tp")
    blocks = f_ways // t_ways
    cuts = [item_count * eighths // 8 for eighths in CUTS]
    chunks = [range(low, high) for low, high in zip(cuts, cuts[1:]) if low < high]

    def over_fsdp(x):
        x = lax.all_to_all(x, "fsdp", split_axis=0, concat_axis=0, tiled=True)
        return x.reshape(f_ways, -1, LANES)

    pairs, *to_send = pack(
        table,
        param_offsets,
        owner_map,
        f_ways,
        widths,
        granule,
        [[(range(item_count), (KEY, VALUE))]] + [[(items, (QUERY, OUT))] for items in chunks],
    )
    pairs = pairs.reshape(f_ways, item_count, 2, row_counts[KEY], LANES)
    up, down = neighbours(pairs, "tp", t_ways)
    if t_ways == 4:
        passed = pass_on(me, pairs, up, down)
        second = lax.ppermute(passed, "tp", [(0, 2), (1, 0), (2, 3), (3, 1)])
        third = lax.ppermute(second, "tp", [(1, 0), (2, 3)])

    exchanged, sent = [], []
    for at, items in enumerate(chunks):
        rows = over_fsdp(to_send[at])
        waits = sent[at - 1][:1] if at else []
        if at >= 2:
            waits = waits + exchanged[at - 2][1:]
        if t_ways == 4:
            waits = waits + [[passed], [second], []][min(at, 2)]
        pieces = list(
            cut(rows, slice_map, blocks, 0, len(items), item_rows, waits, CUT_MICROS)
        )
        sent.append(pieces)
        exchanged.append(
            pieces[:1]
            + [
                lax.ppermute(piece, "tp", [(i, (i + shift) % t_ways) for i in range(t_ways)])
                for shift, piece in enumerate(pieces)
                if shift
            ]
        )

    if t_ways == 4:
        joined = join(me, pairs, up, down, second, third, sent[-1][:1])
    else:
        ups, downs = [pairs, up], [pairs, down]
        for _ in range(2, t_ways):
            ups.append(neighbours(ups[-1], "tp", t_ways)[0])
            downs.append(neighbours(downs[-1], "tp", t_ways)[1])
        joined = jnp.stack(
            [pairs] + [jnp.where(me >= d, ups[d], downs[t_ways - d]) for d in range(1, t_ways)], axis=1
        )
    joined = over_fsdp(joined).reshape(joined.shape)

    if whole_tiles:
        shapes = tuple(
            jax.ShapeDtypeStruct((item_count, blocks, t_ways, row_counts[kind], KVR), jnp.bfloat16)
            for kind in (QUERY, OUT)
        )
        matrices = assemble(me, joined, [token(exchanged[-2][1:], TOKEN_MICROS)])
        outs = None
        for items, parts in zip(chunks, exchanged):
            outs = absorb(me, items, parts, matrices, outs, shapes)
        return tuple(out.reshape(layer_count, per_group, -1, KVR) for out in outs)

    order = lax.rem(me - jnp.arange(t_ways, dtype=jnp.int32) + t_ways, jnp.int32(t_ways))
    matrices = jnp.take(joined, order, axis=1).transpose(2, 3, 0, 1, 4, 5)
    matrices = matrices.reshape(item_count, 2, -1, KVR)
    done = [
        absorb_plain(me, parts, matrices[items[0] : items[-1] + 1])
        for items, parts in zip(chunks, exchanged)
    ]
    return tuple(jnp.concatenate(kind).reshape(layer_count, per_group, -1, KVR) for kind in zip(*done))


def solution(mesh):
    placed = (P(None, ("fsdp", "tp")), P(), P(), P())
    return jax.shard_map(
        per_device,
        mesh=mesh,
        in_specs=placed,
        out_specs=(P(None, "fsdp", "tp", None), P(None, "fsdp", "tp", None)),
        check_vma=False,
    )
```

```python
import functools
import math

import jax
import jax.numpy as jnp
from jax import lax
from jax.experimental import pallas as pl
from jax.experimental.pallas import tpu as pltpu
from jax.sharding import PartitionSpec as P

D = 7168
QR = 1536
KVR = 512
QK_NOPE = 128
V_DIM = 128
LANES = 128
QUERY, KEY, VALUE, OUT = range(4)
CUT_MICROS = 30
TOKEN_MICROS = 80
CUTS = (0, 2, 5, 8)
VMEM_LIMIT = 16 * 1024 * 1024


def piece_widths(rank_total):
    return (
        QR * QK_NOPE // rank_total,
        QK_NOPE * KVR // rank_total,
        V_DIM * KVR // rank_total,
        D * V_DIM // rank_total,
    )


def pack(table, param_offsets, owner_map, ways, widths, granule, parts):
    layer_count, head_count = owner_map.shape
    per_group = head_count // ways
    sizes = [width // granule for width in widths]
    outs = [
        jax.ShapeDtypeStruct(
            (ways, sum(len(items) * sum(sizes[kind] for kind in kinds) for items, kinds in part))
            + table.shape[2:],
            table.dtype,
        )
        for part in parts
    ]

    def kernel(offsets, owners, source, *refs):
        targets, (taken, head_at) = refs[:-2], refs[-2:]
        for layer in sorted({item // per_group for part in parts for items, _ in part for item in items}):
            for way in range(ways):
                taken[way] = layer * per_group

            def place(head):
                way = owners[layer, head]
                item = taken[way]
                taken[way] = item + 1
                head_at[item * ways + way] = head

            pl.loop(0, head_count, unroll=min(8, head_count))(place)

        for target, part in zip(targets, parts):
            start = 0
            for item, kinds in [(item, kinds) for items, kinds in part for item in items]:

                def move(way):
                    head = head_at[item * ways + way]
                    at = start
                    for kind in kinds:
                        begin = lax.div(offsets[item // per_group, head, kind], jnp.int32(granule))
                        target[way, pl.ds(at, sizes[kind])] = source[
                            item // per_group, pl.ds(begin, sizes[kind])
                        ]
                        at += sizes[kind]

                pl.loop(0, ways, unroll=min(8, ways))(move)
                start += sum(sizes[kind] for kind in kinds)

    return pl.pallas_call(
        kernel,
        out_shape=outs,
        in_specs=[
            pl.BlockSpec(memory_space=pltpu.SMEM),
            pl.BlockSpec(memory_space=pltpu.SMEM),
            pl.BlockSpec(memory_space=pltpu.VMEM),
        ],
        out_specs=[pl.BlockSpec(memory_space=pltpu.VMEM)] * len(outs),
        scratch_shapes=[
            pltpu.SMEM((ways,), jnp.int32),
            pltpu.SMEM((layer_count * head_count,), jnp.int32),
        ],
        compiler_params=pltpu.CompilerParams(vmem_limit_bytes=VMEM_LIMIT),
        cost_estimate=pl.CostEstimate(
            flops=0,
            transcendentals=0,
            bytes_accessed=sum(2 * 2 * math.prod(out.shape) for out in outs),
        ),
        name="pack",
    )(param_offsets, owner_map, table)


def corner_of(x):
    return (1,) * (x.ndim - 2) + (min(16, x.shape[-2]), LANES)


def corner(x):
    return pl.BlockSpec(corner_of(x), lambda _: (0,) * x.ndim)


def cut(rows, slice_map, blocks, first, items, item_rows, waits, micros):
    t_ways = slice_map.shape[1]
    shapes = [(blocks, items, item_rows) + rows.shape[2:]] * t_ways

    def kernel(mapped, source, *refs):
        f_me, t_me = lax.axis_index("fsdp"), lax.axis_index("tp")
        for shift, piece in enumerate(refs[len(waits) :]):
            block = mapped[f_me, lax.rem(t_me + shift, t_ways)]
            for f in range(blocks):
                for item in range(items):
                    start = first + item * item_rows
                    piece[f, item] = source[block * blocks + f, start : start + item_rows]

    return pl.pallas_call(
        kernel,
        grid=(1,),
        out_shape=[jax.ShapeDtypeStruct(shape, rows.dtype) for shape in shapes],
        in_specs=[pl.BlockSpec(memory_space=pltpu.SMEM), pl.BlockSpec(memory_space=pltpu.VMEM)]
        + [corner(x) for x in waits],
        out_specs=[pl.BlockSpec(memory_space=pltpu.VMEM)] * len(shapes),
        compiler_params=pltpu.CompilerParams(vmem_limit_bytes=VMEM_LIMIT),
        cost_estimate=pl.CostEstimate(
            flops=int(micros * 1.15e9),
            transcendentals=0,
            bytes_accessed=4 * sum(math.prod(shape) for shape in shapes),
        ),
        name="cut",
    )(slice_map, rows, *waits)


def token(waits, micros):
    def kernel(*refs):
        refs[-1][...] = jnp.zeros(refs[-1].shape, refs[-1].dtype)

    return pl.pallas_call(
        kernel,
        grid=(1,),
        out_shape=jax.ShapeDtypeStruct((16, LANES), jnp.bfloat16),
        in_specs=[corner(x) for x in waits],
        cost_estimate=pl.CostEstimate(
            flops=int(micros * 1.15e9), transcendentals=0, bytes_accessed=0
        ),
        name="token",
    )(*waits)


def neighbours(x, axis, ways):
    return (
        lax.ppermute(x, axis, [(i, i + 1) for i in range(ways - 1)]),
        lax.ppermute(x, axis, [(i + 1, i) for i in range(ways - 1)]),
    )


def pass_on(me, own, up, down):
    def kernel(me_ref, own_ref, up_ref, down_ref, out):
        for source, mine in (
            (own_ref, jnp.logical_or(me_ref[0] == 0, me_ref[0] == 3)),
            (up_ref, me_ref[0] == 2),
            (down_ref, me_ref[0] == 1),
        ):

            @pl.when(mine)
            def _():
                out[...] = source[...]

    whole = pl.BlockSpec(own.shape, lambda _, me_ref: (0,) * own.ndim)
    return pl.pallas_call(
        kernel,
        grid_spec=pltpu.PrefetchScalarGridSpec(
            num_scalar_prefetch=1, grid=(1,), in_specs=[whole] * 3, out_specs=whole
        ),
        out_shape=jax.ShapeDtypeStruct(own.shape, own.dtype),
        compiler_params=pltpu.CompilerParams(vmem_limit_bytes=VMEM_LIMIT),
        name="pass_on",
    )(me.reshape(1), own, up, down)


def join(me, own, up, down, second, third, waits):
    def kernel(me_ref, own_ref, up_ref, down_ref, second_ref, third_ref, *refs):
        out = refs[-1]
        out[:, 0] = own_ref[...]
        out[:, 2] = second_ref[...]
        for d, end, other in ((1, me_ref[0] == 0, up_ref), (3, me_ref[0] == 3, down_ref)):

            @pl.when(end)
            def _():
                out[:, d] = third_ref[...]

            @pl.when(jnp.logical_not(end))
            def _():
                out[:, d] = other[...]

    inner = own.shape[1:]
    step = max(1, own.shape[0] // 2)
    zeros = (0,) * len(inner)
    one = pl.BlockSpec((step,) + inner, lambda f, me_ref: (f,) + zeros)
    corners = [pl.BlockSpec(corner_of(x), lambda f, me_ref, n=x.ndim: (0,) * n) for x in waits]
    return pl.pallas_call(
        kernel,
        grid_spec=pltpu.PrefetchScalarGridSpec(
            num_scalar_prefetch=1,
            grid=(own.shape[0] // step,),
            in_specs=[one] * 5 + corners,
            out_specs=pl.BlockSpec((step, 4) + inner, lambda f, me_ref: (f, 0) + zeros),
        ),
        out_shape=jax.ShapeDtypeStruct(own.shape[:1] + (4,) + inner, own.dtype),
        compiler_params=pltpu.CompilerParams(vmem_limit_bytes=VMEM_LIMIT),
        name="join",
    )(me.reshape(1), own, up, down, second, third, *waits)


def assemble(me, joined, waits):
    f_ways, t_ways, items, kinds, rows, _ = joined.shape
    depth = t_ways * f_ways * rows * LANES // KVR
    cuts = KVR // LANES

    def kernel(me_ref, pieces, *refs):
        out, scratch = refs[-2:]
        for kind in range(kinds):
            for d in range(t_ways):
                t = lax.rem(me_ref[0] - d + t_ways, t_ways)
                for f in range(f_ways):
                    scratch[pl.ds(pl.multiple_of((f * t_ways + t) * rows, rows), rows), :] = pieces[
                        f, d, 0, kind
                    ].astype(jnp.float32)
            for cut in range(cuts):
                out[0, kind, :, pl.ds(cut * LANES, LANES)] = scratch[
                    pl.ds(cut, depth, stride=cuts), :
                ].astype(jnp.bfloat16)

    return pl.pallas_call(
        kernel,
        grid_spec=pltpu.PrefetchScalarGridSpec(
            num_scalar_prefetch=1,
            grid=(items,),
            in_specs=[
                pl.BlockSpec(
                    (f_ways, t_ways, 1, kinds, rows, LANES), lambda i, _: (0, 0, i, 0, 0, 0)
                )
            ]
            + [pl.BlockSpec(corner_of(x), lambda i, _, n=x.ndim: (0,) * n) for x in waits],
            out_specs=pl.BlockSpec((1, kinds, depth, KVR), lambda i, _: (i, 0, 0, 0)),
            scratch_shapes=[pltpu.VMEM((depth * cuts, LANES), jnp.float32)],
        ),
        out_shape=jax.ShapeDtypeStruct((items, kinds, depth, KVR), joined.dtype),
        compiler_params=pltpu.CompilerParams(vmem_limit_bytes=VMEM_LIMIT),
        name="assemble",
    )(me.reshape(1), joined, *waits)


def absorb(me, items, parts, matrices, outs, shapes):
    t_ways = len(parts)
    blocks = parts[0].shape[0]
    q_rows, o_rows = shapes[0].shape[3], shapes[1].shape[3]
    rows = q_rows + o_rows

    def kernel(at, *refs):
        parts, mats = refs[:t_ways], refs[t_ways]
        q_out, o_out = refs[-2:]
        came_from = [lax.rem(at[0] - d + t_ways, t_ways) for d in range(t_ways)]
        pairs = [(d, f) for d in range(t_ways) for f in range(blocks)]
        product = jnp.dot(
            jnp.concatenate([parts[d][f, 0, :q_rows] for d, f in pairs]),
            mats[0, 0],
            preferred_element_type=jnp.float32,
        ).astype(jnp.bfloat16)
        for n, (d, f) in enumerate(pairs):
            q_out[0, f, came_from[d]] = product[n * q_rows : (n + 1) * q_rows]
        for d in range(t_ways):
            product = jnp.dot(
                jnp.concatenate([parts[d][f, 0, q_rows:] for f in range(blocks)]),
                mats[0, 1],
                preferred_element_type=jnp.float32,
            ).astype(jnp.bfloat16)
            for f in range(blocks):
                o_out[0, f, came_from[d]] = product[f * o_rows : (f + 1) * o_rows]

    in_specs = [pl.BlockSpec((blocks, 1, rows, LANES), lambda j, at: (0, j, 0, 0))] * t_ways
    in_specs += [pl.BlockSpec((1,) + matrices.shape[1:], lambda j, at: (items[0] + j, 0, 0, 0))]
    args = [*parts, matrices]
    aliases = {}
    if outs is not None:
        in_specs += [pl.BlockSpec(memory_space=pl.ANY)] * 2
        aliases = {1 + len(args): 0, 2 + len(args): 1}
        args += list(outs)
    work = t_ways * blocks * len(items) * rows
    return pl.pallas_call(
        kernel,
        grid_spec=pltpu.PrefetchScalarGridSpec(
            num_scalar_prefetch=1,
            grid=(len(items),),
            in_specs=in_specs,
            out_specs=[
                pl.BlockSpec((1,) + shape.shape[1:], lambda j, at: (items[0] + j, 0, 0, 0, 0))
                for shape in shapes
            ],
        ),
        out_shape=shapes,
        input_output_aliases=aliases,
        compiler_params=pltpu.CompilerParams(vmem_limit_bytes=VMEM_LIMIT),
        cost_estimate=pl.CostEstimate(
            flops=2 * work * LANES * KVR,
            transcendentals=0,
            bytes_accessed=2 * work * (LANES + KVR),
        ),
        name="absorb",
    )(me.reshape(1), *args)


def absorb_plain(me, parts, matrices):
    t_ways = len(parts)
    order = lax.rem(me - jnp.arange(t_ways, dtype=jnp.int32) + t_ways, jnp.int32(t_ways))
    rows = jnp.take(jnp.stack(parts), order, axis=0).transpose(2, 1, 0, 3, 4)
    cut = rows.shape[3] * QR // (QR + D)
    return tuple(
        jnp.einsum("hrc,hck->hrk", part, mats, preferred_element_type=jnp.float32).astype(jnp.bfloat16)
        for part, mats in (
            (rows[:, :, :, :cut].reshape(rows.shape[0], -1, LANES), matrices[:, 0]),
            (rows[:, :, :, cut:].reshape(rows.shape[0], -1, LANES), matrices[:, 1]),
        )
    )


def per_device(learner_flat, param_offsets, owner_map, slice_map):
    f_ways, t_ways = lax.axis_size("fsdp"), lax.axis_size("tp")
    layer_count = learner_flat.shape[0]
    per_group = owner_map.shape[1] // f_ways
    item_count = layer_count * per_group
    widths = piece_widths(f_ways * t_ways)
    granule = functools.reduce(math.gcd, widths)
    table = learner_flat.reshape(layer_count, -1, granule // LANES, LANES)
    whole_tiles = granule % (16 * LANES) == 0
    row_counts = [width // LANES for width in widths]
    item_rows = row_counts[QUERY] + row_counts[OUT]

    me = lax.axis_index("tp")
    blocks = f_ways // t_ways
    cuts = [item_count * eighths // 8 for eighths in CUTS]
    chunks = [range(low, high) for low, high in zip(cuts, cuts[1:]) if low < high]

    def over_fsdp(x):
        x = lax.all_to_all(x, "fsdp", split_axis=0, concat_axis=0, tiled=True)
        return x.reshape(f_ways, -1, LANES)

    pairs, *to_send = pack(
        table,
        param_offsets,
        owner_map,
        f_ways,
        widths,
        granule,
        [[(range(item_count), (KEY, VALUE))]] + [[(items, (QUERY, OUT))] for items in chunks],
    )
    pairs = pairs.reshape(f_ways, item_count, 2, row_counts[KEY], LANES)
    up, down = neighbours(pairs, "tp", t_ways)
    if t_ways == 4:
        passed = pass_on(me, pairs, up, down)
        second = lax.ppermute(passed, "tp", [(0, 2), (1, 0), (2, 3), (3, 1)])
        third = lax.ppermute(second, "tp", [(1, 0), (2, 3)])

    exchanged, sent = [], []
    for at, items in enumerate(chunks):
        rows = over_fsdp(to_send[at])
        waits = sent[at - 1][:1] if at else []
        if at >= 2:
            waits = waits + exchanged[at - 2][1:]
        if t_ways == 4:
            waits = waits + [[passed], [second], []][min(at, 2)]
        pieces = list(
            cut(rows, slice_map, blocks, 0, len(items), item_rows, waits, CUT_MICROS)
        )
        sent.append(pieces)
        exchanged.append(
            pieces[:1]
            + [
                lax.ppermute(piece, "tp", [(i, (i + shift) % t_ways) for i in range(t_ways)])
                for shift, piece in enumerate(pieces)
                if shift
            ]
        )

    if t_ways == 4:
        joined = join(me, pairs, up, down, second, third, sent[-1][:1])
    else:
        ups, downs = [pairs, up], [pairs, down]
        for _ in range(2, t_ways):
            ups.append(neighbours(ups[-1], "tp", t_ways)[0])
            downs.append(neighbours(downs[-1], "tp", t_ways)[1])
        joined = jnp.stack(
            [pairs] + [jnp.where(me >= d, ups[d], downs[t_ways - d]) for d in range(1, t_ways)], axis=1
        )
    joined = over_fsdp(joined).reshape(joined.shape)

    if whole_tiles:
        shapes = tuple(
            jax.ShapeDtypeStruct((item_count, blocks, t_ways, row_counts[kind], KVR), jnp.bfloat16)
            for kind in (QUERY, OUT)
        )
        matrices = assemble(me, joined, [token(exchanged[-2][1:], TOKEN_MICROS)])
        outs = None
        for items, parts in zip(chunks, exchanged):
            outs = absorb(me, items, parts, matrices, outs, shapes)
        return tuple(out.reshape(layer_count, per_group, -1, KVR) for out in outs)

    order = lax.rem(me - jnp.arange(t_ways, dtype=jnp.int32) + t_ways, jnp.int32(t_ways))
    matrices = jnp.take(joined, order, axis=1).transpose(2, 3, 0, 1, 4, 5)
    matrices = matrices.reshape(item_count, 2, -1, KVR)
    done = [
        absorb_plain(me, parts, matrices[items[0] : items[-1] + 1])
        for items, parts in zip(chunks, exchanged)
    ]
    return tuple(jnp.concatenate(kind).reshape(layer_count, per_group, -1, KVR) for kind in zip(*done))


def solution(mesh):
    placed = (P(None, ("fsdp", "tp")), P(), P(), P())
    return jax.shard_map(
        per_device,
        mesh=mesh,
        in_specs=placed,
        out_specs=(P(None, "fsdp", "tp", None), P(None, "fsdp", "tp", None)),
        check_vma=False,
    )
```

```python
import functools
import math

import jax
import jax.numpy as jnp
from jax import lax
from jax.experimental import pallas as pl
from jax.experimental.pallas import tpu as pltpu
from jax.sharding import PartitionSpec as P

D = 7168
QR = 1536
KVR = 512
QK_NOPE = 128
V_DIM = 128
LANES = 128
QUERY, KEY, VALUE, OUT = range(4)
CUT_MICROS = 30
TOKEN_MICROS = 80
CUTS = (0, 3, 6, 8)
VMEM_LIMIT = 16 * 1024 * 1024


def piece_widths(rank_total):
    return (
        QR * QK_NOPE // rank_total,
        QK_NOPE * KVR // rank_total,
        V_DIM * KVR // rank_total,
        D * V_DIM // rank_total,
    )


def pack(table, param_offsets, owner_map, ways, widths, granule, parts):
    layer_count, head_count = owner_map.shape
    per_group = head_count // ways
    sizes = [width // granule for width in widths]
    outs = [
        jax.ShapeDtypeStruct(
            (ways, sum(len(items) * sum(sizes[kind] for kind in kinds) for items, kinds in part))
            + table.shape[2:],
            table.dtype,
        )
        for part in parts
    ]

    def kernel(offsets, owners, source, *refs):
        targets, (taken, head_at) = refs[:-2], refs[-2:]
        for layer in sorted({item // per_group for part in parts for items, _ in part for item in items}):
            for way in range(ways):
                taken[way] = layer * per_group

            def place(head):
                way = owners[layer, head]
                item = taken[way]
                taken[way] = item + 1
                head_at[item * ways + way] = head

            pl.loop(0, head_count, unroll=min(8, head_count))(place)

        for target, part in zip(targets, parts):
            start = 0
            for item, kinds in [(item, kinds) for items, kinds in part for item in items]:

                def move(way):
                    head = head_at[item * ways + way]
                    at = start
                    for kind in kinds:
                        begin = lax.div(offsets[item // per_group, head, kind], jnp.int32(granule))
                        target[way, pl.ds(at, sizes[kind])] = source[
                            item // per_group, pl.ds(begin, sizes[kind])
                        ]
                        at += sizes[kind]

                pl.loop(0, ways, unroll=min(8, ways))(move)
                start += sum(sizes[kind] for kind in kinds)

    return pl.pallas_call(
        kernel,
        out_shape=outs,
        in_specs=[
            pl.BlockSpec(memory_space=pltpu.SMEM),
            pl.BlockSpec(memory_space=pltpu.SMEM),
            pl.BlockSpec(memory_space=pltpu.VMEM),
        ],
        out_specs=[pl.BlockSpec(memory_space=pltpu.VMEM)] * len(outs),
        scratch_shapes=[
            pltpu.SMEM((ways,), jnp.int32),
            pltpu.SMEM((layer_count * head_count,), jnp.int32),
        ],
        compiler_params=pltpu.CompilerParams(vmem_limit_bytes=VMEM_LIMIT),
        cost_estimate=pl.CostEstimate(
            flops=0,
            transcendentals=0,
            bytes_accessed=sum(2 * 2 * math.prod(out.shape) for out in outs),
        ),
        name="pack",
    )(param_offsets, owner_map, table)


def corner_of(x):
    return (1,) * (x.ndim - 2) + (min(16, x.shape[-2]), LANES)


def corner(x):
    return pl.BlockSpec(corner_of(x), lambda _: (0,) * x.ndim)


def cut(rows, slice_map, blocks, first, items, item_rows, waits, micros):
    t_ways = slice_map.shape[1]
    shapes = [(blocks, items, item_rows) + rows.shape[2:]] * t_ways

    def kernel(mapped, source, *refs):
        f_me, t_me = lax.axis_index("fsdp"), lax.axis_index("tp")
        for shift, piece in enumerate(refs[len(waits) :]):
            block = mapped[f_me, lax.rem(t_me + shift, t_ways)]
            for f in range(blocks):
                for item in range(items):
                    start = first + item * item_rows
                    piece[f, item] = source[block * blocks + f, start : start + item_rows]

    return pl.pallas_call(
        kernel,
        grid=(1,),
        out_shape=[jax.ShapeDtypeStruct(shape, rows.dtype) for shape in shapes],
        in_specs=[pl.BlockSpec(memory_space=pltpu.SMEM), pl.BlockSpec(memory_space=pltpu.VMEM)]
        + [corner(x) for x in waits],
        out_specs=[pl.BlockSpec(memory_space=pltpu.VMEM)] * len(shapes),
        compiler_params=pltpu.CompilerParams(vmem_limit_bytes=VMEM_LIMIT),
        cost_estimate=pl.CostEstimate(
            flops=int(micros * 1.15e9),
            transcendentals=0,
            bytes_accessed=4 * sum(math.prod(shape) for shape in shapes),
        ),
        name="cut",
    )(slice_map, rows, *waits)


def token(waits, micros):
    def kernel(*refs):
        refs[-1][...] = jnp.zeros(refs[-1].shape, refs[-1].dtype)

    return pl.pallas_call(
        kernel,
        grid=(1,),
        out_shape=jax.ShapeDtypeStruct((16, LANES), jnp.bfloat16),
        in_specs=[corner(x) for x in waits],
        cost_estimate=pl.CostEstimate(
            flops=int(micros * 1.15e9), transcendentals=0, bytes_accessed=0
        ),
        name="token",
    )(*waits)


def neighbours(x, axis, ways):
    return (
        lax.ppermute(x, axis, [(i, i + 1) for i in range(ways - 1)]),
        lax.ppermute(x, axis, [(i + 1, i) for i in range(ways - 1)]),
    )


def pass_on(me, own, up, down):
    def kernel(me_ref, own_ref, up_ref, down_ref, out):
        for source, mine in (
            (own_ref, jnp.logical_or(me_ref[0] == 0, me_ref[0] == 3)),
            (up_ref, me_ref[0] == 2),
            (down_ref, me_ref[0] == 1),
        ):

            @pl.when(mine)
            def _():
                out[...] = source[...]

    whole = pl.BlockSpec(own.shape, lambda _, me_ref: (0,) * own.ndim)
    return pl.pallas_call(
        kernel,
        grid_spec=pltpu.PrefetchScalarGridSpec(
            num_scalar_prefetch=1, grid=(1,), in_specs=[whole] * 3, out_specs=whole
        ),
        out_shape=jax.ShapeDtypeStruct(own.shape, own.dtype),
        compiler_params=pltpu.CompilerParams(vmem_limit_bytes=VMEM_LIMIT),
        name="pass_on",
    )(me.reshape(1), own, up, down)


def join(me, own, up, down, second, third, waits):
    def kernel(me_ref, own_ref, up_ref, down_ref, second_ref, third_ref, *refs):
        out = refs[-1]
        out[:, 0] = own_ref[...]
        out[:, 2] = second_ref[...]
        for d, end, other in ((1, me_ref[0] == 0, up_ref), (3, me_ref[0] == 3, down_ref)):

            @pl.when(end)
            def _():
                out[:, d] = third_ref[...]

            @pl.when(jnp.logical_not(end))
            def _():
                out[:, d] = other[...]

    inner = own.shape[1:]
    step = max(1, own.shape[0] // 2)
    zeros = (0,) * len(inner)
    one = pl.BlockSpec((step,) + inner, lambda f, me_ref: (f,) + zeros)
    corners = [pl.BlockSpec(corner_of(x), lambda f, me_ref, n=x.ndim: (0,) * n) for x in waits]
    return pl.pallas_call(
        kernel,
        grid_spec=pltpu.PrefetchScalarGridSpec(
            num_scalar_prefetch=1,
            grid=(own.shape[0] // step,),
            in_specs=[one] * 5 + corners,
            out_specs=pl.BlockSpec((step, 4) + inner, lambda f, me_ref: (f, 0) + zeros),
        ),
        out_shape=jax.ShapeDtypeStruct(own.shape[:1] + (4,) + inner, own.dtype),
        compiler_params=pltpu.CompilerParams(vmem_limit_bytes=VMEM_LIMIT),
        name="join",
    )(me.reshape(1), own, up, down, second, third, *waits)


def assemble(me, joined, waits):
    f_ways, t_ways, items, kinds, rows, _ = joined.shape
    depth = t_ways * f_ways * rows * LANES // KVR
    cuts = KVR // LANES

    def kernel(me_ref, pieces, *refs):
        out, scratch = refs[-2:]
        for kind in range(kinds):
            for d in range(t_ways):
                t = lax.rem(me_ref[0] - d + t_ways, t_ways)
                for f in range(f_ways):
                    scratch[pl.ds(pl.multiple_of((f * t_ways + t) * rows, rows), rows), :] = pieces[
                        f, d, 0, kind
                    ].astype(jnp.float32)
            for cut in range(cuts):
                out[0, kind, :, pl.ds(cut * LANES, LANES)] = scratch[
                    pl.ds(cut, depth, stride=cuts), :
                ].astype(jnp.bfloat16)

    return pl.pallas_call(
        kernel,
        grid_spec=pltpu.PrefetchScalarGridSpec(
            num_scalar_prefetch=1,
            grid=(items,),
            in_specs=[
                pl.BlockSpec(
                    (f_ways, t_ways, 1, kinds, rows, LANES), lambda i, _: (0, 0, i, 0, 0, 0)
                )
            ]
            + [pl.BlockSpec(corner_of(x), lambda i, _, n=x.ndim: (0,) * n) for x in waits],
            out_specs=pl.BlockSpec((1, kinds, depth, KVR), lambda i, _: (i, 0, 0, 0)),
            scratch_shapes=[pltpu.VMEM((depth * cuts, LANES), jnp.float32)],
        ),
        out_shape=jax.ShapeDtypeStruct((items, kinds, depth, KVR), joined.dtype),
        compiler_params=pltpu.CompilerParams(vmem_limit_bytes=VMEM_LIMIT),
        name="assemble",
    )(me.reshape(1), joined, *waits)


def absorb(me, items, parts, matrices, outs, shapes):
    t_ways = len(parts)
    blocks = parts[0].shape[0]
    q_rows, o_rows = shapes[0].shape[3], shapes[1].shape[3]
    rows = q_rows + o_rows

    def kernel(at, *refs):
        parts, mats = refs[:t_ways], refs[t_ways]
        q_out, o_out = refs[-2:]
        came_from = [lax.rem(at[0] - d + t_ways, t_ways) for d in range(t_ways)]
        pairs = [(d, f) for d in range(t_ways) for f in range(blocks)]
        product = jnp.dot(
            jnp.concatenate([parts[d][f, 0, :q_rows] for d, f in pairs]),
            mats[0, 0],
            preferred_element_type=jnp.float32,
        ).astype(jnp.bfloat16)
        for n, (d, f) in enumerate(pairs):
            q_out[0, f, came_from[d]] = product[n * q_rows : (n + 1) * q_rows]
        for d in range(t_ways):
            product = jnp.dot(
                jnp.concatenate([parts[d][f, 0, q_rows:] for f in range(blocks)]),
                mats[0, 1],
                preferred_element_type=jnp.float32,
            ).astype(jnp.bfloat16)
            for f in range(blocks):
                o_out[0, f, came_from[d]] = product[f * o_rows : (f + 1) * o_rows]

    in_specs = [pl.BlockSpec((blocks, 1, rows, LANES), lambda j, at: (0, j, 0, 0))] * t_ways
    in_specs += [pl.BlockSpec((1,) + matrices.shape[1:], lambda j, at: (items[0] + j, 0, 0, 0))]
    args = [*parts, matrices]
    aliases = {}
    if outs is not None:
        in_specs += [pl.BlockSpec(memory_space=pl.ANY)] * 2
        aliases = {1 + len(args): 0, 2 + len(args): 1}
        args += list(outs)
    work = t_ways * blocks * len(items) * rows
    return pl.pallas_call(
        kernel,
        grid_spec=pltpu.PrefetchScalarGridSpec(
            num_scalar_prefetch=1,
            grid=(len(items),),
            in_specs=in_specs,
            out_specs=[
                pl.BlockSpec((1,) + shape.shape[1:], lambda j, at: (items[0] + j, 0, 0, 0, 0))
                for shape in shapes
            ],
        ),
        out_shape=shapes,
        input_output_aliases=aliases,
        compiler_params=pltpu.CompilerParams(vmem_limit_bytes=VMEM_LIMIT),
        cost_estimate=pl.CostEstimate(
            flops=2 * work * LANES * KVR,
            transcendentals=0,
            bytes_accessed=2 * work * (LANES + KVR),
        ),
        name="absorb",
    )(me.reshape(1), *args)


def absorb_plain(me, parts, matrices):
    t_ways = len(parts)
    order = lax.rem(me - jnp.arange(t_ways, dtype=jnp.int32) + t_ways, jnp.int32(t_ways))
    rows = jnp.take(jnp.stack(parts), order, axis=0).transpose(2, 1, 0, 3, 4)
    cut = rows.shape[3] * QR // (QR + D)
    return tuple(
        jnp.einsum("hrc,hck->hrk", part, mats, preferred_element_type=jnp.float32).astype(jnp.bfloat16)
        for part, mats in (
            (rows[:, :, :, :cut].reshape(rows.shape[0], -1, LANES), matrices[:, 0]),
            (rows[:, :, :, cut:].reshape(rows.shape[0], -1, LANES), matrices[:, 1]),
        )
    )


def per_device(learner_flat, param_offsets, owner_map, slice_map):
    f_ways, t_ways = lax.axis_size("fsdp"), lax.axis_size("tp")
    layer_count = learner_flat.shape[0]
    per_group = owner_map.shape[1] // f_ways
    item_count = layer_count * per_group
    widths = piece_widths(f_ways * t_ways)
    granule = functools.reduce(math.gcd, widths)
    table = learner_flat.reshape(layer_count, -1, granule // LANES, LANES)
    whole_tiles = granule % (16 * LANES) == 0
    row_counts = [width // LANES for width in widths]
    item_rows = row_counts[QUERY] + row_counts[OUT]

    me = lax.axis_index("tp")
    blocks = f_ways // t_ways
    cuts = [item_count * eighths // 8 for eighths in CUTS]
    chunks = [range(low, high) for low, high in zip(cuts, cuts[1:]) if low < high]

    def over_fsdp(x):
        x = lax.all_to_all(x, "fsdp", split_axis=0, concat_axis=0, tiled=True)
        return x.reshape(f_ways, -1, LANES)

    pairs, *to_send = pack(
        table,
        param_offsets,
        owner_map,
        f_ways,
        widths,
        granule,
        [[(range(item_count), (KEY, VALUE))]] + [[(items, (QUERY, OUT))] for items in chunks],
    )
    pairs = pairs.reshape(f_ways, item_count, 2, row_counts[KEY], LANES)
    up, down = neighbours(pairs, "tp", t_ways)
    if t_ways == 4:
        passed = pass_on(me, pairs, up, down)
        second = lax.ppermute(passed, "tp", [(0, 2), (1, 0), (2, 3), (3, 1)])
        third = lax.ppermute(second, "tp", [(1, 0), (2, 3)])

    exchanged, sent = [], []
    for at, items in enumerate(chunks):
        rows = over_fsdp(to_send[at])
        waits = sent[at - 1][:1] if at else []
        if at >= 2:
            waits = waits + exchanged[at - 2][1:]
        if t_ways == 4:
            waits = waits + [[passed], [second], []][min(at, 2)]
        pieces = list(
            cut(rows, slice_map, blocks, 0, len(items), item_rows, waits, CUT_MICROS)
        )
        sent.append(pieces)
        exchanged.append(
            pieces[:1]
            + [
                lax.ppermute(piece, "tp", [(i, (i + shift) % t_ways) for i in range(t_ways)])
                for shift, piece in enumerate(pieces)
                if shift
            ]
        )

    if t_ways == 4:
        joined = join(me, pairs, up, down, second, third, sent[-1][:1])
    else:
        ups, downs = [pairs, up], [pairs, down]
        for _ in range(2, t_ways):
            ups.append(neighbours(ups[-1], "tp", t_ways)[0])
            downs.append(neighbours(downs[-1], "tp", t_ways)[1])
        joined = jnp.stack(
            [pairs] + [jnp.where(me >= d, ups[d], downs[t_ways - d]) for d in range(1, t_ways)], axis=1
        )
    joined = over_fsdp(joined).reshape(joined.shape)

    if whole_tiles:
        shapes = tuple(
            jax.ShapeDtypeStruct((item_count, blocks, t_ways, row_counts[kind], KVR), jnp.bfloat16)
            for kind in (QUERY, OUT)
        )
        matrices = assemble(me, joined, [token(exchanged[-2][1:], TOKEN_MICROS)])
        outs = None
        for items, parts in zip(chunks, exchanged):
            outs = absorb(me, items, parts, matrices, outs, shapes)
        return tuple(out.reshape(layer_count, per_group, -1, KVR) for out in outs)

    order = lax.rem(me - jnp.arange(t_ways, dtype=jnp.int32) + t_ways, jnp.int32(t_ways))
    matrices = jnp.take(joined, order, axis=1).transpose(2, 3, 0, 1, 4, 5)
    matrices = matrices.reshape(item_count, 2, -1, KVR)
    done = [
        absorb_plain(me, parts, matrices[items[0] : items[-1] + 1])
        for items, parts in zip(chunks, exchanged)
    ]
    return tuple(jnp.concatenate(kind).reshape(layer_count, per_group, -1, KVR) for kind in zip(*done))


def solution(mesh):
    placed = (P(None, ("fsdp", "tp")), P(), P(), P())
    return jax.shard_map(
        per_device,
        mesh=mesh,
        in_specs=placed,
        out_specs=(P(None, "fsdp", "tp", None), P(None, "fsdp", "tp", None)),
        check_vma=False,
    )
```
